32 devices in a mesh: rows: 8 (over z, x), blk: 4 (over y, core).
Axes of the slice: x: 2, y: 2, z: 4, core: 2. Of those that a mesh axis runs over, the one named last changes fastest.
Arguments:
- inputs: bfloat16 [32, 1152, 768], P('rows', 'blk'), may hold values from -6 to 6
- image_index: int32 [32, 1152], P('rows', 'blk'), may hold values from -1 to 3, as said below
- keep_mask: int32 [32, 2], P('rows'), may hold values 0 or 1
- first_gain: float32 [768], replicated, may hold values from 0.5 to 1.5
- first_shift: float32 [768], replicated, may hold values from -2.5 to 2.5
- input_weight: bfloat16 [768, 2304], replicated, may hold values from -0.21875 to 0.21875
- input_bias: float32 [2, 768], replicated, may hold values from -2.5 to 2.5
- output_weight: bfloat16 [768, 768], replicated, may hold values from -3.5 to 3.5
- output_bias: float32 [768], replicated, may hold values from -2.5 to 2.5
- second_gain: float32 [768], replicated, may hold values from 0.5 to 1.5
- second_shift: float32 [768], replicated, may hold values from -2.5 to 2.5
- up_weight: bfloat16 [768, 3072], replicated, may hold values from -0.21875 to 0.21875
- up_bias: float32 [3072], replicated, may hold values from -2.5 to 2.5
- down_weight: bfloat16 [3072, 768], replicated, may hold values from -0.109375 to 0.109375
- down_bias: float32 [768], replicated, may hold values from -2.5 to 2.5
- cotangent: bfloat16 [32, 1152, 768], P('rows', 'blk'), may hold values from -6 to 6
Outputs:
- result: bfloat16 [32, 1152, 768], P('rows', 'blk')
- inputs_gradient: bfloat16 [32, 1152, 768], P('rows', 'blk')
- first_gain_gradient: float32 [768], replicated
- first_shift_gradient: float32 [768], replicated
- input_weight_gradient: float32 [768, 2304], replicated
- input_bias_gradient: float32 [2, 768], replicated
- output_weight_gradient: float32 [768, 768], replicated
- output_bias_gradient: float32 [768], replicated
- second_gain_gradient: float32 [768], replicated
- second_shift_gradient: float32 [768], replicated
- up_weight_gradient: float32 [768, 3072], replicated
- up_bias_gradient: float32 [3072], replicated
- down_weight_gradient: float32 [3072, 768], replicated
- down_bias_gradient: float32 [768], replicated
The draws below stay inside these ranges and needn't reach their ends.
Inputs may be any that keep to these rules, and one draw needn't show every extreme that they name: `image_index`: in each row, images 0 to 3 each hold 194 to 282 slots, the rest of the row is padding (-1); every image and the padding of every row have slots on every device of blk.
All inputs are finite; a program needn't handle non-finite values. No bound on the sum of `keep_mask` on one device may be relied on, other than what follows from the above.
Results may differ from the reference program's by a relative error of at most 0.015.
Values may be sent and summed in bfloat16 or wider, within the bound.
No kernel may reach another device: no remote copies, remote signals or barrier semaphores. Data moves between devices by JAX's collectives and lax.ppermute only.
A program may use at most 448 MiB of HBM per device.

```python
import jax
import jax.numpy as jnp
from jax import lax

D = 768
HEADS = 12
HEAD_DIM = 64
FF = 3072
ROW_LEN = 1152
IMAGES = 4
IMG_MIN = 194
IMG_MAX = 282
SLOT_DEV = 288
ROWS = 32


def draw_image_index(key, part):
    key = jax.random.fold_in(key, 11)
    sizes_key, order_key = jax.random.split(key)
    counts = jax.random.randint(sizes_key, (ROWS, IMAGES), IMG_MIN, IMG_MAX + 1)
    bounds = jnp.cumsum(counts, axis=1)
    place = jnp.arange(ROW_LEN, dtype=jnp.int32)
    sorted_ids = jnp.sum((place[None, :, None] >= bounds[:, None, :]).astype(jnp.int32), axis=2)
    sorted_ids = jnp.where(sorted_ids >= IMAGES, -1, sorted_ids)
    blocks_per_row = ROW_LEN // SLOT_DEV
    source = place % SLOT_DEV * blocks_per_row + place // SLOT_DEV
    dealt = sorted_ids[:, source]
    weights = jax.random.randint(order_key, (ROWS, ROW_LEN), 0, 1 << 20) * ROW_LEN + place[None, :]
    order = jnp.argsort(weights.reshape(ROWS, blocks_per_row, SLOT_DEV), axis=2, stable=True)
    shuffled = jnp.take_along_axis(dealt.reshape(ROWS, blocks_per_row, SLOT_DEV), order, axis=2)
    return shuffled.reshape(ROWS, ROW_LEN).astype(jnp.int32)


def place_ends(entries, key, smallest, high):
    shape = entries.shape
    spot = [jax.random.randint(jax.random.fold_in(key, axis), (), 0, shape[axis]) for axis in range(len(shape))]
    entries = entries.at[tuple(spot)].set(smallest)
    longest = shape.index(max(shape))
    spot[longest] = (spot[longest] + 1) % shape[longest]
    return entries.at[tuple(spot)].set(high)


def shard_levels(own_key, shape, pieces, least, largest):
    def one(axis_at, parts):
        steps = jax.random.uniform(jax.random.fold_in(jax.random.fold_in(own_key, 6), axis_at), (parts,), jnp.float32, least / len(pieces), largest / len(pieces))
        return jnp.repeat(jnp.exp(steps), shape[axis_at] // parts).reshape((-1,) + (1,) * (len(shape) - axis_at - 1))

    level = one(*pieces[0])
    for cut in pieces[1:]:
        level = level * one(*cut)
    return level


def centred(stream_key, dims, width, bound, cuts=(), held_as=jnp.bfloat16):
    array = width * jax.random.normal(stream_key, dims, jnp.float32)
    if cuts:
        array = array * shard_levels(stream_key, dims, cuts, -0.22, 0.18)
    return jnp.clip(array, -bound, bound).astype(held_as)


def setup_inputs(seed: int = 0) -> dict:
    seeds = jax.random.split(jax.random.key(seed), 17)
    return {
        "inputs": centred(seeds[0], (ROWS, ROW_LEN, D), 1.0, 6.0, ((0, 8), (1, 4))),
        "image_index": draw_image_index(jax.random.fold_in(seeds[16], 71), 0),
        "keep_mask": place_ends((jax.random.randint(seeds[2], (ROWS, 2), 0, 10) < 9).astype(jnp.int32), jax.random.fold_in(seeds[2], 1), 0, 1),
        "first_gain": jnp.clip(1.0 + 0.1 * jax.random.normal(seeds[3], (D,), jnp.float32), 0.5, 1.5),
        "first_shift": centred(seeds[4], (D,), 0.3, 2.5, (), jnp.float32),
        "input_weight": centred(seeds[5], (D, 3 * D), D ** -0.5, 0.21875),
        "input_bias": centred(seeds[6], (2, D), 0.3, 2.5, (), jnp.float32),
        "output_weight": centred(seeds[7], (D, D), (max(D // 256, 1)) ** -0.5, 3.5),
        "output_bias": centred(seeds[8], (D,), 0.3, 2.5, (), jnp.float32),
        "second_gain": jnp.clip(1.0 + 0.1 * jax.random.normal(seeds[9], (D,), jnp.float32), 0.5, 1.5),
        "second_shift": centred(seeds[10], (D,), 0.3, 2.5, (), jnp.float32),
        "up_weight": centred(seeds[11], (D, FF), D ** -0.5, 0.21875),
        "up_bias": centred(seeds[12], (FF,), 0.3, 2.5, (), jnp.float32),
        "down_weight": centred(seeds[13], (FF, D), FF ** -0.5, 0.109375),
        "down_bias": centred(seeds[14], (D,), 0.3, 2.5, (), jnp.float32),
        "cotangent": centred(seeds[15], (ROWS, ROW_LEN, D), 1.0, 6.0, ((0, 8), (1, 4))),
    }


@jax.custom_vjp
def low(v):
    return lax.optimization_barrier(v.astype(jnp.bfloat16)).astype(jnp.float32)

@jax.custom_vjp
def low_back(v):
    return v

def low_keep(v):
    return (low(v), None)

def low_pass(kept, grad):
    return (grad,)

def back_keep(v):
    return (v, None)

def back_low(kept, grad):
    return (low(grad),)
low.defvjp(low_keep, low_pass)
low_back.defvjp(back_keep, back_low)

def norm_rows(values, gain, shift):
    centre = values - lax.optimization_barrier(jnp.mean(values, axis=-1, keepdims=True))
    spread = lax.optimization_barrier(jnp.mean(centre * centre, axis=-1, keepdims=True))
    return centre * lax.rsqrt(spread + 1e-06) * gain + shift

def row_forward(row, ids, keep, first_gain, first_shift, input_weight, input_bias, output_weight, output_bias, second_gain, second_shift, up_weight, up_bias, down_weight, down_bias):
    highest = lax.Precision.HIGHEST
    length = row.shape[0]
    normed = low(norm_rows(row, first_gain, first_shift))
    mixed = jnp.dot(normed, input_weight, precision=highest)
    query = low(low_back(mixed[:, :D] + input_bias[0]))
    keys = low(low_back(mixed[:, D:2 * D]))
    values = low(low_back(mixed[:, 2 * D:] + input_bias[1]))
    query_heads = query.reshape(length, HEADS, HEAD_DIM)
    key_heads = keys.reshape(length, HEADS, HEAD_DIM)
    value_heads = values.reshape(length, HEADS, HEAD_DIM)
    scores = jnp.einsum('qhd,khd->hqk', query_heads, key_heads, precision=highest) * HEAD_DIM ** (-0.5)
    scores = low_back(scores)
    same = ids[:, None] == ids[None, :]
    scores = jnp.where(same[None], scores, -jnp.inf)
    probs = jax.nn.softmax(scores, axis=-1)
    attended = jnp.einsum('hqk,khd->qhd', low(probs), value_heads, precision=highest).reshape(length, D)
    attended = low(low_back(attended))
    branch = low_back(jnp.dot(attended, output_weight, precision=highest) + output_bias)
    middle = row + keep[0] * branch
    normed_second = low(norm_rows(middle, second_gain, second_shift))
    hidden = low_back(jnp.dot(normed_second, up_weight, precision=highest) + up_bias)
    active = low(jax.nn.gelu(hidden, approximate=False))
    branch_second = low_back(jnp.dot(active, down_weight, precision=highest) + down_bias)
    return middle + keep[1] * branch_second

def reference(inputs, image_index, keep_mask, first_gain, first_shift, input_weight, input_bias, output_weight, output_bias, second_gain, second_shift, up_weight, up_bias, down_weight, down_bias, cotangent):
    params = (first_gain.astype(jnp.float32), first_shift.astype(jnp.float32), input_weight.astype(jnp.float32), input_bias.astype(jnp.float32), output_weight.astype(jnp.float32), output_bias.astype(jnp.float32), second_gain.astype(jnp.float32), second_shift.astype(jnp.float32), up_weight.astype(jnp.float32), up_bias.astype(jnp.float32), down_weight.astype(jnp.float32), down_bias.astype(jnp.float32))
    keep_scale = keep_mask.astype(jnp.float32) / 0.9
    checked = jax.checkpoint(row_forward)

    def forward(tokens, weights):

        def one_row(items):
            return checked(items[0], items[1], items[2], *weights)
        return lax.map(one_row, (tokens, image_index, keep_scale))
    output, pullback = jax.vjp(forward, inputs.astype(jnp.float32), params)
    token_grad, grads = pullback(cotangent.astype(jnp.float32))
    return (output.astype(jnp.bfloat16), token_grad.astype(jnp.bfloat16), grads[0], grads[1], grads[2], grads[3], grads[4], grads[5], grads[6], grads[7], grads[8], grads[9], grads[10], grads[11])
```

```python
import functools

import jax
import jax.numpy as jnp
from jax import lax
from jax.experimental import pallas as pl
from jax.experimental.pallas import tpu as pltpu
from jax.sharding import PartitionSpec as P

HEADS = 12
HEAD_DIM = 64
PAIR = 2 * HEAD_DIM
PAIRS = HEADS // 2
eps_norm = 1e-06
keep_rate = 0.9
F32 = jnp.float32
BF16 = jnp.bfloat16
NEG = -1e30
VMEM = 62 * 1024 * 1024


def dot(a, b):
    return jnp.dot(a, b, preferred_element_type=F32)


def dot_nt(a, b):
    return lax.dot_general(a, b, (((1,), (1,)), ((), ())), preferred_element_type=F32)


def dot_tn(a, b):
    return lax.dot_general(a, b, (((0,), (0,)), ((), ())), preferred_element_type=F32)


def whole(shape):
    return pl.BlockSpec(shape, lambda *g: (0,) * len(shape), pipeline_mode=pl.Buffered(1))


def centre_scale(values):
    centre = values - jnp.mean(values, axis=-1, keepdims=True)
    spread = jnp.mean(centre * centre, axis=-1, keepdims=True)
    inv = lax.rsqrt(spread + eps_norm)
    return centre * inv, inv


def norm_back(grad_hat, hat, inv):
    first = jnp.mean(grad_hat, axis=-1, keepdims=True)
    second = jnp.mean(grad_hat * hat, axis=-1, keepdims=True)
    return (grad_hat - first - hat * second) * inv


def sort_tile(rank_row, tile, step, pieces):
    span = pieces[0].shape[0]
    place = step * tile + lax.broadcasted_iota(jnp.int32, (tile, span), 0)
    total = None
    for i, piece in enumerate(pieces):
        pick = (rank_row[:, i * span : (i + 1) * span] == place).astype(BF16)
        part = dot(pick, piece[...])
        total = part if total is None else total + part
    return total


def qkv_kernel(n, tile, *refs):
    rank, *pieces = refs[: n + 1]
    gain, shift, weight, bias, xs_out, normed_out, qkv_out = refs[n + 1 :]
    xs = sort_tile(rank[...], tile, pl.program_id(0), pieces)
    xs_out[...] = xs.astype(BF16)
    hat, _ = centre_scale(xs)
    normed = (hat * gain[...] + shift[...]).astype(BF16)
    normed_out[...] = normed
    width = 3 * PAIR
    for p in range(PAIRS):
        cols = pl.ds(p * width, width)
        mixed = (dot(normed, weight[:, cols]) + bias[:, cols]).astype(BF16)
        qkv_out[:, p * width : p * width + PAIR] = mixed[:, :PAIR] * BF16(HEAD_DIM**-0.5)
        qkv_out[:, p * width + PAIR : (p + 1) * width] = mixed[:, PAIR:]


def qkv_call(rank, pieces, gain, shift, weight, bias, tile=288):
    n = len(pieces)
    span, width = pieces[0].shape
    count = n * span
    return pl.pallas_call(
        functools.partial(qkv_kernel, n, tile),
        grid=(count // tile,),
        in_specs=[whole((1, count))]
        + [whole((span, width))] * n
        + [whole((1, width)), whole((1, width)), whole(weight.shape), whole(bias.shape)],
        out_specs=[
            pl.BlockSpec((tile, width), lambda i: (i, 0)),
            pl.BlockSpec((tile, width), lambda i: (i, 0)),
            pl.BlockSpec((tile, 3 * width), lambda i: (i, 0)),
        ],
        out_shape=[
            jax.ShapeDtypeStruct((count, width), BF16),
            jax.ShapeDtypeStruct((count, width), BF16),
            jax.ShapeDtypeStruct((count, 3 * width), BF16),
        ],
        compiler_params=pltpu.CompilerParams(vmem_limit_bytes=VMEM),
        cost_estimate=pl.CostEstimate(
            flops=2 * count * width * (3 * width + count), bytes_accessed=16 * count * width, transcendentals=0
        ),
        name="sort_qkv",
    )(rank, *pieces, gain, shift, weight, bias)


SMALL = 304
LARGE = 384


def windows(starts, seg, length):
    first, last = starts[seg], starts[seg + 1]
    aligned = first // 16 * 16
    small = SMALL if seg < 4 else LARGE
    at_small = pl.multiple_of(jnp.minimum(aligned, length - small), 16)
    at_large = pl.multiple_of(jnp.minimum(aligned, length - LARGE), 16)
    return first, last, small, at_small, at_large


def inside(at, size, lanes, first, last):
    place = at + lax.broadcasted_iota(jnp.int32, (size, lanes), 0)
    return (place >= first) & (place < last)


def forward_kernel(starts, qkv, out, stat):
    length = qkv.shape[0]
    for seg in range(5):
        first, last, small, at_q, at_k = windows(starts, seg, length)
        rows_q = pl.ds(at_q, small)
        q = qkv[rows_q, 0:PAIR]
        k = qkv[pl.ds(at_k, LARGE), PAIR : 2 * PAIR]
        v = qkv[pl.ds(at_k, LARGE), 2 * PAIR : 3 * PAIR]
        lane = lax.broadcasted_iota(jnp.int32, (LARGE, PAIR), 1)
        lane_q = lax.broadcasted_iota(jnp.int32, (small, PAIR), 1)
        low = lane < HEAD_DIM
        seen = inside(at_k, LARGE, PAIR, first, last)
        zero = jnp.zeros((LARGE, PAIR), BF16)
        one = jnp.ones((LARGE, PAIR), BF16)
        bias = jnp.where((lane == 0) & ~seen, NEG, 0.0).astype(BF16)
        q_ext = jnp.concatenate([q, (lane_q == 0).astype(BF16)], axis=1)
        tops, weights, mixes = [], [], []
        for half in (low, ~low):
            k_ext = jnp.concatenate([jnp.where(half, k, zero), bias], axis=1)
            scores = dot_nt(q_ext, k_ext)
            top = jnp.max(scores, axis=-1, keepdims=True)
            tops.append(top)
            weights.append(jnp.exp(scores - top).astype(BF16))
            mixes.append(jnp.concatenate([jnp.where(half, v, zero), jnp.where(half, one, zero)], axis=1))
        both = dot(jnp.concatenate(weights, axis=1), jnp.concatenate(mixes, axis=0))
        total = both[:, PAIR:]
        peak = jnp.where(lane_q < HEAD_DIM, tops[0], tops[1])
        mine = inside(at_q, small, PAIR, first, last)
        out[rows_q, :] = jnp.where(mine, both[:, :PAIR] / total, out[rows_q, :])
        stat[rows_q, :] = jnp.where(mine, peak + jnp.log(total), stat[rows_q, :])


def forward_call(starts, qkv):
    count, wide = qkv.shape
    pairs = wide // (3 * PAIR)
    return pl.pallas_call(
        forward_kernel,
        grid_spec=pltpu.PrefetchScalarGridSpec(
            num_scalar_prefetch=1,
            grid=(pairs,),
            in_specs=[pl.BlockSpec((count, 3 * PAIR), lambda p, s: (0, p))],
            out_specs=[
                pl.BlockSpec((count, PAIR), lambda p, s: (0, p)),
                pl.BlockSpec((count, PAIR), lambda p, s: (0, p)),
            ],
        ),
        out_shape=[jax.ShapeDtypeStruct((count, pairs * PAIR), F32)] * 2,
        compiler_params=pltpu.CompilerParams(vmem_limit_bytes=VMEM),
        cost_estimate=pl.CostEstimate(
            flops=4 * count * 1024 * wide // 3, bytes_accessed=10 * count * wide, transcendentals=count * 400 * HEADS
        ),
        name="attention_forward",
    )(starts, qkv)


def split3(value):
    high = value.astype(BF16)
    rest = value - high.astype(F32)
    mid = rest.astype(BF16)
    return high, mid, (rest - mid.astype(F32)).astype(BF16)


def backward_kernel(starts, qkv, grad, att, stat, out, sums):
    length = qkv.shape[0]
    third = lax.broadcasted_iota(jnp.int32, (PAIR, PAIR), 0) // HEAD_DIM
    block = (third == lax.broadcasted_iota(jnp.int32, (PAIR, PAIR), 1) // HEAD_DIM).astype(BF16)
    for seg in range(5):
        first, last, small, at_k, at_q = windows(starts, seg, length)
        rows_q, rows_k = pl.ds(at_q, LARGE), pl.ds(at_k, small)
        lane_q = lax.broadcasted_iota(jnp.int32, (LARGE, PAIR), 1)
        lane_k = lax.broadcasted_iota(jnp.int32, (small, PAIR), 1)
        spot_q, spot_k = lane_q % HEAD_DIM, lane_k % HEAD_DIM
        mine_q = inside(at_q, LARGE, PAIR, first, last)
        mine_k = inside(at_k, small, PAIR, first, last)
        zero_q = jnp.zeros((LARGE, PAIR), BF16)
        zero_k = jnp.zeros((small, PAIR), BF16)
        q = qkv[rows_q, 0:PAIR]
        k = jnp.where(mine_k, qkv[rows_k, PAIR : 2 * PAIR], zero_k)
        v = qkv[rows_k, 2 * PAIR : 3 * PAIR]
        g = jnp.where(mine_q, grad[rows_q, :], zero_q)
        prod = g.astype(F32) * jnp.where(mine_q, att[rows_q, :], 0.0)
        p_high = prod.astype(BF16)
        p_low = (prod - p_high.astype(F32)).astype(BF16)
        inner = dot(p_high, block) + dot(p_low, block)
        logs = jnp.where(mine_q, stat[rows_q, :], 0.0)

        def spread(value, fifth):
            a, b, c = split3(value)
            return jnp.where(
                spot_q == 0, a, jnp.where(spot_q == 1, b, jnp.where(spot_q == 2, c, fifth))
            )

        query_bias = jnp.where(mine_q, 0.0, NEG).astype(BF16)
        unit = jnp.ones((LARGE, PAIR), BF16)
        q_ext = jnp.concatenate(
            [q, spread(logs, jnp.where(spot_q == 3, unit, jnp.where(spot_q == 4, query_bias, zero_q)))], axis=1
        )
        g_ext = jnp.concatenate([g, spread(inner, zero_q)], axis=1)
        key_bias = jnp.where(mine_k, 0.0, NEG).astype(BF16)
        minus = jnp.where(spot_k < 3, -1.0, 0.0).astype(BF16)
        k_tail = jnp.where(
            spot_k == 3, key_bias, jnp.where(spot_k == 4, jnp.ones((small, PAIR), BF16), minus)
        )
        probs, score_grads, ks, gs, qs = [], [], [], [], []
        for h in range(2):
            half_k = lane_k // HEAD_DIM == h
            half_q = lane_q // HEAD_DIM == h
            k_half = jnp.where(half_k, k, zero_k)
            shifted = dot_nt(jnp.concatenate([k_half, jnp.where(half_k, k_tail, zero_k)], axis=1), q_ext)
            prob = jnp.exp(shifted)
            v_half = jnp.where(half_k, v, zero_k)
            prob_grad = dot_nt(jnp.concatenate([v_half, jnp.where(half_k, minus, zero_k)], axis=1), g_ext)
            probs.append(prob.astype(BF16))
            score_grads.append((prob * prob_grad).astype(BF16))
            ks.append(k_half)
            gs.append(jnp.where(half_q, g, zero_q))
            qs.append(jnp.where(half_q, q, zero_q))
        value_grad = dot(jnp.concatenate(probs, axis=1), jnp.concatenate(gs, axis=0))
        key_grad = dot(jnp.concatenate(score_grads, axis=1), jnp.concatenate(qs, axis=0))
        query_grad = dot_tn(jnp.concatenate(score_grads, axis=0), jnp.concatenate(ks, axis=0))
        query_grad = (query_grad * HEAD_DIM**-0.5).astype(BF16)
        out[rows_q, 0:PAIR] = jnp.where(mine_q, query_grad, out[rows_q, 0:PAIR])
        out[rows_k, PAIR : 2 * PAIR] = jnp.where(mine_k, key_grad.astype(BF16), out[rows_k, PAIR : 2 * PAIR])
        out[rows_k, 2 * PAIR :] = jnp.where(mine_k, value_grad.astype(BF16), out[rows_k, 2 * PAIR :])
    sums[...] = jnp.sum(out[...].astype(F32), axis=0, keepdims=True)


def backward_call(starts, qkv, grad, att, stat, first_pair, pairs):
    count = qkv.shape[0]
    return pl.pallas_call(
        backward_kernel,
        grid_spec=pltpu.PrefetchScalarGridSpec(
            num_scalar_prefetch=1,
            grid=(pairs,),
            in_specs=[pl.BlockSpec((count, 3 * PAIR), lambda p, s: (0, p + first_pair))]
            + [pl.BlockSpec((count, PAIR), lambda p, s: (0, p + first_pair))] * 3,
            out_specs=[
                pl.BlockSpec((count, 3 * PAIR), lambda p, s: (0, p)),
                pl.BlockSpec((1, 3 * PAIR), lambda p, s: (0, p)),
            ],
        ),
        out_shape=[
            jax.ShapeDtypeStruct((count, pairs * 3 * PAIR), BF16),
            jax.ShapeDtypeStruct((1, pairs * 3 * PAIR), F32),
        ],
        compiler_params=pltpu.CompilerParams(vmem_limit_bytes=VMEM),
        cost_estimate=pl.CostEstimate(
            flops=10 * count * 1024 * pairs * PAIR, bytes_accessed=20 * count * pairs * PAIR, transcendentals=count * 400 * 2 * pairs
        ),
        name="attention_backward",
    )(starts, qkv, grad, att, stat)


ERF = (0.254829592, -0.284496736, 1.421413741, -1.453152027, 1.061405429)


def gelu_pair(u):
    size = jnp.abs(u)
    t = 1.0 / (1.0 + (0.3275911 * 0.5**0.5) * size)
    bell = jnp.exp(u * u * -0.5)
    poly = ERF[4] * t + ERF[3]
    for c in (ERF[2], ERF[1], ERF[0]):
        poly = poly * t + c
    tail = 0.5 * poly * t * bell
    phi = jnp.where(u < 0, tail, 1.0 - tail)
    return u * phi, phi + u * bell * 0.3989422804014327


def mlp_kernel(n, tile, chunk, *refs):
    keep, rank, *pieces = refs[: n + 2]
    (
        att, xs, out_w, up_w, down_w, vectors, up_b,
        result, middle_grad_out, att_low_out, normed_out, active_out, hidden_out, mlp_out, branch_out, att_grad_out,
        sums, up_sums,
    ) = refs[n + 2 :]
    out_b, gain, shift, down_b = (vectors[i : i + 1, :] for i in range(4))
    keep_attn, keep_mlp = keep[0], keep[1]
    step = pl.program_id(0)
    cot = sort_tile(rank[...], tile, step, pieces)
    att_low = att[...].astype(BF16)
    att_low_out[...] = att_low
    middle = xs[...].astype(F32) + keep_attn * (dot(att_low, out_w[...]) + out_b)
    hat, inv = centre_scale(middle)
    normed = (hat * gain + shift).astype(BF16)
    normed_out[...] = normed
    mlp_grad = (cot * keep_mlp).astype(BF16)
    mlp_out[...] = mlp_grad

    @pl.when(step == 0)
    def _():
        sums[...] = jnp.zeros_like(sums)
        up_sums[...] = jnp.zeros_like(up_sums)

    lift = jnp.zeros(middle.shape, F32)
    back = jnp.zeros(middle.shape, F32)
    for c in range(up_w.shape[1] // chunk):
        cols = slice(c * chunk, (c + 1) * chunk)
        u = dot(normed, up_w[:, cols]) + up_b[:, cols]
        act, slope = gelu_pair(u)
        act = act.astype(BF16)
        active_out[:, cols] = act
        lift = lift + dot(act, down_w[cols, :])
        hidden = (dot_nt(mlp_grad, down_w[cols, :]) * slope).astype(BF16)
        hidden_out[:, cols] = hidden
        up_sums[:, cols] += jnp.sum(hidden.astype(F32), axis=0, keepdims=True)
        back = back + dot_nt(hidden, up_w[:, cols])
    result[...] = (middle + keep_mlp * (lift + down_b)).astype(BF16)
    middle_grad = cot + norm_back(back * gain, hat, inv)
    middle_grad_out[...] = middle_grad
    branch = (keep_attn * middle_grad).astype(BF16)
    branch_out[...] = branch
    att_grad_out[...] = dot_nt(branch, out_w[...]).astype(BF16)
    sums[0:1, :] += jnp.sum(back * hat, axis=0, keepdims=True)
    sums[1:2, :] += jnp.sum(back, axis=0, keepdims=True)
    sums[2:3, :] += jnp.sum(mlp_grad.astype(F32), axis=0, keepdims=True)
    sums[3:4, :] += jnp.sum(branch.astype(F32), axis=0, keepdims=True)


def mlp_call(keep, rank, pieces, att, xs, out_w, up_w, down_w, vectors, up_b, tile=192, chunk=512):
    n = len(pieces)
    span, width = pieces[0].shape
    count = n * span
    ff = up_w.shape[1]

    def rows(w):
        return pl.BlockSpec((tile, w), lambda i: (i, 0))

    def shape(w, dtype):
        return jax.ShapeDtypeStruct((count, w), dtype)

    return pl.pallas_call(
        functools.partial(mlp_kernel, n, tile, chunk),
        grid=(count // tile,),
        in_specs=[pl.BlockSpec(memory_space=pltpu.SMEM), whole((1, count))]
        + [whole((span, width))] * n
        + [rows(width), rows(width), whole(out_w.shape), whole(up_w.shape), whole(down_w.shape)]
        + [whole(vectors.shape), whole(up_b.shape)],
        out_specs=[rows(width)] * 4
        + [rows(ff), rows(ff)]
        + [rows(width)] * 3
        + [pl.BlockSpec((8, width), lambda i: (0, 0)), pl.BlockSpec((1, ff), lambda i: (0, 0))],
        out_shape=[
            shape(width, BF16),
            shape(width, F32),
            shape(width, BF16),
            shape(width, BF16),
            shape(ff, BF16),
            shape(ff, BF16),
            shape(width, BF16),
            shape(width, BF16),
            shape(width, BF16),
            jax.ShapeDtypeStruct((8, width), F32),
            jax.ShapeDtypeStruct((1, ff), F32),
        ],
        compiler_params=pltpu.CompilerParams(vmem_limit_bytes=VMEM),
        cost_estimate=pl.CostEstimate(
            flops=2 * count * width * (4 * ff + 2 * width), bytes_accessed=40 * count * width, transcendentals=2 * count * ff
        ),
        name="mlp",
    )(keep, rank, *pieces, att, xs, out_w, up_w, down_w, vectors, up_b)


def input_kernel(groups, *refs):
    gs = refs[:groups]
    weight, xs, middle_grad, gain, out, sums = refs[groups:]
    span = gs[0].shape[1]
    back = None
    for i, g in enumerate(gs):
        part = dot_nt(g[...], weight[:, i * span : (i + 1) * span])
        back = part if back is None else back + part
    hat, inv = centre_scale(xs[...].astype(F32))
    out[...] = (middle_grad[...] + norm_back(back * gain[...], hat, inv)).astype(BF16)

    @pl.when(pl.program_id(0) == 0)
    def _():
        sums[...] = jnp.zeros_like(sums)

    sums[0:1, :] += jnp.sum(back * hat, axis=0, keepdims=True)
    sums[1:2, :] += jnp.sum(back, axis=0, keepdims=True)


def input_call(gs, weight, xs, middle_grad, gain, tile=288):
    count, width = xs.shape
    return pl.pallas_call(
        functools.partial(input_kernel, len(gs)),
        grid=(count // tile,),
        in_specs=[pl.BlockSpec((tile, g.shape[1]), lambda i: (i, 0)) for g in gs]
        + [
            whole(weight.shape),
            pl.BlockSpec((tile, width), lambda i: (i, 0)),
            pl.BlockSpec((tile, width), lambda i: (i, 0)),
            whole((1, width)),
        ],
        out_specs=[pl.BlockSpec((tile, width), lambda i: (i, 0)), pl.BlockSpec((8, width), lambda i: (0, 0))],
        out_shape=[jax.ShapeDtypeStruct((count, width), BF16), jax.ShapeDtypeStruct((8, width), F32)],
        compiler_params=pltpu.CompilerParams(vmem_limit_bytes=VMEM),
        cost_estimate=pl.CostEstimate(
            flops=6 * count * width * width, bytes_accessed=16 * count * width, transcendentals=0
        ),
        name="input_backward",
    )(*gs, weight, xs, middle_grad, gain)


def unsort_kernel(n, rank, xs, *outs):
    count = xs.shape[0]
    span = count // n
    place = lax.broadcasted_iota(jnp.int32, (span, count), 1)
    for i, out in enumerate(outs):
        pick = (rank[i * span : (i + 1) * span, :] == place).astype(BF16)
        out[...] = dot(pick, xs[...]).astype(BF16)


def unsort_call(rank_col, xs, n):
    count, width = xs.shape
    span = count // n
    return pl.pallas_call(
        functools.partial(unsort_kernel, n),
        out_shape=[jax.ShapeDtypeStruct((span, width), BF16)] * n,
        compiler_params=pltpu.CompilerParams(vmem_limit_bytes=VMEM),
        cost_estimate=pl.CostEstimate(
            flops=2 * count * width * count, bytes_accessed=6 * count * width, transcendentals=0
        ),
        name="unsort",
    )(rank_col, xs)


MICRO = 2


def from_behind(value, axis, steps):
    count = lax.axis_size(axis)
    pairs = [(source, (source + steps) % count) for source in range(count)]
    return lax.ppermute(value, axis, pairs)


def norm_rows(values, gain, shift):
    centre = values - jnp.mean(values, axis=-1, keepdims=True)
    spread = jnp.mean(centre * centre, axis=-1, keepdims=True)
    return centre * lax.rsqrt(spread + eps_norm) * gain + shift


def gelu_exact(values):
    return jax.nn.gelu(values, approximate=False)


def split_heads(block):
    return block.reshape(block.shape[0], block.shape[1], HEADS, HEAD_DIM)


def take_rows(array, first_row, count_rows):
    return lax.slice_in_dim(array, first_row, first_row + count_rows, axis=0)


def masked_scores(query, keys, ids_query, ids_keys):
    scores = jnp.einsum(
        "rqhd,rkhd->rhqk", split_heads(query), split_heads(keys), preferred_element_type=jnp.float32
    ) * HEAD_DIM ** (-0.5)
    same = ids_query[:, None, :, None] == ids_keys[:, None, None, :]
    return jnp.where(same, scores, -jnp.inf)


def attend_piece(carry, query, ids_query, piece):
    keys, values, ids_keys = piece
    peak, total, accum = carry
    scores = masked_scores(query, keys, ids_query, ids_keys)
    top = jnp.maximum(peak, jnp.max(scores, axis=-1))
    weights = jnp.exp(scores - top[..., None])
    total = jnp.sum(weights, axis=-1)
    update = jnp.einsum(
        "rhqk,rkhd->rqhd",
        weights.astype(jnp.bfloat16),
        split_heads(values),
        preferred_element_type=jnp.float32,
    )
    return (top, total, update.reshape(accum.shape))


def attention_forward(query, keys, values, ids_query):
    rows_here, slots, width = query.shape
    start_state = (
        jnp.full((rows_here, HEADS, slots), -1e30, jnp.float32),
        jnp.zeros((rows_here, HEADS, slots), jnp.float32),
        jnp.zeros((rows_here, slots, width), jnp.float32),
    )
    carry = attend_piece(
        start_state,
        query,
        ids_query,
        (
            lax.all_gather(keys, "blk", axis=1, tiled=True),
            lax.all_gather(values, "blk", axis=1, tiled=True),
            lax.all_gather(ids_query, "blk", axis=1, tiled=True),
        ),
    )
    return (carry[0], carry[1], carry[2], None)


def attention_back(query, out_grad, ids_query, log_total, inner, piece):
    keys, values, ids_keys = piece
    scale = HEAD_DIM ** (-0.5)
    scores = masked_scores(query, keys, ids_query, ids_keys)
    probs = jnp.exp(scores - log_total[..., None])
    prob_grad = jnp.einsum(
        "rqhd,rkhd->rhqk",
        split_heads(out_grad),
        split_heads(values),
        preferred_element_type=jnp.float32,
    )
    score_grad = (probs * (prob_grad - inner[..., None])).astype(jnp.bfloat16)
    value_grad = jnp.einsum(
        "rhqk,rqhd->rkhd",
        probs.astype(jnp.bfloat16),
        split_heads(out_grad),
        preferred_element_type=jnp.float32,
    )
    key_grad = (
        jnp.einsum(
            "rhqk,rqhd->rkhd", score_grad, split_heads(query), preferred_element_type=jnp.float32
        )
        * scale
    )
    query_grad = (
        jnp.einsum(
            "rhqk,rkhd->rqhd", score_grad, split_heads(keys), preferred_element_type=jnp.float32
        )
        * scale
    )
    return (
        query_grad.reshape(query.shape),
        key_grad.reshape(keys.shape),
        value_grad.reshape(values.shape),
    )


def local(
    inputs,
    image_index,
    keep_mask,
    first_gain,
    first_shift,
    input_weight,
    input_bias,
    output_weight,
    output_bias,
    second_gain,
    second_shift,
    up_weight,
    up_bias,
    down_weight,
    down_bias,
    cotangent,
):
    rows_local, slots, width = inputs.shape
    rows_micro = rows_local // MICRO
    count = rows_micro * slots
    blocks = lax.axis_size("blk")
    params = (
        first_gain,
        first_shift,
        input_weight,
        input_bias,
        output_weight,
        output_bias,
        second_gain,
        second_shift,
        up_weight,
        up_bias,
        down_weight,
        down_bias,
    )
    sums = [jnp.zeros(item.shape, jnp.float32) for item in params]
    results = []
    input_grads = []
    for micro in range(MICRO):
        first_row = micro * rows_micro
        rows_in = take_rows(inputs, first_row, rows_micro).astype(jnp.float32).reshape(count, width)
        out_cot = (
            take_rows(cotangent, first_row, rows_micro).astype(jnp.float32).reshape(count, width)
        )
        ids_query = take_rows(image_index, first_row, rows_micro).astype(jnp.bfloat16)
        keep = take_rows(keep_mask, first_row, rows_micro).astype(jnp.float32) / keep_rate
        keep_attn = jnp.broadcast_to(keep[:, None, 0:1], (rows_micro, slots, 1)).reshape(count, 1)
        keep_mlp = jnp.broadcast_to(keep[:, None, 1:2], (rows_micro, slots, 1)).reshape(count, 1)
        normed = norm_rows(rows_in, first_gain, first_shift).astype(jnp.bfloat16)
        mixed = jnp.dot(normed, input_weight, preferred_element_type=jnp.float32)
        query = (
            (mixed[:, :width] + input_bias[0])
            .astype(jnp.bfloat16)
            .reshape(rows_micro, slots, width)
        )
        keys = mixed[:, width : 2 * width].astype(jnp.bfloat16).reshape(rows_micro, slots, width)
        values = (
            (mixed[:, 2 * width :] + input_bias[1])
            .astype(jnp.bfloat16)
            .reshape(rows_micro, slots, width)
        )
        top, total, accum, whole = attention_forward(query, keys, values, ids_query)
        attended = (split_heads(accum) / jnp.transpose(total, (0, 2, 1))[..., None]).reshape(
            count, width
        )
        log_total = top + jnp.log(total)
        attended_low = attended.astype(jnp.bfloat16)
        branch = (
            jnp.dot(attended_low, output_weight, preferred_element_type=jnp.float32) + output_bias
        )
        middle = rows_in + keep_attn * branch
        normed_second = norm_rows(middle, second_gain, second_shift).astype(jnp.bfloat16)
        hidden = jnp.dot(normed_second, up_weight, preferred_element_type=jnp.float32) + up_bias
        active = gelu_exact(hidden).astype(jnp.bfloat16)
        branch_second = jnp.dot(active, down_weight, preferred_element_type=jnp.float32) + down_bias
        results.append(
            (middle + keep_mlp * branch_second)
            .astype(jnp.bfloat16)
            .reshape(rows_micro, slots, width)
        )
        mlp_grad = (out_cot * keep_mlp).astype(jnp.bfloat16)
        sums[10] = sums[10] + jnp.dot(active.T, mlp_grad, preferred_element_type=jnp.float32)
        sums[11] = sums[11] + jnp.sum(mlp_grad.astype(jnp.float32), axis=0)
        active_grad = jnp.dot(mlp_grad, down_weight.T, preferred_element_type=jnp.float32)
        hidden_grad = jax.vjp(gelu_exact, hidden)[1](active_grad)[0].astype(jnp.bfloat16)
        sums[8] = sums[8] + jnp.dot(
            normed_second.T, hidden_grad, preferred_element_type=jnp.float32
        )
        sums[9] = sums[9] + jnp.sum(hidden_grad.astype(jnp.float32), axis=0)
        second_in_grad = jnp.dot(hidden_grad, up_weight.T, preferred_element_type=jnp.float32)
        middle_part, second_gain_part, second_shift_part = jax.vjp(
            norm_rows, middle, second_gain, second_shift
        )[1](second_in_grad)
        sums[6] = sums[6] + second_gain_part
        sums[7] = sums[7] + second_shift_part
        middle_grad = middle_part + out_cot
        branch_grad = (middle_grad * keep_attn).astype(jnp.bfloat16)
        sums[4] = sums[4] + jnp.dot(attended_low.T, branch_grad, preferred_element_type=jnp.float32)
        sums[5] = sums[5] + jnp.sum(branch_grad.astype(jnp.float32), axis=0)
        attended_grad = jnp.dot(
            branch_grad, output_weight.T, preferred_element_type=jnp.float32
        ).astype(jnp.bfloat16)
        out_grad = attended_grad.reshape(rows_micro, slots, width)
        inner = jnp.transpose(
            jnp.sum(
                split_heads(
                    (attended_grad.astype(jnp.float32) * attended).reshape(rows_micro, slots, width)
                ),
                axis=-1,
            ),
            (0, 2, 1),
        )
        query_grad = jnp.zeros((rows_micro, slots, width), jnp.float32)
        visiting = (keys, values, ids_query)
        key_grad = jnp.zeros((rows_micro, slots, width), jnp.float32)
        value_grad = jnp.zeros((rows_micro, slots, width), jnp.float32)
        for step in range(blocks):
            query_part, key_part, value_part = attention_back(
                query, out_grad, ids_query, log_total, inner, visiting
            )
            query_grad = query_grad + query_part
            key_grad, value_grad = (
                from_behind((key_grad + key_part).astype(jnp.bfloat16), "blk", 1).astype(
                    jnp.float32
                ),
                from_behind((value_grad + value_part).astype(jnp.bfloat16), "blk", 1).astype(
                    jnp.float32
                ),
            )
            if step + 1 < blocks:
                visiting = from_behind((visiting[0], visiting[1], visiting[2]), "blk", 1)
        joined_grad = (
            jnp.concatenate([query_grad, key_grad, value_grad], axis=-1)
            .astype(jnp.bfloat16)
            .reshape(count, 3 * width)
        )
        sums[2] = sums[2] + jnp.dot(normed.T, joined_grad, preferred_element_type=jnp.float32)
        joined_sums = jnp.sum(joined_grad.astype(jnp.float32), axis=0)
        sums[3] = sums[3] + jnp.stack([joined_sums[:width], joined_sums[2 * width :]])
        first_in_grad = jnp.dot(joined_grad, input_weight.T, preferred_element_type=jnp.float32)
        rows_part, first_gain_part, first_shift_part = jax.vjp(
            norm_rows, rows_in, first_gain, first_shift
        )[1](first_in_grad)
        sums[0] = sums[0] + first_gain_part
        sums[1] = sums[1] + first_shift_part
        input_grads.append(
            (rows_part + middle_grad).astype(jnp.bfloat16).reshape(rows_micro, slots, width)
        )
    totals = lax.psum(
        (
            sums[0],
            sums[1],
            sums[2],
            sums[3],
            sums[4],
            sums[5],
            sums[6],
            sums[7],
            sums[8],
            sums[9],
            sums[10],
            sums[11],
        ),
        ("rows", "blk"),
    )
    return (
        jnp.concatenate(results, axis=0),
        jnp.concatenate(input_grads, axis=0),
        totals[0],
        totals[1],
        totals[2],
        totals[3],
        totals[4],
        totals[5],
        totals[6],
        totals[7],
        totals[8],
        totals[9],
        totals[10],
        totals[11],
    )


def swap(value, axis, bit):
    return lax.ppermute(value, axis, [(i, i ^ bit) for i in range(lax.axis_size(axis))])


def side(axis, bit):
    return (lax.axis_index(axis) // bit) % 2


def after(value, *others):
    return lax.optimization_barrier((value, *others))[0]


def add_low(a, b):
    return (a.astype(F32) + b.astype(F32)).astype(BF16)


def axis_bits(axis):
    bits, bit = [], 1
    while bit < lax.axis_size(axis):
        bits.append((axis, bit))
        bit *= 2
    return bits


def scatter_sum(keep, recv, order):
    for axis, bit in order:
        half = keep.shape[0] // 2
        own = side(axis, bit)

        def part(which, keep=keep, recv=recv, half=half):
            return add_low(
                lax.dynamic_slice_in_dim(keep, which * half, half, 0),
                lax.dynamic_slice_in_dim(recv, which * half, half, 0),
            )

        recv = swap(part(1 - own), axis, bit)
        keep = part(own)
    return add_low(keep, recv)


def in_order(mine, other, own, dim):
    mine, other = jnp.expand_dims(mine, dim), jnp.expand_dims(other, dim)
    shape = [1] * mine.ndim
    shape[dim] = 2
    place = lax.broadcasted_iota(jnp.int32, shape, dim)
    return jnp.where(place == own, mine, other)


def gather_back(block, order):
    for axis, bit in reversed(order):
        pair = in_order(block, swap(block, axis, bit), side(axis, bit), 0)
        block = pair.reshape(2 * block.shape[0], block.shape[1])
    return block


def sum_weights(make, orders, dim):
    own = side("blk", 1)
    send = make(1 - own)
    recv = swap(send, "blk", 1)
    keep = make(own)
    cols = keep.shape[1] // len(orders)
    parts = []
    for i, order in enumerate(orders):
        cut = slice(i * cols, (i + 1) * cols)
        parts.append(gather_back(scatter_sum(keep[:, cut], recv[:, cut], order), order))
    block = jnp.concatenate(parts, axis=1) if len(parts) > 1 else parts[0]
    return in_order(block, swap(block, "blk", 1), own, dim).astype(F32)


def sum_small(value):
    for axis, bit in axis_bits("blk") + axis_bits("rows"):
        value = value + swap(value, axis, bit)
    return value


def half_cols(array, which, size):
    return lax.dynamic_slice_in_dim(array, which * size, size, 1)


def local_rows(
    inputs,
    image_index,
    keep_mask,
    first_gain,
    first_shift,
    input_weight,
    input_bias,
    output_weight,
    output_bias,
    second_gain,
    second_shift,
    up_weight,
    up_bias,
    down_weight,
    down_bias,
    cotangent,
):
    blocks, span, width = inputs.shape
    ff = up_weight.shape[1]
    me = lax.axis_index("blk")

    def row_piece(array, s):
        return lax.dynamic_index_in_dim(array, me ^ s, 0, keepdims=False)

    ids = [row_piece(image_index, 0)] + [swap(row_piece(image_index, s), "blk", s) for s in range(1, blocks)]
    xs_in = [row_piece(inputs, 0)] + [swap(row_piece(inputs, s), "blk", s) for s in range(1, blocks)]
    cots = [row_piece(cotangent, 0)] + [
        swap(after(row_piece(cotangent, s), xs_in[-1]), "blk", s) for s in range(1, blocks)
    ]
    ids = jnp.concatenate(ids)
    image = jnp.where(ids < 0, 4, ids)
    order_key = image * ids.shape[0] + jnp.arange(ids.shape[0], dtype=jnp.int32)
    less = (order_key[None, :] < order_key[:, None]).astype(jnp.int32)
    rank = jnp.sum(less, axis=1)
    starts = jnp.sum((image[None, :] < jnp.arange(6, dtype=jnp.int32)[:, None]).astype(jnp.int32), axis=1)
    keep = lax.dynamic_index_in_dim(keep_mask, me, 0, keepdims=False).astype(F32) / keep_rate
    rank_row, rank_col = rank[None, :], rank[:, None]

    paired = input_weight.reshape(width, 3, PAIRS, PAIR).transpose(0, 2, 1, 3).reshape(width, 3 * width)
    bias = jnp.stack([input_bias[0], jnp.zeros_like(input_bias[0]), input_bias[1]])
    bias = bias.reshape(3, PAIRS, PAIR).transpose(1, 0, 2).reshape(1, 3 * width)

    xs, normed, qkv = qkv_call(rank_row, xs_in, first_gain[None], first_shift[None], paired, bias)
    attended, stat = forward_call(starts, qkv)
    vectors = jnp.stack([output_bias, second_gain, second_shift, down_bias])
    (result, middle_grad, att_low, normed2, active, hidden, mlp_grad, branch, att_grad, sums2, up_sums) = mlp_call(
        keep, rank_row, cots, attended, xs, output_weight, up_weight, down_weight, vectors, up_bias[None]
    )

    y, x = axis_bits("blk")[1:], axis_bits("rows")[:1]
    z = axis_bits("rows")[1:]
    low_z, high_z = z[:1], z[1:]
    thirds = [x + low_z + y + high_z, low_z + x + y + high_z, y + x + low_z + high_z]
    down_total = sum_weights(lambda h: dot_tn(half_cols(active, h, ff // 2), mlp_grad).astype(BF16), thirds, 0)
    up_total = sum_weights(lambda h: dot_tn(normed2, half_cols(hidden, h, ff // 2)).astype(BF16), thirds, 1)
    out_total = sum_weights(lambda h: dot_tn(att_low, half_cols(branch, h, width // 2)).astype(BF16), thirds[:1], 1)
    small = sum_small(jnp.concatenate([sums2[:4], up_sums.reshape(4, width)]))

    results = unsort_call(rank_col, result, blocks)
    groups = 3
    each = PAIRS // groups
    grads, bias_sums, input_totals = [], [], []
    for g in range(groups):
        grad, col_sums = backward_call(starts, qkv, att_grad, attended, stat, g * each, each)
        grads.append(grad)
        bias_sums.append(col_sums)
        total = sum_weights(
            lambda h, grad=grad: dot_tn(normed, half_cols(grad, h, 3 * PAIR * each // 2)).astype(BF16), thirds[g : g + 1], 1
        )
        input_totals.append(total.reshape(width, each, 3, PAIR))
    inputs_grad, sums1 = input_call(grads, paired, xs, middle_grad, first_gain[None])
    back = unsort_call(rank_col, inputs_grad, blocks)
    bias_sum = jnp.concatenate(bias_sums, axis=1).reshape(PAIRS, 3, PAIR).transpose(1, 0, 2).reshape(3, width)
    small_last = sum_small(jnp.concatenate([sums1[:2], bias_sum]))
    input_total = jnp.concatenate(input_totals, axis=1).transpose(0, 2, 1, 3).reshape(width, 3 * width)

    def send_back(pieces):
        home = [pieces[0]] + [swap(pieces[s], "blk", s) for s in range(1, blocks)]
        stacked = jnp.stack(home)
        return jnp.stack([lax.dynamic_index_in_dim(stacked, me ^ r, 0, keepdims=False) for r in range(blocks)])

    return (
        send_back(results),
        send_back(back),
        small_last[0],
        small_last[1],
        input_total,
        jnp.stack([small_last[2], small_last[4]]),
        out_total.reshape(width, width),
        small[3],
        small[0],
        small[1],
        up_total.reshape(width, ff),
        small[4:].reshape(ff),
        down_total.reshape(ff, width),
        small[2],
    )


def solution(mesh):
    blocks, groups = mesh.shape["blk"], mesh.shape["rows"]

    def run(*args):
        whole_rows = args[0].shape[0] // groups == blocks and blocks & (blocks - 1) == 0 and groups & (groups - 1) == 0
        return jax.shard_map(
            local_rows if whole_rows else local,
            mesh=mesh,
            in_specs=(P("rows", "blk", None), P("rows", "blk"), P("rows", None)) + (P(),) * 12 + (P("rows", "blk", None),),
            out_specs=(P("rows", "blk", None),) * 2 + (P(),) * 12,
            check_vma=False,
        )(*args)

    return run
```

```python
import functools

import jax
import jax.numpy as jnp
from jax import lax
from jax.experimental import pallas as pl
from jax.experimental.pallas import tpu as pltpu
from jax.sharding import PartitionSpec as P

HEADS = 12
HEAD_DIM = 64
PAIR = 2 * HEAD_DIM
PAIRS = HEADS // 2
eps_norm = 1e-06
keep_rate = 0.9
F32 = jnp.float32
BF16 = jnp.bfloat16
NEG = -1e30
VMEM = 62 * 1024 * 1024
QUICK = pl.CostEstimate(flops=1 << 20, bytes_accessed=1 << 16, transcendentals=0)


def dot(a, b):
    return jnp.dot(a, b, preferred_element_type=F32)


def dot_nt(a, b):
    return lax.dot_general(a, b, (((1,), (1,)), ((), ())), preferred_element_type=F32)


def dot_tn(a, b):
    return lax.dot_general(a, b, (((0,), (0,)), ((), ())), preferred_element_type=F32)


def whole(shape):
    return pl.BlockSpec(shape, lambda *g: (0,) * len(shape), pipeline_mode=pl.Buffered(1))


def centre_scale(values):
    centre = values - jnp.mean(values, axis=-1, keepdims=True)
    spread = jnp.mean(centre * centre, axis=-1, keepdims=True)
    inv = lax.rsqrt(spread + eps_norm)
    return centre * inv, inv


def norm_back(grad_hat, hat, inv):
    first = jnp.mean(grad_hat, axis=-1, keepdims=True)
    second = jnp.mean(grad_hat * hat, axis=-1, keepdims=True)
    return (grad_hat - first - hat * second) * inv


def sort_tile(rank_row, tile, step, pieces):
    span = pieces[0].shape[0]
    place = step * tile + lax.broadcasted_iota(jnp.int32, (tile, span), 0)
    total = None
    for i, piece in enumerate(pieces):
        pick = (rank_row[:, i * span : (i + 1) * span] == place).astype(BF16)
        part = dot(pick, piece[...])
        total = part if total is None else total + part
    return total


def qkv_kernel(n, tile, *refs):
    rank, *pieces = refs[: n + 1]
    gain, shift, weight, bias, xs_out, normed_out, qkv_out = refs[n + 1 :]
    xs = sort_tile(rank[...], tile, pl.program_id(0), pieces)
    xs_out[...] = xs.astype(BF16)
    hat, _ = centre_scale(xs)
    normed = (hat * gain[...] + shift[...]).astype(BF16)
    normed_out[...] = normed
    width = normed.shape[1]
    for j in range(3):
        cols = slice(j * width, (j + 1) * width)
        mixed = (dot(normed, weight[:, cols]) + bias[j : j + 1, :]).astype(BF16)
        qkv_out[j] = mixed * BF16(HEAD_DIM**-0.5) if j == 0 else mixed


def qkv_call(rank, pieces, gain, shift, weight, bias, tile=288):
    n = len(pieces)
    span, width = pieces[0].shape
    count = n * span
    return pl.pallas_call(
        functools.partial(qkv_kernel, n, tile),
        grid=(count // tile,),
        in_specs=[whole((1, count))]
        + [whole((span, width))] * n
        + [whole((1, width)), whole((1, width)), whole(weight.shape), whole(bias.shape)],
        out_specs=[
            pl.BlockSpec((tile, width), lambda i: (i, 0)),
            pl.BlockSpec((tile, width), lambda i: (i, 0)),
            pl.BlockSpec((3, tile, width), lambda i: (0, i, 0)),
        ],
        out_shape=[
            jax.ShapeDtypeStruct((count, width), BF16),
            jax.ShapeDtypeStruct((count, width), BF16),
            jax.ShapeDtypeStruct((3, count, width), BF16),
        ],
        compiler_params=pltpu.CompilerParams(vmem_limit_bytes=VMEM),
        cost_estimate=QUICK,
        name="sort_qkv",
    )(rank, *pieces, gain, shift, weight, bias)


SMALL = 304
LARGE = 384


def windows(starts, seg, length):
    first, last = starts[seg], starts[seg + 1]
    aligned = first // 16 * 16
    small = SMALL if seg < 4 else LARGE
    at_small = pl.multiple_of(jnp.minimum(aligned, length - small), 16)
    at_large = pl.multiple_of(jnp.minimum(aligned, length - LARGE), 16)
    return first, last, small, at_small, at_large


def inside(at, size, lanes, first, last):
    place = at + lax.broadcasted_iota(jnp.int32, (size, lanes), 0)
    return (place >= first) & (place < last)


def forward_kernel(starts, qkv, out, stat):
    length = qkv.shape[1]
    for seg in range(5):
        first, last, small, at_q, at_k = windows(starts, seg, length)
        rows_q = pl.ds(at_q, small)
        q = qkv[0, rows_q, :]
        k = qkv[1, pl.ds(at_k, LARGE), :]
        v = qkv[2, pl.ds(at_k, LARGE), :]
        lane = lax.broadcasted_iota(jnp.int32, (LARGE, PAIR), 1)
        lane_q = lax.broadcasted_iota(jnp.int32, (small, PAIR), 1)
        low = lane < HEAD_DIM
        seen = inside(at_k, LARGE, PAIR, first, last)
        zero = jnp.zeros((LARGE, PAIR), BF16)
        one = jnp.ones((LARGE, PAIR), BF16)
        bias = jnp.where((lane == 0) & ~seen, NEG, 0.0).astype(BF16)
        q_ext = jnp.concatenate([q, (lane_q == 0).astype(BF16)], axis=1)
        tops, weights, mixes = [], [], []
        for half in (low, ~low):
            k_ext = jnp.concatenate([jnp.where(half, k, zero), bias], axis=1)
            scores = dot_nt(q_ext, k_ext)
            top = jnp.max(scores, axis=-1, keepdims=True)
            tops.append(top)
            weights.append(jnp.exp(scores - top).astype(BF16))
            mixes.append(jnp.concatenate([jnp.where(half, v, zero), jnp.where(half, one, zero)], axis=1))
        both = dot(jnp.concatenate(weights, axis=1), jnp.concatenate(mixes, axis=0))
        total = both[:, PAIR:]
        peak = jnp.where(lane_q < HEAD_DIM, tops[0], tops[1])
        mine = inside(at_q, small, PAIR, first, last)
        out[rows_q, :] = jnp.where(mine, both[:, :PAIR] / total, out[rows_q, :])
        stat[rows_q, :] = jnp.where(mine, peak + jnp.log(total), stat[rows_q, :])


def forward_call(starts, qkv):
    _, count, wide = qkv.shape
    pairs = wide // PAIR
    return pl.pallas_call(
        forward_kernel,
        grid_spec=pltpu.PrefetchScalarGridSpec(
            num_scalar_prefetch=1,
            grid=(pairs,),
            in_specs=[pl.BlockSpec((3, count, PAIR), lambda p, s: (0, 0, p))],
            out_specs=[
                pl.BlockSpec((count, PAIR), lambda p, s: (0, p)),
                pl.BlockSpec((count, PAIR), lambda p, s: (0, p)),
            ],
        ),
        out_shape=[jax.ShapeDtypeStruct((count, pairs * PAIR), F32)] * 2,
        compiler_params=pltpu.CompilerParams(vmem_limit_bytes=VMEM),
        cost_estimate=QUICK,
        name="attention_forward",
    )(starts, qkv)


def split3(value):
    high = value.astype(BF16)
    rest = value - high.astype(F32)
    mid = rest.astype(BF16)
    return high, mid, (rest - mid.astype(F32)).astype(BF16)


def backward_kernel(starts, qkv, grad, att, stat, *refs):
    out, sums = refs[-2:]
    length = qkv.shape[1]
    third = lax.broadcasted_iota(jnp.int32, (PAIR, PAIR), 0) // HEAD_DIM
    block = (third == lax.broadcasted_iota(jnp.int32, (PAIR, PAIR), 1) // HEAD_DIM).astype(BF16)
    for seg in range(5):
        first, last, small, at_k, at_q = windows(starts, seg, length)
        rows_q, rows_k = pl.ds(at_q, LARGE), pl.ds(at_k, small)
        lane_q = lax.broadcasted_iota(jnp.int32, (LARGE, PAIR), 1)
        lane_k = lax.broadcasted_iota(jnp.int32, (small, PAIR), 1)
        spot_q, spot_k = lane_q % HEAD_DIM, lane_k % HEAD_DIM
        mine_q = inside(at_q, LARGE, PAIR, first, last)
        mine_k = inside(at_k, small, PAIR, first, last)
        zero_q = jnp.zeros((LARGE, PAIR), BF16)
        zero_k = jnp.zeros((small, PAIR), BF16)
        q = qkv[0, rows_q, :]
        k = jnp.where(mine_k, qkv[1, rows_k, :], zero_k)
        v = qkv[2, rows_k, :]
        g = jnp.where(mine_q, grad[rows_q, :], zero_q)
        prod = g.astype(F32) * jnp.where(mine_q, att[rows_q, :], 0.0)
        p_high = prod.astype(BF16)
        p_low = (prod - p_high.astype(F32)).astype(BF16)
        inner = dot(p_high, block) + dot(p_low, block)
        logs = jnp.where(mine_q, stat[rows_q, :], 0.0)

        def spread(value, fifth):
            a, b, c = split3(value)
            return jnp.where(
                spot_q == 0, a, jnp.where(spot_q == 1, b, jnp.where(spot_q == 2, c, fifth))
            )

        query_bias = jnp.where(mine_q, 0.0, NEG).astype(BF16)
        unit = jnp.ones((LARGE, PAIR), BF16)
        q_ext = jnp.concatenate(
            [q, spread(logs, jnp.where(spot_q == 3, unit, jnp.where(spot_q == 4, query_bias, zero_q)))], axis=1
        )
        g_ext = jnp.concatenate([g, spread(inner, zero_q)], axis=1)
        key_bias = jnp.where(mine_k, 0.0, NEG).astype(BF16)
        minus = jnp.where(spot_k < 3, -1.0, 0.0).astype(BF16)
        k_tail = jnp.where(
            spot_k == 3, key_bias, jnp.where(spot_k == 4, jnp.ones((small, PAIR), BF16), minus)
        )
        probs, score_grads, ks, gs, qs = [], [], [], [], []
        for h in range(2):
            half_k = lane_k // HEAD_DIM == h
            half_q = lane_q // HEAD_DIM == h
            k_half = jnp.where(half_k, k, zero_k)
            shifted = dot_nt(jnp.concatenate([k_half, jnp.where(half_k, k_tail, zero_k)], axis=1), q_ext)
            prob = jnp.exp(shifted)
            v_half = jnp.where(half_k, v, zero_k)
            prob_grad = dot_nt(jnp.concatenate([v_half, jnp.where(half_k, minus, zero_k)], axis=1), g_ext)
            probs.append(prob.astype(BF16))
            score_grads.append((prob * prob_grad).astype(BF16))
            ks.append(k_half)
            gs.append(jnp.where(half_q, g, zero_q))
            qs.append(jnp.where(half_q, q, zero_q))
        value_grad = dot(jnp.concatenate(probs, axis=1), jnp.concatenate(gs, axis=0))
        key_grad = dot(jnp.concatenate(score_grads, axis=1), jnp.concatenate(qs, axis=0))
        query_grad = dot_tn(jnp.concatenate(score_grads, axis=0), jnp.concatenate(ks, axis=0))
        query_grad = (query_grad * HEAD_DIM**-0.5).astype(BF16)
        out[0, rows_q, :] = jnp.where(mine_q, query_grad, out[0, rows_q, :])
        out[1, rows_k, :] = jnp.where(mine_k, key_grad.astype(BF16), out[1, rows_k, :])
        out[2, rows_k, :] = jnp.where(mine_k, value_grad.astype(BF16), out[2, rows_k, :])
    for j in range(3):
        sums[j : j + 1, :] = jnp.sum(out[j].astype(F32), axis=0, keepdims=True)


def backward_call(starts, qkv, grad, att, stat, first_pair, pairs, before=None):
    _, count, width = qkv.shape
    held = [] if before is None else list(before)
    return pl.pallas_call(
        backward_kernel,
        grid_spec=pltpu.PrefetchScalarGridSpec(
            num_scalar_prefetch=1,
            grid=(pairs,),
            in_specs=[pl.BlockSpec((3, count, PAIR), lambda p, s: (0, 0, p + first_pair))]
            + [pl.BlockSpec((count, PAIR), lambda p, s: (0, p + first_pair))] * 3
            + [pl.BlockSpec(memory_space=pl.ANY)] * len(held),
            out_specs=[
                pl.BlockSpec((3, count, PAIR), lambda p, s: (0, 0, p + first_pair)),
                pl.BlockSpec((8, PAIR), lambda p, s: (0, p + first_pair)),
            ],
        ),
        out_shape=[
            jax.ShapeDtypeStruct((3, count, width), BF16),
            jax.ShapeDtypeStruct((8, width), F32),
        ],
        input_output_aliases={5: 0, 6: 1} if held else {},
        compiler_params=pltpu.CompilerParams(vmem_limit_bytes=VMEM),
        cost_estimate=QUICK,
        name="attention_backward",
    )(starts, qkv, grad, att, stat, *held)


ERF = (0.254829592, -0.284496736, 1.421413741, -1.453152027, 1.061405429)


def gelu_pair(u):
    size = jnp.abs(u)
    t = 1.0 / (1.0 + (0.3275911 * 0.5**0.5) * size)
    bell = jnp.exp(u * u * -0.5)
    poly = ERF[4] * t + ERF[3]
    for c in (ERF[2], ERF[1], ERF[0]):
        poly = poly * t + c
    tail = 0.5 * poly * t * bell
    phi = jnp.where(u < 0, tail, 1.0 - tail)
    return u * phi, phi + u * bell * 0.3989422804014327


def middle_kernel(n, tile, *refs):
    keep, rank, *pieces = refs[: n + 2]
    att, xs, out_w, vectors, cot_out, att_low_out, middle_out, normed_out, mlp_out, sums = refs[n + 2 :]
    step = pl.program_id(0)
    cot = sort_tile(rank[...], tile, step, pieces)
    cot_out[...] = cot.astype(BF16)
    mlp_grad = (cot * keep[1]).astype(BF16)
    mlp_out[...] = mlp_grad
    att_low = att[...].astype(BF16)
    att_low_out[...] = att_low
    middle = xs[...].astype(F32) + keep[0] * (dot(att_low, out_w[...]) + vectors[0:1, :])
    middle_out[...] = middle
    hat, _ = centre_scale(middle)
    normed_out[...] = (hat * vectors[1:2, :] + vectors[2:3, :]).astype(BF16)

    @pl.when(step == 0)
    def _():
        sums[...] = jnp.zeros_like(sums)

    sums[0:1, :] += jnp.sum(mlp_grad.astype(F32), axis=0, keepdims=True)


def middle_call(keep, rank, pieces, att, xs, out_w, vectors, tile=384):
    n = len(pieces)
    span, width = pieces[0].shape
    count = n * span
    rows = pl.BlockSpec((tile, width), lambda i: (i, 0))
    low, full = jax.ShapeDtypeStruct((count, width), BF16), jax.ShapeDtypeStruct((count, width), F32)
    return pl.pallas_call(
        functools.partial(middle_kernel, n, tile),
        grid=(count // tile,),
        in_specs=[pl.BlockSpec(memory_space=pltpu.SMEM), whole((1, count))]
        + [whole((span, width))] * n
        + [rows, rows, whole(out_w.shape), whole(vectors.shape)],
        out_specs=[rows] * 5 + [pl.BlockSpec((8, width), lambda i: (0, 0))],
        out_shape=[low, low, full, low, low, jax.ShapeDtypeStruct((8, width), F32)],
        compiler_params=pltpu.CompilerParams(vmem_limit_bytes=VMEM),
        cost_estimate=QUICK,
        name="middle",
    )(keep, rank, *pieces, att, xs, out_w, vectors)


def mlp_kernel(parts, core, keep, normed, mlp_grad, middle, cot, out_w, vectors, up_w, up_b, down_w, *refs):
    (
        up_send, up_keep, down_send, down_keep, up_sums, result, middle_grad_out, branch_out, att_grad_out, sums,
        lift, back, act_all, hidden_all,
    ) = refs
    step, steps = pl.program_id(0), pl.num_programs(0)
    count = normed.shape[0]
    cuts = [slice(i * (count // parts), (i + 1) * (count // parts)) for i in range(parts)]

    @pl.when(step == 0)
    def _():
        lift[...] = jnp.zeros_like(lift)
        back[...] = jnp.zeros_like(back)

    total = jnp.zeros(up_sums.shape, F32)
    for rows in cuts:
        act, slope = gelu_pair(dot(normed[rows, :], up_w[...]) + up_b[...])
        act = act.astype(BF16)
        act_all[rows, :] = act
        hidden = (dot_nt(mlp_grad[rows, :], down_w[...]) * slope).astype(BF16)
        hidden_all[rows, :] = hidden
        total = total + jnp.sum(hidden.astype(F32), axis=0, keepdims=True)
        lift[rows, :] += dot(act, down_w[...])
        back[rows, :] += dot_nt(hidden, up_w[...])
    up_sums[...] = total
    up_part = dot_tn(normed[...], hidden_all[...]).astype(BF16)
    down_part = dot_tn(act_all[...], mlp_grad[...]).astype(BF16)

    @pl.when(step < steps // 2)
    def _():
        up_send[...] = up_part
        down_send[...] = down_part

    @pl.when(step >= steps // 2)
    def _():
        up_keep[...] = up_part
        down_keep[...] = down_part

    @pl.when(step == steps - 1)
    def _():
        gain, down_b = vectors[1:2, :], vectors[3:4, :]
        sums[...] = jnp.zeros_like(sums)
        for rows in cuts:
            mid, grad = middle[rows, :], back[rows, :]
            hat, inv = centre_scale(mid)
            result[rows, :] = (mid + keep[1] * (lift[rows, :] + down_b)).astype(BF16)
            middle_grad = cot[rows, :].astype(F32) + norm_back(grad * gain, hat, inv)
            middle_grad_out[rows, :] = middle_grad
            branch = (keep[0] * middle_grad).astype(BF16)
            branch_out[rows, :] = branch
            att_grad_out[rows, :] = dot_nt(branch, out_w[...]).astype(BF16)
            sums[0:1, :] += jnp.sum(grad * hat, axis=0, keepdims=True)
            sums[1:2, :] += jnp.sum(grad, axis=0, keepdims=True)
            sums[2:3, :] += jnp.sum(branch.astype(F32), axis=0, keepdims=True)


def mlp_call(core, keep, normed, mlp_grad, middle, cot, out_w, vectors, up_w, up_b, down_w, chunk=512, parts=3):
    count, width = normed.shape
    ff = up_w.shape[1]
    half = ff // 2 // chunk

    def place(i, c):
        return jnp.where(i < half, (1 - c[0]) * half + i, c[0] * half + i - half)

    low, full = jax.ShapeDtypeStruct((count, width), BF16), jax.ShapeDtypeStruct((count, width), F32)
    up_part, down_part = jax.ShapeDtypeStruct((width, ff // 2), BF16), jax.ShapeDtypeStruct((ff // 2, width), BF16)
    return pl.pallas_call(
        functools.partial(mlp_kernel, parts),
        grid_spec=pltpu.PrefetchScalarGridSpec(
            num_scalar_prefetch=1,
            grid=(2 * half,),
            in_specs=[
                pl.BlockSpec(memory_space=pltpu.SMEM),
                whole((count, width)),
                whole((count, width)),
                whole((count, width)),
                whole((count, width)),
                whole(out_w.shape),
                whole(vectors.shape),
                pl.BlockSpec((width, chunk), lambda i, c: (0, place(i, c))),
                pl.BlockSpec((1, chunk), lambda i, c: (0, place(i, c))),
                pl.BlockSpec((chunk, width), lambda i, c: (place(i, c), 0)),
            ],
            out_specs=[
                pl.BlockSpec((width, chunk), lambda i, c: (0, jnp.minimum(i, half - 1))),
                pl.BlockSpec((width, chunk), lambda i, c: (0, jnp.maximum(i - half, 0))),
                pl.BlockSpec((chunk, width), lambda i, c: (jnp.minimum(i, half - 1), 0)),
                pl.BlockSpec((chunk, width), lambda i, c: (jnp.maximum(i - half, 0), 0)),
                pl.BlockSpec((1, chunk), lambda i, c: (0, place(i, c))),
            ]
            + [whole((count, width))] * 4
            + [whole((8, width))],
            scratch_shapes=[pltpu.VMEM((count, width), F32)] * 2 + [pltpu.VMEM((count, chunk), BF16)] * 2,
        ),
        out_shape=[up_part, up_part, down_part, down_part, jax.ShapeDtypeStruct((1, ff), F32)]
        + [low, full, low, low, jax.ShapeDtypeStruct((8, width), F32)],
        compiler_params=pltpu.CompilerParams(vmem_limit_bytes=VMEM),
        cost_estimate=QUICK,
        name="mlp",
    )(core, keep, normed, mlp_grad, middle, cot, out_w, vectors, up_w, up_b, down_w)


def input_kernel(grads, weight, xs, middle_grad, gain, out, sums):
    span = xs.shape[1]
    back = None
    for j in range(3):
        part = dot_nt(grads[j], weight[:, j * span : (j + 1) * span])
        back = part if back is None else back + part
    hat, inv = centre_scale(xs[...].astype(F32))
    out[...] = (middle_grad[...] + norm_back(back * gain[...], hat, inv)).astype(BF16)

    @pl.when(pl.program_id(0) == 0)
    def _():
        sums[...] = jnp.zeros_like(sums)

    sums[0:1, :] += jnp.sum(back * hat, axis=0, keepdims=True)
    sums[1:2, :] += jnp.sum(back, axis=0, keepdims=True)


def input_call(grads, weight, xs, middle_grad, gain, tile=288):
    count, width = xs.shape
    return pl.pallas_call(
        input_kernel,
        grid=(count // tile,),
        in_specs=[pl.BlockSpec((3, tile, width), lambda i: (0, i, 0))]
        + [
            whole(weight.shape),
            pl.BlockSpec((tile, width), lambda i: (i, 0)),
            pl.BlockSpec((tile, width), lambda i: (i, 0)),
            whole((1, width)),
        ],
        out_specs=[pl.BlockSpec((tile, width), lambda i: (i, 0)), pl.BlockSpec((8, width), lambda i: (0, 0))],
        out_shape=[jax.ShapeDtypeStruct((count, width), BF16), jax.ShapeDtypeStruct((8, width), F32)],
        compiler_params=pltpu.CompilerParams(vmem_limit_bytes=VMEM),
        cost_estimate=QUICK,
        name="input_backward",
    )(grads, weight, xs, middle_grad, gain)


def unsort_kernel(n, rank, xs, *outs):
    count = xs.shape[0]
    span = count // n
    place = lax.broadcasted_iota(jnp.int32, (span, count), 1)
    for i, out in enumerate(outs):
        pick = (rank[i * span : (i + 1) * span, :] == place).astype(BF16)
        out[...] = dot(pick, xs[...]).astype(BF16)


def unsort_call(rank_col, xs, n):
    count, width = xs.shape
    span = count // n
    return pl.pallas_call(
        functools.partial(unsort_kernel, n),
        out_shape=[jax.ShapeDtypeStruct((span, width), BF16)] * n,
        compiler_params=pltpu.CompilerParams(vmem_limit_bytes=VMEM),
        cost_estimate=QUICK,
        name="unsort",
    )(rank_col, xs)


def weights_kernel(half, left, right, out):
    out[...] = dot_tn(left[...], right[...]).astype(BF16)


def weights_call(half, left, right, split_left, tile=768):
    count, m = left.shape
    n = right.shape[1]
    tiles = (m if split_left else n) // 2 // tile

    def cut(i, h):
        return (0, h[0] * tiles + i)

    if split_left:
        specs = [pl.BlockSpec((count, tile), cut), whole((count, n))]
        out, out_spec = (m // 2, n), pl.BlockSpec((tile, n), lambda i, h: (i, 0))
    else:
        specs = [whole((count, m)), pl.BlockSpec((count, tile), cut)]
        out, out_spec = (m, n // 2), pl.BlockSpec((m, tile), lambda i, h: (0, i))
    return pl.pallas_call(
        weights_kernel,
        grid_spec=pltpu.PrefetchScalarGridSpec(
            num_scalar_prefetch=1, grid=(tiles,), in_specs=specs, out_specs=out_spec
        ),
        out_shape=jax.ShapeDtypeStruct(out, BF16),
        compiler_params=pltpu.CompilerParams(vmem_limit_bytes=VMEM),
        cost_estimate=QUICK,
        name="weights",
    )(half, left, right)


def input_weights_kernel(half, normed, grads, *refs):
    out, piece = refs[-1], normed[...]
    span = grads.shape[2]
    for j in range(3):
        out[:, j * span : (j + 1) * span] = dot_tn(piece, grads[j]).astype(BF16)
    if len(refs) == 3:
        out[:, 3 * span :] = dot_tn(refs[0][...], refs[1][...]).astype(BF16)


def input_weights_call(half, normed, grads, part, parts, *more):
    count, width = normed.shape
    span = width // parts
    cols = 3 * span + (more[1].shape[1] if more else 0)
    extra = [pl.BlockSpec((count, width // 2), lambda i, h: (0, h[0])), whole((count, width))] if more else []
    return pl.pallas_call(
        input_weights_kernel,
        grid_spec=pltpu.PrefetchScalarGridSpec(
            num_scalar_prefetch=1,
            grid=(1,),
            in_specs=[
                pl.BlockSpec((count, width // 2), lambda i, h: (0, h[0])),
                pl.BlockSpec((3, count, span), lambda i, h: (0, 0, part)),
            ]
            + extra,
            out_specs=whole((width // 2, cols)),
        ),
        out_shape=jax.ShapeDtypeStruct((width // 2, cols), BF16),
        compiler_params=pltpu.CompilerParams(vmem_limit_bytes=VMEM),
        cost_estimate=QUICK,
        name="input_weights",
    )(half, normed, grads, *more)


GROUP = 8


def final_call(core, places, pairs, name, spread, outs):
    groups = places.shape[0] // 2 - 1
    n = len(pairs)

    def kernel(c, t, *refs):
        h = pl.program_id(0)
        turn = t[2 * groups + h]

        def write(sources):
            blocks = [ref[...].astype(F32) for ref in sources]
            rows = [block.shape[0] // GROUP for block in blocks]
            for j in range(GROUP):
                spread([b[j * r : (j + 1) * r] for b, r in zip(blocks, rows)], j ^ turn, refs[2 * n :])

        pl.when(h == 0)(lambda: write(refs[:n]))
        pl.when(h == 1)(lambda: write(refs[n : 2 * n]))

    def in_spec(array, which):
        rows = array.shape[0] // groups
        if which == 0:
            return pl.BlockSpec((rows, array.shape[1]), lambda h, s, c, t: (jnp.where(h == 0, s, groups - 1), 0))
        return pl.BlockSpec((rows, array.shape[1]), lambda h, s, c, t: (jnp.where(h == 0, 0, s), 0))

    def out_spec(block, index):
        return pl.BlockSpec(block, lambda h, s, c, t: index(jnp.where(h == 0, c[0], 1 - c[0]), t[h * groups + s]))

    return pl.pallas_call(
        kernel,
        grid_spec=pltpu.PrefetchScalarGridSpec(
            num_scalar_prefetch=2,
            grid=(2, groups),
            in_specs=[in_spec(p[0], 0) for p in pairs] + [in_spec(p[1], 1) for p in pairs],
            out_specs=[out_spec(block, index) for _, block, index in outs],
        ),
        out_shape=[jax.ShapeDtypeStruct(shape, F32) for shape, _, _ in outs],
        compiler_params=pltpu.CompilerParams(vmem_limit_bytes=VMEM),
        cost_estimate=QUICK,
        name=name,
    )(core, places, *[p[0] for p in pairs], *[p[1] for p in pairs])


def rows_at(ref, place, value, *cols):
    rows = value.shape[0]
    ref[(pl.ds(pl.multiple_of(place * rows, 8), rows), *cols)] = value


def down_final(core, places, held, other):
    rows, cols = held.shape
    groups = places.shape[0] // 2 - 1
    block = (rows // groups, cols)

    def spread(blocks, place, refs):
        rows_at(refs[0], place, blocks[0], slice(None))

    outs = [((2 * rows, cols), block, lambda h, t: (h * groups + t, 0))]
    return final_call(core, places, [(held, other)], "down_final", spread, outs)[0]


def up_final(core, places, held, other):
    rows, cols = held.shape
    groups = places.shape[0] // 2 - 1

    def spread(blocks, place, refs):
        rows_at(refs[0], place, blocks[0], slice(None))

    outs = [((rows, 2 * cols), (rows // groups, cols), lambda h, t: (t, h))]
    return final_call(core, places, [(held, other)], "up_final", spread, outs)[0]


def input_final(core, places, pairs):
    half = pairs[0][0].shape[0]
    width = 2 * half
    groups = places.shape[0] // 2 - 1
    span = width // len(pairs)

    def spread(blocks, place, refs):
        for g, block in enumerate(blocks):
            for j in range(3):
                at = j * width + g * span
                rows_at(refs[0], place, block[:, j * span : (j + 1) * span], slice(at, at + span))
        rows_at(refs[1], place, blocks[0][:, 3 * span :], slice(None))

    index = lambda h, t: (h * groups + t, 0)
    outs = [((width, 3 * width), (half // groups, 3 * width), index), ((width, width), (half // groups, width), index)]
    return final_call(core, places, pairs, "input_final", spread, outs)


MICRO = 2


def from_behind(value, axis, steps):
    count = lax.axis_size(axis)
    pairs = [(source, (source + steps) % count) for source in range(count)]
    return lax.ppermute(value, axis, pairs)


def norm_rows(values, gain, shift):
    centre = values - jnp.mean(values, axis=-1, keepdims=True)
    spread = jnp.mean(centre * centre, axis=-1, keepdims=True)
    return centre * lax.rsqrt(spread + eps_norm) * gain + shift


def gelu_exact(values):
    return jax.nn.gelu(values, approximate=False)


def split_heads(block):
    return block.reshape(block.shape[0], block.shape[1], HEADS, HEAD_DIM)


def take_rows(array, first_row, count_rows):
    return lax.slice_in_dim(array, first_row, first_row + count_rows, axis=0)


def masked_scores(query, keys, ids_query, ids_keys):
    scores = jnp.einsum(
        "rqhd,rkhd->rhqk", split_heads(query), split_heads(keys), preferred_element_type=jnp.float32
    ) * HEAD_DIM ** (-0.5)
    same = ids_query[:, None, :, None] == ids_keys[:, None, None, :]
    return jnp.where(same, scores, -jnp.inf)


def attend_piece(carry, query, ids_query, piece):
    keys, values, ids_keys = piece
    peak, total, accum = carry
    scores = masked_scores(query, keys, ids_query, ids_keys)
    top = jnp.maximum(peak, jnp.max(scores, axis=-1))
    weights = jnp.exp(scores - top[..., None])
    total = jnp.sum(weights, axis=-1)
    update = jnp.einsum(
        "rhqk,rkhd->rqhd",
        weights.astype(jnp.bfloat16),
        split_heads(values),
        preferred_element_type=jnp.float32,
    )
    return (top, total, update.reshape(accum.shape))


def attention_forward(query, keys, values, ids_query):
    rows_here, slots, width = query.shape
    start_state = (
        jnp.full((rows_here, HEADS, slots), -1e30, jnp.float32),
        jnp.zeros((rows_here, HEADS, slots), jnp.float32),
        jnp.zeros((rows_here, slots, width), jnp.float32),
    )
    carry = attend_piece(
        start_state,
        query,
        ids_query,
        (
            lax.all_gather(keys, "blk", axis=1, tiled=True),
            lax.all_gather(values, "blk", axis=1, tiled=True),
            lax.all_gather(ids_query, "blk", axis=1, tiled=True),
        ),
    )
    return (carry[0], carry[1], carry[2], None)


def attention_back(query, out_grad, ids_query, log_total, inner, piece):
    keys, values, ids_keys = piece
    scale = HEAD_DIM ** (-0.5)
    scores = masked_scores(query, keys, ids_query, ids_keys)
    probs = jnp.exp(scores - log_total[..., None])
    prob_grad = jnp.einsum(
        "rqhd,rkhd->rhqk",
        split_heads(out_grad),
        split_heads(values),
        preferred_element_type=jnp.float32,
    )
    score_grad = (probs * (prob_grad - inner[..., None])).astype(jnp.bfloat16)
    value_grad = jnp.einsum(
        "rhqk,rqhd->rkhd",
        probs.astype(jnp.bfloat16),
        split_heads(out_grad),
        preferred_element_type=jnp.float32,
    )
    key_grad = (
        jnp.einsum(
            "rhqk,rqhd->rkhd", score_grad, split_heads(query), preferred_element_type=jnp.float32
        )
        * scale
    )
    query_grad = (
        jnp.einsum(
            "rhqk,rkhd->rqhd", score_grad, split_heads(keys), preferred_element_type=jnp.float32
        )
        * scale
    )
    return (
        query_grad.reshape(query.shape),
        key_grad.reshape(keys.shape),
        value_grad.reshape(values.shape),
    )


def local(
    inputs,
    image_index,
    keep_mask,
    first_gain,
    first_shift,
    input_weight,
    input_bias,
    output_weight,
    output_bias,
    second_gain,
    second_shift,
    up_weight,
    up_bias,
    down_weight,
    down_bias,
    cotangent,
):
    rows_local, slots, width = inputs.shape
    rows_micro = rows_local // MICRO
    count = rows_micro * slots
    blocks = lax.axis_size("blk")
    params = (
        first_gain,
        first_shift,
        input_weight,
        input_bias,
        output_weight,
        output_bias,
        second_gain,
        second_shift,
        up_weight,
        up_bias,
        down_weight,
        down_bias,
    )
    sums = [jnp.zeros(item.shape, jnp.float32) for item in params]
    results = []
    input_grads = []
    for micro in range(MICRO):
        first_row = micro * rows_micro
        rows_in = take_rows(inputs, first_row, rows_micro).astype(jnp.float32).reshape(count, width)
        out_cot = (
            take_rows(cotangent, first_row, rows_micro).astype(jnp.float32).reshape(count, width)
        )
        ids_query = take_rows(image_index, first_row, rows_micro).astype(jnp.bfloat16)
        keep = take_rows(keep_mask, first_row, rows_micro).astype(jnp.float32) / keep_rate
        keep_attn = jnp.broadcast_to(keep[:, None, 0:1], (rows_micro, slots, 1)).reshape(count, 1)
        keep_mlp = jnp.broadcast_to(keep[:, None, 1:2], (rows_micro, slots, 1)).reshape(count, 1)
        normed = norm_rows(rows_in, first_gain, first_shift).astype(jnp.bfloat16)
        mixed = jnp.dot(normed, input_weight, preferred_element_type=jnp.float32)
        query = (
            (mixed[:, :width] + input_bias[0])
            .astype(jnp.bfloat16)
            .reshape(rows_micro, slots, width)
        )
        keys = mixed[:, width : 2 * width].astype(jnp.bfloat16).reshape(rows_micro, slots, width)
        values = (
            (mixed[:, 2 * width :] + input_bias[1])
            .astype(jnp.bfloat16)
            .reshape(rows_micro, slots, width)
        )
        top, total, accum, whole = attention_forward(query, keys, values, ids_query)
        attended = (split_heads(accum) / jnp.transpose(total, (0, 2, 1))[..., None]).reshape(
            count, width
        )
        log_total = top + jnp.log(total)
        attended_low = attended.astype(jnp.bfloat16)
        branch = (
            jnp.dot(attended_low, output_weight, preferred_element_type=jnp.float32) + output_bias
        )
        middle = rows_in + keep_attn * branch
        normed_second = norm_rows(middle, second_gain, second_shift).astype(jnp.bfloat16)
        hidden = jnp.dot(normed_second, up_weight, preferred_element_type=jnp.float32) + up_bias
        active = gelu_exact(hidden).astype(jnp.bfloat16)
        branch_second = jnp.dot(active, down_weight, preferred_element_type=jnp.float32) + down_bias
        results.append(
            (middle + keep_mlp * branch_second)
            .astype(jnp.bfloat16)
            .reshape(rows_micro, slots, width)
        )
        mlp_grad = (out_cot * keep_mlp).astype(jnp.bfloat16)
        sums[10] = sums[10] + jnp.dot(active.T, mlp_grad, preferred_element_type=jnp.float32)
        sums[11] = sums[11] + jnp.sum(mlp_grad.astype(jnp.float32), axis=0)
        active_grad = jnp.dot(mlp_grad, down_weight.T, preferred_element_type=jnp.float32)
        hidden_grad = jax.vjp(gelu_exact, hidden)[1](active_grad)[0].astype(jnp.bfloat16)
        sums[8] = sums[8] + jnp.dot(
            normed_second.T, hidden_grad, preferred_element_type=jnp.float32
        )
        sums[9] = sums[9] + jnp.sum(hidden_grad.astype(jnp.float32), axis=0)
        second_in_grad = jnp.dot(hidden_grad, up_weight.T, preferred_element_type=jnp.float32)
        middle_part, second_gain_part, second_shift_part = jax.vjp(
            norm_rows, middle, second_gain, second_shift
        )[1](second_in_grad)
        sums[6] = sums[6] + second_gain_part
        sums[7] = sums[7] + second_shift_part
        middle_grad = middle_part + out_cot
        branch_grad = (middle_grad * keep_attn).astype(jnp.bfloat16)
        sums[4] = sums[4] + jnp.dot(attended_low.T, branch_grad, preferred_element_type=jnp.float32)
        sums[5] = sums[5] + jnp.sum(branch_grad.astype(jnp.float32), axis=0)
        attended_grad = jnp.dot(
            branch_grad, output_weight.T, preferred_element_type=jnp.float32
        ).astype(jnp.bfloat16)
        out_grad = attended_grad.reshape(rows_micro, slots, width)
        inner = jnp.transpose(
            jnp.sum(
                split_heads(
                    (attended_grad.astype(jnp.float32) * attended).reshape(rows_micro, slots, width)
                ),
                axis=-1,
            ),
            (0, 2, 1),
        )
        query_grad = jnp.zeros((rows_micro, slots, width), jnp.float32)
        visiting = (keys, values, ids_query)
        key_grad = jnp.zeros((rows_micro, slots, width), jnp.float32)
        value_grad = jnp.zeros((rows_micro, slots, width), jnp.float32)
        for step in range(blocks):
            query_part, key_part, value_part = attention_back(
                query, out_grad, ids_query, log_total, inner, visiting
            )
            query_grad = query_grad + query_part
            key_grad, value_grad = (
                from_behind((key_grad + key_part).astype(jnp.bfloat16), "blk", 1).astype(
                    jnp.float32
                ),
                from_behind((value_grad + value_part).astype(jnp.bfloat16), "blk", 1).astype(
                    jnp.float32
                ),
            )
            if step + 1 < blocks:
                visiting = from_behind((visiting[0], visiting[1], visiting[2]), "blk", 1)
        joined_grad = (
            jnp.concatenate([query_grad, key_grad, value_grad], axis=-1)
            .astype(jnp.bfloat16)
            .reshape(count, 3 * width)
        )
        sums[2] = sums[2] + jnp.dot(normed.T, joined_grad, preferred_element_type=jnp.float32)
        joined_sums = jnp.sum(joined_grad.astype(jnp.float32), axis=0)
        sums[3] = sums[3] + jnp.stack([joined_sums[:width], joined_sums[2 * width :]])
        first_in_grad = jnp.dot(joined_grad, input_weight.T, preferred_element_type=jnp.float32)
        rows_part, first_gain_part, first_shift_part = jax.vjp(
            norm_rows, rows_in, first_gain, first_shift
        )[1](first_in_grad)
        sums[0] = sums[0] + first_gain_part
        sums[1] = sums[1] + first_shift_part
        input_grads.append(
            (rows_part + middle_grad).astype(jnp.bfloat16).reshape(rows_micro, slots, width)
        )
    totals = lax.psum(
        (
            sums[0],
            sums[1],
            sums[2],
            sums[3],
            sums[4],
            sums[5],
            sums[6],
            sums[7],
            sums[8],
            sums[9],
            sums[10],
            sums[11],
        ),
        ("rows", "blk"),
    )
    return (
        jnp.concatenate(results, axis=0),
        jnp.concatenate(input_grads, axis=0),
        totals[0],
        totals[1],
        totals[2],
        totals[3],
        totals[4],
        totals[5],
        totals[6],
        totals[7],
        totals[8],
        totals[9],
        totals[10],
        totals[11],
    )


def swap(value, axis, bit):
    return lax.ppermute(value, axis, [(i, i ^ bit) for i in range(lax.axis_size(axis))])


def side(axis, bit):
    return (lax.axis_index(axis) // bit) % 2


def after(value, *others):
    return lax.optimization_barrier((value, *others))[0]


def axis_bits(axis):
    bits, bit = [], 1
    while bit < lax.axis_size(axis):
        bits.append((axis, bit))
        bit *= 2
    return bits


def add_low(a, b):
    return (a.astype(F32) + b.astype(F32)).astype(BF16)


def swap_two(value, step):
    rows, blocks = lax.axis_size("rows"), lax.axis_size("blk")
    pairs = []
    for r in range(rows):
        for b in range(blocks):
            axis, bit = step[b % 2]
            other = (r ^ bit, b) if axis == "rows" else (r, b ^ bit)
            pairs.append((r * blocks + b, other[0] * blocks + other[1]))
    return lax.ppermute(value, ("rows", "blk"), pairs)


def side_two(step):
    return jnp.where(side("blk", 1) == 0, side(*step[0]), side(*step[1]))


class Order:
    def __init__(self):
        self.last = ()

    def hold(self, value):
        return after(value, *self.last) if self.last else value

    def done(self, *values):
        self.last = values
        return values[0] if len(values) == 1 else values


class Chain:
    def __init__(self, order, steps):
        self.order, self.steps, self.at = order, steps, 0

    def start(self, make):
        core = side("blk", 1).astype(jnp.int32).reshape(1)
        self.begin(self.order.done(make(1 - core)), self.order.done(make(core)))

    def begin(self, send, keep):
        self.recv, self.keep = swap(send, "blk", 1), keep

    def next(self, count=1):
        for _ in range(count):
            self._next()

    def finish(self):
        while not hasattr(self, "result"):
            self._next()

    def _next(self):
        recv, keep, n = self.order.hold(self.recv), self.keep, len(self.steps)
        if self.at < n:
            step = self.steps[self.at]
            half = keep.shape[0] // 2
            own = side_two(step)

            def part(which):
                return add_low(
                    lax.dynamic_slice_in_dim(keep, which * half, half, 0),
                    lax.dynamic_slice_in_dim(recv, which * half, half, 0),
                )

            send, self.keep = part(1 - own), part(own)
            self.recv = swap_two(send, step)
        elif self.at <= 2 * n:
            send = add_low(keep, recv) if self.at == n else jnp.concatenate([keep, recv], axis=0)
            self.keep = send
            back = 2 * n - 1 - self.at
            self.recv = swap_two(send, self.steps[back]) if back >= 0 else swap(send, "blk", 1)
        else:
            self.result = (keep, recv)
            return
        self.at += 1
        self.order.done(send, self.keep)


def block_places(steps):
    core = side("blk", 1)
    bases = []
    for c in range(2):
        base = 0
        for step in steps:
            base = base * 2 + side(*step[c])
        bases.append(base)
    first = jnp.where(core == 0, bases[0], bases[1])
    second = jnp.where(core == 0, bases[1], bases[0])
    index = jnp.arange((1 << len(steps)) // GROUP, dtype=jnp.int32)
    parts = [index ^ (first // GROUP), index ^ (second // GROUP), jnp.stack([first % GROUP, second % GROUP])]
    return core.astype(jnp.int32).reshape(1), jnp.concatenate(parts).astype(jnp.int32)


class Small:
    def __init__(self, order, value):
        self.order, self.value = order, value
        self.steps = axis_bits("blk") + axis_bits("rows")
        self.at = 0
        self._send()

    def _send(self):
        if self.at < len(self.steps):
            self.recv = swap(self.value, *self.steps[self.at])
        self.at += 1

    def next(self):
        if self.at <= len(self.steps):
            self.value = self.order.done(self.value + self.order.hold(self.recv))
            self._send()

    def finish(self):
        while self.at <= len(self.steps):
            self.next()
        return self.value


def local_rows(
    inputs,
    image_index,
    keep_mask,
    first_gain,
    first_shift,
    input_weight,
    input_bias,
    output_weight,
    output_bias,
    second_gain,
    second_shift,
    up_weight,
    up_bias,
    down_weight,
    down_bias,
    cotangent,
):
    blocks, span, width = inputs.shape
    ff = up_weight.shape[1]
    me = lax.axis_index("blk")

    def row_piece(array, s):
        return lax.dynamic_index_in_dim(array, me ^ s, 0, keepdims=False)

    xs_send = [row_piece(inputs, s) for s in range(blocks)]
    xs_in = xs_send[:1] + [swap(xs_send[s], "blk", s) for s in range(1, blocks)]
    ids = [row_piece(image_index, 0)] + [
        swap(row_piece(after(image_index, *xs_send), s), "blk", s) for s in range(1, blocks)
    ]
    cots = [row_piece(cotangent, 0)] + [
        swap(after(row_piece(cotangent, s), *xs_in), "blk", s) for s in range(1, blocks)
    ]
    ids = jnp.concatenate(ids)
    image = jnp.where(ids < 0, 4, ids)
    order_key = image * ids.shape[0] + jnp.arange(ids.shape[0], dtype=jnp.int32)
    less = (order_key[None, :] < order_key[:, None]).astype(jnp.int32)
    rank = jnp.sum(less, axis=1)
    starts = jnp.sum((image[None, :] < jnp.arange(6, dtype=jnp.int32)[:, None]).astype(jnp.int32), axis=1)
    keep = lax.dynamic_index_in_dim(keep_mask, me, 0, keepdims=False).astype(F32) / keep_rate
    rank_row, rank_col = rank[None, :], rank[:, None]

    bias = jnp.stack([input_bias[0], jnp.zeros_like(input_bias[0]), input_bias[1]])
    xs, normed, qkv = qkv_call(rank_row, xs_in, first_gain[None], first_shift[None], input_weight, bias)
    attended, stat = forward_call(starts, qkv)
    vectors = jnp.stack([output_bias, second_gain, second_shift, down_bias])
    core = side("blk", 1).astype(jnp.int32).reshape(1)
    cot, att_low, middle, normed2, mlp_grad, sums_mid = middle_call(
        keep, rank_row, cots, attended, xs, output_weight, vectors
    )
    (up_send, up_keep, down_send, down_keep, up_sums, result, middle_grad, branch, att_grad, sums2) = mlp_call(
        core, keep, normed2, mlp_grad, middle, cot, output_weight, vectors, up_weight, up_bias[None], down_weight
    )

    y, x = axis_bits("blk")[1:], axis_bits("rows")[:1]
    z = axis_bits("rows")[1:]
    low_z, rest = z[:1], z[1:]

    def steps(first, second):
        return list(zip(first + rest, second + rest))

    xy = steps(x + y + low_z, y + x + low_z)
    zx = steps(low_z + y + x, x + low_z + y)
    yz = steps(y + low_z + x, low_z + y + x)
    order = Order()
    order.done(att_grad)

    def send_home(pieces):
        return [pieces[0]] + [swap(pieces[s], "blk", s) for s in range(1, blocks)]

    def at_home(pieces):
        stacked = jnp.stack(pieces)
        return jnp.stack([lax.dynamic_index_in_dim(stacked, me ^ r, 0, keepdims=False) for r in range(blocks)])

    down, up, first_in, last_in = Chain(order, xy), Chain(order, zx), Chain(order, yz), Chain(order, yz)
    down.begin(down_send, down_keep)
    up.begin(up_send, up_keep)
    results = send_home(order.done(*unsort_call(rank_col, order.hold(result), blocks)))
    rounds = 2 * len(xy) + 2

    def advance(*chains):
        for chain in chains:
            if chain.at < rounds - 1:
                chain.next()

    advance(down, up)
    parts = 2
    each = PAIRS // parts
    first = backward_call(starts, qkv, order.hold(att_grad), attended, stat, 0, each)
    order.done(first[0])
    advance(down, up)
    first_in.start(lambda h: input_weights_call(h, order.hold(normed), first[0], 0, parts, att_low, branch))
    advance(down, up)
    grads, bias_sums = backward_call(starts, qkv, order.hold(att_grad), attended, stat, each, each, first)
    order.done(grads)
    advance(first_in, down, up)
    last_in.start(lambda h: input_weights_call(h, order.hold(normed), grads, 1, parts))
    advance(first_in, down, up)
    inputs_grad, sums1 = order.done(*input_call(grads, input_weight, xs, order.hold(middle_grad), first_gain[None]))
    small = Small(
        order,
        jnp.concatenate([sums1[:2], bias_sums[:3], sums2[:3], sums_mid[:1], up_sums.reshape(ff // width, width)]),
    )
    advance(last_in, first_in, down, up)
    home = send_home(order.done(*unsort_call(rank_col, order.hold(inputs_grad), blocks)))
    for _ in range(3):
        advance(last_in, first_in, down, up)
        small.next()
    advance(last_in, first_in)
    small.next()
    down.finish()
    down_total = order.done(down_final(*block_places(xy), *down.result))
    advance(last_in, first_in)
    small.next()
    up.finish()
    up_total = order.done(up_final(*block_places(zx), *up.result))
    while last_in.at < rounds - 1 or first_in.at < rounds - 1:
        advance(last_in, first_in)
        small.next()
    sums = small.finish()
    first_in.finish()
    last_in.finish()
    input_total, out_total = input_final(*block_places(yz), [first_in.result, last_in.result])

    return (
        at_home(results),
        at_home(home),
        sums[0],
        sums[1],
        input_total,
        jnp.stack([sums[2], sums[4]]),
        out_total,
        sums[7],
        sums[5],
        sums[6],
        up_total,
        sums[9:].reshape(ff),
        down_total,
        sums[8],
    )


def solution(mesh):
    blocks, groups = mesh.shape["blk"], mesh.shape["rows"]

    def run(*args):
        whole_rows = args[0].shape[0] // groups == blocks and blocks & (blocks - 1) == 0 and groups & (groups - 1) == 0
        return jax.shard_map(
            local_rows if whole_rows else local,
            mesh=mesh,
            in_specs=(P("rows", "blk", None), P("rows", "blk"), P("rows", None)) + (P(),) * 12 + (P("rows", "blk", None),),
            out_specs=(P("rows", "blk", None),) * 2 + (P(),) * 12,
            check_vma=False,
        )(*args)

    return run
```

```python
import functools

import jax
import jax.numpy as jnp
from jax import lax
from jax.experimental import pallas as pl
from jax.experimental.pallas import tpu as pltpu
from jax.sharding import PartitionSpec as P

HEADS = 12
HEAD_DIM = 64
PAIR = 2 * HEAD_DIM
PAIRS = HEADS // 2
eps_norm = 1e-06
keep_rate = 0.9
F32 = jnp.float32
BF16 = jnp.bfloat16
NEG = -1e30
VMEM = 62 * 1024 * 1024
QUICK = pl.CostEstimate(flops=1 << 20, bytes_accessed=1 << 16, transcendentals=0)


def dot(a, b):
    return jnp.dot(a, b, preferred_element_type=F32)


def dot_nt(a, b):
    return lax.dot_general(a, b, (((1,), (1,)), ((), ())), preferred_element_type=F32)


def dot_tn(a, b):
    return lax.dot_general(a, b, (((0,), (0,)), ((), ())), preferred_element_type=F32)


def whole(shape):
    return pl.BlockSpec(shape, lambda *g: (0,) * len(shape), pipeline_mode=pl.Buffered(1))


def centre_scale(values):
    centre = values - jnp.mean(values, axis=-1, keepdims=True)
    spread = jnp.mean(centre * centre, axis=-1, keepdims=True)
    inv = lax.rsqrt(spread + eps_norm)
    return centre * inv, inv


def norm_back(grad_hat, hat, inv):
    first = jnp.mean(grad_hat, axis=-1, keepdims=True)
    second = jnp.mean(grad_hat * hat, axis=-1, keepdims=True)
    return (grad_hat - first - hat * second) * inv


def sort_tile(rank_row, tile, step, pieces):
    span = pieces[0].shape[0]
    place = step * tile + lax.broadcasted_iota(jnp.int32, (tile, span), 0)
    total = None
    for i, piece in enumerate(pieces):
        pick = (rank_row[:, i * span : (i + 1) * span] == place).astype(BF16)
        part = dot(pick, piece[...])
        total = part if total is None else total + part
    return total


def qkv_kernel(n, tile, *refs):
    rank, *pieces = refs[: n + 1]
    gain, shift, weight, bias, xs_out, normed_out, qkv_out = refs[n + 1 :]
    xs = sort_tile(rank[...], tile, pl.program_id(0), pieces)
    xs_out[...] = xs.astype(BF16)
    hat, _ = centre_scale(xs)
    normed = (hat * gain[...] + shift[...]).astype(BF16)
    normed_out[...] = normed
    width = normed.shape[1]
    for j in range(3):
        cols = slice(j * width, (j + 1) * width)
        mixed = (dot(normed, weight[:, cols]) + bias[j : j + 1, :]).astype(BF16)
        qkv_out[j] = mixed * BF16(HEAD_DIM**-0.5) if j == 0 else mixed


def qkv_call(rank, pieces, gain, shift, weight, bias, tile=288):
    n = len(pieces)
    span, width = pieces[0].shape
    count = n * span
    return pl.pallas_call(
        functools.partial(qkv_kernel, n, tile),
        grid=(count // tile,),
        in_specs=[whole((1, count))]
        + [whole((span, width))] * n
        + [whole((1, width)), whole((1, width)), whole(weight.shape), whole(bias.shape)],
        out_specs=[
            pl.BlockSpec((tile, width), lambda i: (i, 0)),
            pl.BlockSpec((tile, width), lambda i: (i, 0)),
            pl.BlockSpec((3, tile, width), lambda i: (0, i, 0)),
        ],
        out_shape=[
            jax.ShapeDtypeStruct((count, width), BF16),
            jax.ShapeDtypeStruct((count, width), BF16),
            jax.ShapeDtypeStruct((3, count, width), BF16),
        ],
        compiler_params=pltpu.CompilerParams(vmem_limit_bytes=VMEM),
        cost_estimate=QUICK,
        name="sort_qkv",
    )(rank, *pieces, gain, shift, weight, bias)


SMALL = 304
LARGE = 384


def windows(starts, seg, length):
    first, last = starts[seg], starts[seg + 1]
    aligned = first // 16 * 16
    small = SMALL if seg < 4 else LARGE
    at_small = pl.multiple_of(jnp.minimum(aligned, length - small), 16)
    at_large = pl.multiple_of(jnp.minimum(aligned, length - LARGE), 16)
    return first, last, small, at_small, at_large


def inside(at, size, lanes, first, last):
    place = at + lax.broadcasted_iota(jnp.int32, (size, lanes), 0)
    return (place >= first) & (place < last)


def forward_kernel(starts, qkv, out, stat):
    length = qkv.shape[1]
    for seg in range(5):
        first, last, small, at_q, at_k = windows(starts, seg, length)
        rows_q = pl.ds(at_q, small)
        q = qkv[0, rows_q, :]
        k = qkv[1, pl.ds(at_k, LARGE), :]
        v = qkv[2, pl.ds(at_k, LARGE), :]
        lane = lax.broadcasted_iota(jnp.int32, (LARGE, PAIR), 1)
        lane_q = lax.broadcasted_iota(jnp.int32, (small, PAIR), 1)
        low = lane < HEAD_DIM
        seen = inside(at_k, LARGE, PAIR, first, last)
        zero = jnp.zeros((LARGE, PAIR), BF16)
        one = jnp.ones((LARGE, PAIR), BF16)
        bias = jnp.where((lane == 0) & ~seen, NEG, 0.0).astype(BF16)
        q_ext = jnp.concatenate([q, (lane_q == 0).astype(BF16)], axis=1)
        tops, weights, mixes = [], [], []
        for half in (low, ~low):
            k_ext = jnp.concatenate([jnp.where(half, k, zero), bias], axis=1)
            scores = dot_nt(q_ext, k_ext)
            top = jnp.max(scores, axis=-1, keepdims=True)
            tops.append(top)
            weights.append(jnp.exp(scores - top).astype(BF16))
            mixes.append(jnp.concatenate([jnp.where(half, v, zero), jnp.where(half, one, zero)], axis=1))
        both = dot(jnp.concatenate(weights, axis=1), jnp.concatenate(mixes, axis=0))
        total = both[:, PAIR:]
        peak = jnp.where(lane_q < HEAD_DIM, tops[0], tops[1])
        mine = inside(at_q, small, PAIR, first, last)
        out[rows_q, :] = jnp.where(mine, both[:, :PAIR] / total, out[rows_q, :])
        stat[rows_q, :] = jnp.where(mine, peak + jnp.log(total), stat[rows_q, :])


def forward_call(starts, qkv):
    _, count, wide = qkv.shape
    pairs = wide // PAIR
    return pl.pallas_call(
        forward_kernel,
        grid_spec=pltpu.PrefetchScalarGridSpec(
            num_scalar_prefetch=1,
            grid=(pairs,),
            in_specs=[pl.BlockSpec((3, count, PAIR), lambda p, s: (0, 0, p))],
            out_specs=[
                pl.BlockSpec((count, PAIR), lambda p, s: (0, p)),
                pl.BlockSpec((count, PAIR), lambda p, s: (0, p)),
            ],
        ),
        out_shape=[jax.ShapeDtypeStruct((count, pairs * PAIR), F32)] * 2,
        compiler_params=pltpu.CompilerParams(vmem_limit_bytes=VMEM),
        cost_estimate=QUICK,
        name="attention_forward",
    )(starts, qkv)


def split3(value):
    high = value.astype(BF16)
    rest = value - high.astype(F32)
    mid = rest.astype(BF16)
    return high, mid, (rest - mid.astype(F32)).astype(BF16)


def backward_kernel(starts, qkv, grad, att, stat, *refs):
    out, sums = refs[-2:]
    length = qkv.shape[1]
    third = lax.broadcasted_iota(jnp.int32, (PAIR, PAIR), 0) // HEAD_DIM
    block = (third == lax.broadcasted_iota(jnp.int32, (PAIR, PAIR), 1) // HEAD_DIM).astype(BF16)
    for seg in range(5):
        first, last, small, at_k, at_q = windows(starts, seg, length)
        rows_q, rows_k = pl.ds(at_q, LARGE), pl.ds(at_k, small)
        lane_q = lax.broadcasted_iota(jnp.int32, (LARGE, PAIR), 1)
        lane_k = lax.broadcasted_iota(jnp.int32, (small, PAIR), 1)
        spot_q, spot_k = lane_q % HEAD_DIM, lane_k % HEAD_DIM
        mine_q = inside(at_q, LARGE, PAIR, first, last)
        mine_k = inside(at_k, small, PAIR, first, last)
        zero_q = jnp.zeros((LARGE, PAIR), BF16)
        zero_k = jnp.zeros((small, PAIR), BF16)
        q = qkv[0, rows_q, :]
        k = jnp.where(mine_k, qkv[1, rows_k, :], zero_k)
        v = qkv[2, rows_k, :]
        g = jnp.where(mine_q, grad[rows_q, :], zero_q)
        prod = g.astype(F32) * jnp.where(mine_q, att[rows_q, :], 0.0)
        p_high = prod.astype(BF16)
        p_low = (prod - p_high.astype(F32)).astype(BF16)
        inner = dot(p_high, block) + dot(p_low, block)
        logs = jnp.where(mine_q, stat[rows_q, :], 0.0)

        def spread(value, fifth):
            a, b, c = split3(value)
            return jnp.where(
                spot_q == 0, a, jnp.where(spot_q == 1, b, jnp.where(spot_q == 2, c, fifth))
            )

        query_bias = jnp.where(mine_q, 0.0, NEG).astype(BF16)
        unit = jnp.ones((LARGE, PAIR), BF16)
        q_ext = jnp.concatenate(
            [q, spread(logs, jnp.where(spot_q == 3, unit, jnp.where(spot_q == 4, query_bias, zero_q)))], axis=1
        )
        g_ext = jnp.concatenate([g, spread(inner, zero_q)], axis=1)
        key_bias = jnp.where(mine_k, 0.0, NEG).astype(BF16)
        minus = jnp.where(spot_k < 3, -1.0, 0.0).astype(BF16)
        k_tail = jnp.where(
            spot_k == 3, key_bias, jnp.where(spot_k == 4, jnp.ones((small, PAIR), BF16), minus)
        )
        probs, score_grads, ks, gs, qs = [], [], [], [], []
        for h in range(2):
            half_k = lane_k // HEAD_DIM == h
            half_q = lane_q // HEAD_DIM == h
            k_half = jnp.where(half_k, k, zero_k)
            shifted = dot_nt(jnp.concatenate([k_half, jnp.where(half_k, k_tail, zero_k)], axis=1), q_ext)
            prob = jnp.exp(shifted)
            v_half = jnp.where(half_k, v, zero_k)
            prob_grad = dot_nt(jnp.concatenate([v_half, jnp.where(half_k, minus, zero_k)], axis=1), g_ext)
            probs.append(prob.astype(BF16))
            score_grads.append((prob * prob_grad).astype(BF16))
            ks.append(k_half)
            gs.append(jnp.where(half_q, g, zero_q))
            qs.append(jnp.where(half_q, q, zero_q))
        value_grad = dot(jnp.concatenate(probs, axis=1), jnp.concatenate(gs, axis=0))
        key_grad = dot(jnp.concatenate(score_grads, axis=1), jnp.concatenate(qs, axis=0))
        query_grad = dot_tn(jnp.concatenate(score_grads, axis=0), jnp.concatenate(ks, axis=0))
        query_grad = (query_grad * HEAD_DIM**-0.5).astype(BF16)
        out[0, rows_q, :] = jnp.where(mine_q, query_grad, out[0, rows_q, :])
        out[1, rows_k, :] = jnp.where(mine_k, key_grad.astype(BF16), out[1, rows_k, :])
        out[2, rows_k, :] = jnp.where(mine_k, value_grad.astype(BF16), out[2, rows_k, :])
    for j in range(3):
        sums[j : j + 1, :] = jnp.sum(out[j].astype(F32), axis=0, keepdims=True)


def backward_call(starts, qkv, grad, att, stat, first_pair, pairs, before=None):
    _, count, width = qkv.shape
    held = [] if before is None else list(before)
    return pl.pallas_call(
        backward_kernel,
        grid_spec=pltpu.PrefetchScalarGridSpec(
            num_scalar_prefetch=1,
            grid=(pairs,),
            in_specs=[pl.BlockSpec((3, count, PAIR), lambda p, s: (0, 0, p + first_pair))]
            + [pl.BlockSpec((count, PAIR), lambda p, s: (0, p + first_pair))] * 3
            + [pl.BlockSpec(memory_space=pl.ANY)] * len(held),
            out_specs=[
                pl.BlockSpec((3, count, PAIR), lambda p, s: (0, 0, p + first_pair)),
                pl.BlockSpec((8, PAIR), lambda p, s: (0, p + first_pair)),
            ],
        ),
        out_shape=[
            jax.ShapeDtypeStruct((3, count, width), BF16),
            jax.ShapeDtypeStruct((8, width), F32),
        ],
        input_output_aliases={5: 0, 6: 1} if held else {},
        compiler_params=pltpu.CompilerParams(vmem_limit_bytes=VMEM),
        cost_estimate=QUICK,
        name="attention_backward",
    )(starts, qkv, grad, att, stat, *held)


ERF = (0.254829592, -0.284496736, 1.421413741, -1.453152027, 1.061405429)


def gelu_pair(u):
    size = jnp.abs(u)
    t = 1.0 / (1.0 + (0.3275911 * 0.5**0.5) * size)
    bell = jnp.exp(u * u * -0.5)
    poly = ERF[4] * t + ERF[3]
    for c in (ERF[2], ERF[1], ERF[0]):
        poly = poly * t + c
    tail = 0.5 * poly * t * bell
    phi = jnp.where(u < 0, tail, 1.0 - tail)
    return u * phi, phi + u * bell * 0.3989422804014327


def middle_kernel(n, tile, *refs):
    keep, rank, *pieces = refs[: n + 2]
    att, xs, out_w, vectors, cot_out, att_low_out, middle_out, normed_out, mlp_out, sums = refs[n + 2 :]
    step = pl.program_id(0)
    cot = sort_tile(rank[...], tile, step, pieces)
    cot_out[...] = cot.astype(BF16)
    mlp_grad = (cot * keep[1]).astype(BF16)
    mlp_out[...] = mlp_grad
    att_low = att[...].astype(BF16)
    att_low_out[...] = att_low
    middle = xs[...].astype(F32) + keep[0] * (dot(att_low, out_w[...]) + vectors[0:1, :])
    middle_out[...] = middle
    hat, _ = centre_scale(middle)
    normed_out[...] = (hat * vectors[1:2, :] + vectors[2:3, :]).astype(BF16)

    @pl.when(step == 0)
    def _():
        sums[...] = jnp.zeros_like(sums)

    sums[0:1, :] += jnp.sum(mlp_grad.astype(F32), axis=0, keepdims=True)


def middle_call(keep, rank, pieces, att, xs, out_w, vectors, tile=384):
    n = len(pieces)
    span, width = pieces[0].shape
    count = n * span
    rows = pl.BlockSpec((tile, width), lambda i: (i, 0))
    low, full = jax.ShapeDtypeStruct((count, width), BF16), jax.ShapeDtypeStruct((count, width), F32)
    return pl.pallas_call(
        functools.partial(middle_kernel, n, tile),
        grid=(count // tile,),
        in_specs=[pl.BlockSpec(memory_space=pltpu.SMEM), whole((1, count))]
        + [whole((span, width))] * n
        + [rows, rows, whole(out_w.shape), whole(vectors.shape)],
        out_specs=[rows] * 5 + [pl.BlockSpec((8, width), lambda i: (0, 0))],
        out_shape=[low, low, full, low, low, jax.ShapeDtypeStruct((8, width), F32)],
        compiler_params=pltpu.CompilerParams(vmem_limit_bytes=VMEM),
        cost_estimate=QUICK,
        name="middle",
    )(keep, rank, *pieces, att, xs, out_w, vectors)


def mlp_kernel(parts, core, keep, normed, mlp_grad, middle, cot, att, out_w, vectors, up_w, up_b, down_w, *refs):
    (
        up_send, up_keep, down_send, down_keep, up_sums, result, middle_grad_out, branch_out, att_grad_out, sums,
        lift, back, act_all, hidden_all,
    ) = refs
    step, half = pl.program_id(0), pl.num_programs(0) // 2
    count, width = normed.shape
    cuts = [slice(i * (count // parts), (i + 1) * (count // parts)) for i in range(parts)]

    @pl.when(step == 0)
    def _():
        lift[...] = jnp.zeros_like(lift)
        back[...] = jnp.zeros_like(back)

    @pl.when(step < 2 * half)
    def _():
        total = jnp.zeros(up_sums.shape, F32)
        ready = None
        for rows in cuts + [None]:
            fresh = None
            if rows is not None:
                u = dot(normed[rows, :], up_w[...]) + up_b[...]
                fresh = (rows, u, dot_nt(mlp_grad[rows, :], down_w[...]))
            if ready is not None:
                past, u, act_grad = ready
                act, slope = gelu_pair(u)
                act_all[past, :] = act.astype(BF16)
                hidden = (act_grad * slope).astype(BF16)
                hidden_all[past, :] = hidden
                total = total + jnp.sum(hidden.astype(F32), axis=0, keepdims=True)
            ready = fresh
        lift[...] += dot(act_all[...], down_w[...])
        back[...] += dot_nt(hidden_all[...], up_w[...])
        up_sums[...] = total
        up_part = dot_tn(normed[...], hidden_all[...]).astype(BF16)
        down_part = dot_tn(act_all[...], mlp_grad[...]).astype(BF16)

        @pl.when(step < half)
        def _():
            up_send[...] = up_part
            down_send[...] = down_part

        @pl.when(step >= half)
        def _():
            up_keep[...] = up_part
            down_keep[...] = down_part

    @pl.when(step == 2 * half)
    def _():
        gain, down_b = vectors[1:2, :], vectors[3:4, :]
        sums[...] = jnp.zeros_like(sums)
        for rows in cuts:
            mid, grad = middle[rows, :], back[rows, :]
            hat, inv = centre_scale(mid)
            result[rows, :] = (mid + keep[1] * (lift[rows, :] + down_b)).astype(BF16)
            middle_grad = cot[rows, :].astype(F32) + norm_back(grad * gain, hat, inv)
            middle_grad_out[rows, :] = middle_grad
            branch = (keep[0] * middle_grad).astype(BF16)
            branch_out[rows, :] = branch
            att_grad_out[rows, :] = dot_nt(branch, out_w[...]).astype(BF16)
            sums[0:1, :] += jnp.sum(grad * hat, axis=0, keepdims=True)
            sums[1:2, :] += jnp.sum(grad, axis=0, keepdims=True)
            sums[2:3, :] += jnp.sum(branch.astype(F32), axis=0, keepdims=True)
        for out, c in ((down_send, 1 - core[0]), (down_keep, core[0])):
            cols = pl.ds(pl.multiple_of(c * (width // 2), 128), width // 2)
            out[: width // 2, :] = dot_tn(att[:, cols], branch_out[...]).astype(BF16)
            out[width // 2 :, :] = jnp.zeros((out.shape[0] - width // 2, width), BF16)


def mlp_call(core, keep, normed, mlp_grad, middle, cot, att, out_w, vectors, up_w, up_b, down_w, chunk=512, parts=4):
    count, width = normed.shape
    ff = up_w.shape[1]
    half = ff // 2 // chunk

    def place(i, c):
        i = jnp.minimum(i, 2 * half - 1)
        return jnp.where(i < half, (1 - c[0]) * half + i, c[0] * half + i - half)

    def first(i):
        return jnp.minimum(i, half - 1)

    def second(i):
        return jnp.clip(i - half, 0, half - 1)

    def extra(i, index):
        return jnp.where(i == 2 * half, half, index)

    low, full = jax.ShapeDtypeStruct((count, width), BF16), jax.ShapeDtypeStruct((count, width), F32)
    return pl.pallas_call(
        functools.partial(mlp_kernel, parts),
        grid_spec=pltpu.PrefetchScalarGridSpec(
            num_scalar_prefetch=1,
            grid=(2 * half + 1,),
            in_specs=[pl.BlockSpec(memory_space=pltpu.SMEM)]
            + [whole((count, width))] * 5
            + [
                whole(out_w.shape),
                whole(vectors.shape),
                pl.BlockSpec((width, chunk), lambda i, c: (0, place(i, c))),
                pl.BlockSpec((1, chunk), lambda i, c: (0, place(i, c))),
                pl.BlockSpec((chunk, width), lambda i, c: (place(i, c), 0)),
            ],
            out_specs=[
                pl.BlockSpec((width, chunk), lambda i, c: (0, first(i))),
                pl.BlockSpec((width, chunk), lambda i, c: (0, second(i))),
                pl.BlockSpec((chunk, width), lambda i, c: (extra(i, first(i)), 0)),
                pl.BlockSpec((chunk, width), lambda i, c: (extra(i, second(i)), 0)),
                pl.BlockSpec((1, chunk), lambda i, c: (0, place(i, c))),
            ]
            + [whole((count, width))] * 4
            + [whole((8, width))],
            scratch_shapes=[pltpu.VMEM((count, width), F32)] * 2 + [pltpu.VMEM((count, chunk), BF16)] * 2,
        ),
        out_shape=[jax.ShapeDtypeStruct((width, ff // 2), BF16)] * 2
        + [jax.ShapeDtypeStruct((ff // 2 + chunk, width), BF16)] * 2
        + [jax.ShapeDtypeStruct((1, ff), F32), low, full, low, low, jax.ShapeDtypeStruct((8, width), F32)],
        compiler_params=pltpu.CompilerParams(vmem_limit_bytes=VMEM),
        cost_estimate=QUICK,
        name="mlp",
    )(core, keep, normed, mlp_grad, middle, cot, att, out_w, vectors, up_w, up_b, down_w)


def input_kernel(grads, weight, xs, middle_grad, gain, out, sums):
    span = xs.shape[1]
    back = None
    for j in range(3):
        part = dot_nt(grads[j], weight[:, j * span : (j + 1) * span])
        back = part if back is None else back + part
    hat, inv = centre_scale(xs[...].astype(F32))
    out[...] = (middle_grad[...] + norm_back(back * gain[...], hat, inv)).astype(BF16)

    @pl.when(pl.program_id(0) == 0)
    def _():
        sums[...] = jnp.zeros_like(sums)

    sums[0:1, :] += jnp.sum(back * hat, axis=0, keepdims=True)
    sums[1:2, :] += jnp.sum(back, axis=0, keepdims=True)


def input_call(grads, weight, xs, middle_grad, gain, tile=288):
    count, width = xs.shape
    return pl.pallas_call(
        input_kernel,
        grid=(count // tile,),
        in_specs=[pl.BlockSpec((3, tile, width), lambda i: (0, i, 0))]
        + [
            whole(weight.shape),
            pl.BlockSpec((tile, width), lambda i: (i, 0)),
            pl.BlockSpec((tile, width), lambda i: (i, 0)),
            whole((1, width)),
        ],
        out_specs=[pl.BlockSpec((tile, width), lambda i: (i, 0)), pl.BlockSpec((8, width), lambda i: (0, 0))],
        out_shape=[jax.ShapeDtypeStruct((count, width), BF16), jax.ShapeDtypeStruct((8, width), F32)],
        compiler_params=pltpu.CompilerParams(vmem_limit_bytes=VMEM),
        cost_estimate=QUICK,
        name="input_backward",
    )(grads, weight, xs, middle_grad, gain)


def unsort_kernel(me, rank, source, out):
    count, span = source.shape[0], rank.shape[0]
    place = lax.broadcasted_iota(jnp.int32, (span, count), 1)
    out[0] = dot((rank[...] == place).astype(BF16), source[...]).astype(BF16)


def unsort_call(me, rank_col, n, array):
    count, width = array.shape
    span = count // n
    return pl.pallas_call(
        unsort_kernel,
        grid_spec=pltpu.PrefetchScalarGridSpec(
            num_scalar_prefetch=1,
            grid=(n,),
            in_specs=[pl.BlockSpec((span, 1), lambda i, m: (i, 0)), whole((count, width))],
            out_specs=pl.BlockSpec((1, span, width), lambda i, m: (m[0] ^ i, 0, 0)),
        ),
        out_shape=jax.ShapeDtypeStruct((n, span, width), BF16),
        compiler_params=pltpu.CompilerParams(vmem_limit_bytes=VMEM),
        cost_estimate=QUICK,
        name="unsort",
    )(me, rank_col, array)


VECTORS = 128


def input_weights_kernel(core, normed, grads, first, second, third, up_sums, send, keep):
    mid, width = normed.shape[1], grads.shape[2]
    h = core[0] ^ 1 ^ pl.program_id(0)

    def write(out):
        for j in range(3):
            out[:, j * width : (j + 1) * width] = dot_tn(normed[...], grads[j]).astype(BF16)
        rows = [first[0:3, :], second[0:3, :], third[0:1, :]]
        for i in range(up_sums.shape[1] // width):
            rows.append(up_sums[:, pl.ds(pl.multiple_of(i * width + h * mid, 128), mid)])
        count = sum(row.shape[0] for row in rows)
        rows.append(jnp.zeros((VECTORS - count, mid), F32))
        out[:, 3 * width :] = jnp.concatenate(rows, axis=0).T.astype(BF16)

    pl.when(pl.program_id(0) == 0)(lambda: write(send))
    pl.when(pl.program_id(0) == 1)(lambda: write(keep))


def input_weights_call(core, normed, grads, first, second, third, up_sums):
    count, width = normed.shape
    half = jax.ShapeDtypeStruct((width // 2, 3 * width + VECTORS), BF16)
    rows = pl.BlockSpec((count, width // 2), lambda i, c: (0, c[0] ^ 1 ^ i))
    vector = pl.BlockSpec((8, width // 2), lambda i, c: (0, c[0] ^ 1 ^ i))
    return pl.pallas_call(
        input_weights_kernel,
        grid_spec=pltpu.PrefetchScalarGridSpec(
            num_scalar_prefetch=1,
            grid=(2,),
            in_specs=[rows, whole(grads.shape), vector, vector, vector, whole(up_sums.shape)],
            out_specs=[whole(half.shape)] * 2,
        ),
        out_shape=[half] * 2,
        compiler_params=pltpu.CompilerParams(vmem_limit_bytes=VMEM),
        cost_estimate=QUICK,
        name="input_weights",
    )(core, normed, grads, first, second, third, up_sums)


GROUPS = 4


def final_call(core, turns, blocks, pieces, name, spread, outs):
    size = blocks // GROUPS
    rows = pieces[0].shape[0] // (blocks // 2)
    whole_tile = 1 if rows % 16 == 0 else 2

    def kernel(c, t, *refs):
        h, g = pl.program_id(0), pl.program_id(1)
        active = (h * GROUPS + g) // (GROUPS // 2)
        turn = t[h]
        place = g ^ (turn // size)

        def write(source):
            for j in range(0, size, whole_tile):
                part = source[j * rows : (j + whole_tile) * rows, :].astype(F32)
                for i in range(whole_tile):
                    spread(part[i * rows : (i + 1) * rows], (j + i) ^ (turn % size), place, refs[4:])

        for q in range(4):
            pl.when(active == q)(functools.partial(write, refs[q]))

    def in_spec(q):
        def index(h, g, c, t):
            return jnp.clip(h * GROUPS + g - q * (GROUPS // 2), 0, GROUPS // 2 - 1), 0

        return pl.BlockSpec((size * rows, pieces[q].shape[1]), index)

    def out_spec(block, index):
        return pl.BlockSpec(block, lambda h, g, c, t: index(h ^ c[0], g, lambda n: n ^ (t[h] // size)))

    return pl.pallas_call(
        kernel,
        grid_spec=pltpu.PrefetchScalarGridSpec(
            num_scalar_prefetch=2,
            grid=(2, GROUPS),
            in_specs=[in_spec(q) for q in range(4)],
            out_specs=[out_spec(block, index) for _, block, index in outs],
        ),
        out_shape=[jax.ShapeDtypeStruct(shape, F32) for shape, _, _ in outs],
        compiler_params=pltpu.CompilerParams(vmem_limit_bytes=VMEM),
        cost_estimate=QUICK,
        name=name,
    )(core, turns, *pieces)


def rows_at(ref, place, value):
    rows = value.shape[0]
    ref[pl.ds(pl.multiple_of(place * rows, 8), rows), :] = value


def down_final(core, turns, blocks, pieces, ff):
    rows, width = pieces[0].shape[0] // (blocks // 2), pieces[0].shape[1]
    size = blocks // GROUPS * rows

    def spread(block, j, place, refs):
        @pl.when(place < GROUPS - 1)
        def _():
            rows_at(refs[0], j, block)

        @pl.when((place == GROUPS - 1) & (j * rows < width // 2))
        def _():
            rows_at(refs[1], j, block)

    def down_index(h, g, place):
        at = place(g)
        near = place(jnp.where(g == 0, 1, g - 1))
        return h * (GROUPS - 1) + jnp.where(at == GROUPS - 1, near, at), 0

    outs = [
        ((ff, width), (size, width), down_index),
        ((width, width), (width // 2, width), lambda h, g, place: (h, 0)),
    ]
    return final_call(core, turns, blocks, pieces, "down_final", spread, outs)


def up_final(core, turns, blocks, pieces):
    rows, cols = pieces[0].shape[0] * 2, pieces[0].shape[1]

    def spread(block, j, place, refs):
        rows_at(refs[0], j, block)

    outs = [((rows, 2 * cols), (rows // GROUPS, cols), lambda h, g, place: (place(g), h))]
    return final_call(core, turns, blocks, pieces, "up_final", spread, outs)[0]


def input_final(core, turns, blocks, pieces):
    width, cols = pieces[0].shape[0] * 4, pieces[0].shape[1]

    def spread(block, j, place, refs):
        rows_at(refs[0], j, block[:, : 3 * width])
        rows_at(refs[1], j, block[:, 3 * width :])

    outs = [
        ((width, n), (width // 2 // GROUPS, n), lambda h, g, place: (h * GROUPS + place(g), 0))
        for n in (3 * width, cols - 3 * width)
    ]
    return final_call(core, turns, blocks, pieces, "input_final", spread, outs)


def copy_kernel(source, out):
    out[...] = source[...]


def copy_call(array):
    spec = pl.BlockSpec((1, *array.shape[1:]), lambda i: (i, 0, 0))
    return pl.pallas_call(
        copy_kernel,
        grid=(array.shape[0],),
        in_specs=[spec],
        out_specs=spec,
        out_shape=jax.ShapeDtypeStruct(array.shape, array.dtype),
        compiler_params=pltpu.CompilerParams(vmem_limit_bytes=VMEM),
        cost_estimate=QUICK,
        name="copy",
    )(array)


MICRO = 2


def from_behind(value, axis, steps):
    count = lax.axis_size(axis)
    pairs = [(source, (source + steps) % count) for source in range(count)]
    return lax.ppermute(value, axis, pairs)


def norm_rows(values, gain, shift):
    centre = values - jnp.mean(values, axis=-1, keepdims=True)
    spread = jnp.mean(centre * centre, axis=-1, keepdims=True)
    return centre * lax.rsqrt(spread + eps_norm) * gain + shift


def gelu_exact(values):
    return jax.nn.gelu(values, approximate=False)


def split_heads(block):
    return block.reshape(block.shape[0], block.shape[1], HEADS, HEAD_DIM)


def take_rows(array, first_row, count_rows):
    return lax.slice_in_dim(array, first_row, first_row + count_rows, axis=0)


def masked_scores(query, keys, ids_query, ids_keys):
    scores = jnp.einsum(
        "rqhd,rkhd->rhqk", split_heads(query), split_heads(keys), preferred_element_type=jnp.float32
    ) * HEAD_DIM ** (-0.5)
    same = ids_query[:, None, :, None] == ids_keys[:, None, None, :]
    return jnp.where(same, scores, -jnp.inf)


def attend_piece(carry, query, ids_query, piece):
    keys, values, ids_keys = piece
    peak, total, accum = carry
    scores = masked_scores(query, keys, ids_query, ids_keys)
    top = jnp.maximum(peak, jnp.max(scores, axis=-1))
    weights = jnp.exp(scores - top[..., None])
    total = jnp.sum(weights, axis=-1)
    update = jnp.einsum(
        "rhqk,rkhd->rqhd",
        weights.astype(jnp.bfloat16),
        split_heads(values),
        preferred_element_type=jnp.float32,
    )
    return (top, total, update.reshape(accum.shape))


def attention_forward(query, keys, values, ids_query):
    rows_here, slots, width = query.shape
    start_state = (
        jnp.full((rows_here, HEADS, slots), -1e30, jnp.float32),
        jnp.zeros((rows_here, HEADS, slots), jnp.float32),
        jnp.zeros((rows_here, slots, width), jnp.float32),
    )
    carry = attend_piece(
        start_state,
        query,
        ids_query,
        (
            lax.all_gather(keys, "blk", axis=1, tiled=True),
            lax.all_gather(values, "blk", axis=1, tiled=True),
            lax.all_gather(ids_query, "blk", axis=1, tiled=True),
        ),
    )
    return (carry[0], carry[1], carry[2], None)


def attention_back(query, out_grad, ids_query, log_total, inner, piece):
    keys, values, ids_keys = piece
    scale = HEAD_DIM ** (-0.5)
    scores = masked_scores(query, keys, ids_query, ids_keys)
    probs = jnp.exp(scores - log_total[..., None])
    prob_grad = jnp.einsum(
        "rqhd,rkhd->rhqk",
        split_heads(out_grad),
        split_heads(values),
        preferred_element_type=jnp.float32,
    )
    score_grad = (probs * (prob_grad - inner[..., None])).astype(jnp.bfloat16)
    value_grad = jnp.einsum(
        "rhqk,rqhd->rkhd",
        probs.astype(jnp.bfloat16),
        split_heads(out_grad),
        preferred_element_type=jnp.float32,
    )
    key_grad = (
        jnp.einsum(
            "rhqk,rqhd->rkhd", score_grad, split_heads(query), preferred_element_type=jnp.float32
        )
        * scale
    )
    query_grad = (
        jnp.einsum(
            "rhqk,rkhd->rqhd", score_grad, split_heads(keys), preferred_element_type=jnp.float32
        )
        * scale
    )
    return (
        query_grad.reshape(query.shape),
        key_grad.reshape(keys.shape),
        value_grad.reshape(values.shape),
    )


def local(
    inputs,
    image_index,
    keep_mask,
    first_gain,
    first_shift,
    input_weight,
    input_bias,
    output_weight,
    output_bias,
    second_gain,
    second_shift,
    up_weight,
    up_bias,
    down_weight,
    down_bias,
    cotangent,
):
    rows_local, slots, width = inputs.shape
    rows_micro = rows_local // MICRO
    count = rows_micro * slots
    blocks = lax.axis_size("blk")
    params = (
        first_gain,
        first_shift,
        input_weight,
        input_bias,
        output_weight,
        output_bias,
        second_gain,
        second_shift,
        up_weight,
        up_bias,
        down_weight,
        down_bias,
    )
    sums = [jnp.zeros(item.shape, jnp.float32) for item in params]
    results = []
    input_grads = []
    for micro in range(MICRO):
        first_row = micro * rows_micro
        rows_in = take_rows(inputs, first_row, rows_micro).astype(jnp.float32).reshape(count, width)
        out_cot = (
            take_rows(cotangent, first_row, rows_micro).astype(jnp.float32).reshape(count, width)
        )
        ids_query = take_rows(image_index, first_row, rows_micro).astype(jnp.bfloat16)
        keep = take_rows(keep_mask, first_row, rows_micro).astype(jnp.float32) / keep_rate
        keep_attn = jnp.broadcast_to(keep[:, None, 0:1], (rows_micro, slots, 1)).reshape(count, 1)
        keep_mlp = jnp.broadcast_to(keep[:, None, 1:2], (rows_micro, slots, 1)).reshape(count, 1)
        normed = norm_rows(rows_in, first_gain, first_shift).astype(jnp.bfloat16)
        mixed = jnp.dot(normed, input_weight, preferred_element_type=jnp.float32)
        query = (
            (mixed[:, :width] + input_bias[0])
            .astype(jnp.bfloat16)
            .reshape(rows_micro, slots, width)
        )
        keys = mixed[:, width : 2 * width].astype(jnp.bfloat16).reshape(rows_micro, slots, width)
        values = (
            (mixed[:, 2 * width :] + input_bias[1])
            .astype(jnp.bfloat16)
            .reshape(rows_micro, slots, width)
        )
        top, total, accum, whole = attention_forward(query, keys, values, ids_query)
        attended = (split_heads(accum) / jnp.transpose(total, (0, 2, 1))[..., None]).reshape(
            count, width
        )
        log_total = top + jnp.log(total)
        attended_low = attended.astype(jnp.bfloat16)
        branch = (
            jnp.dot(attended_low, output_weight, preferred_element_type=jnp.float32) + output_bias
        )
        middle = rows_in + keep_attn * branch
        normed_second = norm_rows(middle, second_gain, second_shift).astype(jnp.bfloat16)
        hidden = jnp.dot(normed_second, up_weight, preferred_element_type=jnp.float32) + up_bias
        active = gelu_exact(hidden).astype(jnp.bfloat16)
        branch_second = jnp.dot(active, down_weight, preferred_element_type=jnp.float32) + down_bias
        results.append(
            (middle + keep_mlp * branch_second)
            .astype(jnp.bfloat16)
            .reshape(rows_micro, slots, width)
        )
        mlp_grad = (out_cot * keep_mlp).astype(jnp.bfloat16)
        sums[10] = sums[10] + jnp.dot(active.T, mlp_grad, preferred_element_type=jnp.float32)
        sums[11] = sums[11] + jnp.sum(mlp_grad.astype(jnp.float32), axis=0)
        active_grad = jnp.dot(mlp_grad, down_weight.T, preferred_element_type=jnp.float32)
        hidden_grad = jax.vjp(gelu_exact, hidden)[1](active_grad)[0].astype(jnp.bfloat16)
        sums[8] = sums[8] + jnp.dot(
            normed_second.T, hidden_grad, preferred_element_type=jnp.float32
        )
        sums[9] = sums[9] + jnp.sum(hidden_grad.astype(jnp.float32), axis=0)
        second_in_grad = jnp.dot(hidden_grad, up_weight.T, preferred_element_type=jnp.float32)
        middle_part, second_gain_part, second_shift_part = jax.vjp(
            norm_rows, middle, second_gain, second_shift
        )[1](second_in_grad)
        sums[6] = sums[6] + second_gain_part
        sums[7] = sums[7] + second_shift_part
        middle_grad = middle_part + out_cot
        branch_grad = (middle_grad * keep_attn).astype(jnp.bfloat16)
        sums[4] = sums[4] + jnp.dot(attended_low.T, branch_grad, preferred_element_type=jnp.float32)
        sums[5] = sums[5] + jnp.sum(branch_grad.astype(jnp.float32), axis=0)
        attended_grad = jnp.dot(
            branch_grad, output_weight.T, preferred_element_type=jnp.float32
        ).astype(jnp.bfloat16)
        out_grad = attended_grad.reshape(rows_micro, slots, width)
        inner = jnp.transpose(
            jnp.sum(
                split_heads(
                    (attended_grad.astype(jnp.float32) * attended).reshape(rows_micro, slots, width)
                ),
                axis=-1,
            ),
            (0, 2, 1),
        )
        query_grad = jnp.zeros((rows_micro, slots, width), jnp.float32)
        visiting = (keys, values, ids_query)
        key_grad = jnp.zeros((rows_micro, slots, width), jnp.float32)
        value_grad = jnp.zeros((rows_micro, slots, width), jnp.float32)
        for step in range(blocks):
            query_part, key_part, value_part = attention_back(
                query, out_grad, ids_query, log_total, inner, visiting
            )
            query_grad = query_grad + query_part
            key_grad, value_grad = (
                from_behind((key_grad + key_part).astype(jnp.bfloat16), "blk", 1).astype(
                    jnp.float32
                ),
                from_behind((value_grad + value_part).astype(jnp.bfloat16), "blk", 1).astype(
                    jnp.float32
                ),
            )
            if step + 1 < blocks:
                visiting = from_behind((visiting[0], visiting[1], visiting[2]), "blk", 1)
        joined_grad = (
            jnp.concatenate([query_grad, key_grad, value_grad], axis=-1)
            .astype(jnp.bfloat16)
            .reshape(count, 3 * width)
        )
        sums[2] = sums[2] + jnp.dot(normed.T, joined_grad, preferred_element_type=jnp.float32)
        joined_sums = jnp.sum(joined_grad.astype(jnp.float32), axis=0)
        sums[3] = sums[3] + jnp.stack([joined_sums[:width], joined_sums[2 * width :]])
        first_in_grad = jnp.dot(joined_grad, input_weight.T, preferred_element_type=jnp.float32)
        rows_part, first_gain_part, first_shift_part = jax.vjp(
            norm_rows, rows_in, first_gain, first_shift
        )[1](first_in_grad)
        sums[0] = sums[0] + first_gain_part
        sums[1] = sums[1] + first_shift_part
        input_grads.append(
            (rows_part + middle_grad).astype(jnp.bfloat16).reshape(rows_micro, slots, width)
        )
    totals = lax.psum(
        (
            sums[0],
            sums[1],
            sums[2],
            sums[3],
            sums[4],
            sums[5],
            sums[6],
            sums[7],
            sums[8],
            sums[9],
            sums[10],
            sums[11],
        ),
        ("rows", "blk"),
    )
    return (
        jnp.concatenate(results, axis=0),
        jnp.concatenate(input_grads, axis=0),
        totals[0],
        totals[1],
        totals[2],
        totals[3],
        totals[4],
        totals[5],
        totals[6],
        totals[7],
        totals[8],
        totals[9],
        totals[10],
        totals[11],
    )


def swap(value, axis, bit):
    return lax.ppermute(value, axis, [(i, i ^ bit) for i in range(lax.axis_size(axis))])


def side(axis, bit):
    return (lax.axis_index(axis) // bit) % 2


def after(value, *others):
    return lax.optimization_barrier((value, *others))[0]


def axis_bits(axis):
    bits, bit = [], 1
    while bit < lax.axis_size(axis):
        bits.append((axis, bit))
        bit *= 2
    return bits


def add_low(a, b):
    return (a.astype(F32) + b.astype(F32)).astype(BF16)


def swap_two(value, step):
    rows, blocks = lax.axis_size("rows"), lax.axis_size("blk")
    pairs = []
    for r in range(rows):
        for b in range(blocks):
            axis, bit = step[b % 2]
            other = (r ^ bit, b) if axis == "rows" else (r, b ^ bit)
            pairs.append((r * blocks + b, other[0] * blocks + other[1]))
    return lax.ppermute(value, ("rows", "blk"), pairs)


def side_two(step):
    return jnp.where(side("blk", 1) == 0, side(*step[0]), side(*step[1]))


class Order:
    def __init__(self):
        self.last = ()

    def hold(self, value):
        return after(value, *self.last) if self.last else value

    def advance(self, *parts):
        parts = [part for part in parts if part.result is None]
        if parts:
            held = lax.optimization_barrier(([part.recv for part in parts], self.last))[0]
            self.done(*[value for part, recv in zip(parts, held) for value in part.step(recv)])

    def done(self, *values):
        self.last = values
        return values[0] if len(values) == 1 else values


class Chain:
    def __init__(self, steps, send, keep):
        self.steps, self.at = steps, -1
        self.recv, self.keep, self.result = send, keep, None

    def step(self, recv):
        keep, n = self.keep, len(self.steps)
        if self.at < 0:
            send, self.recv = recv, swap(recv, "blk", 1)
        elif self.at < n:
            step = self.steps[self.at]
            half = keep.shape[0] // 2
            own = side_two(step)

            def part(which):
                return add_low(
                    lax.dynamic_slice_in_dim(keep, which * half, half, 0),
                    lax.dynamic_slice_in_dim(recv, which * half, half, 0),
                )

            send, self.keep = part(1 - own), part(own)
            self.recv = swap_two(send, step)
        elif self.at < 2 * n:
            send = add_low(keep, recv) if self.at == n else jnp.concatenate([keep, recv], axis=0)
            send = self.keep = lax.optimization_barrier(send)
            self.recv = swap_two(send, self.steps[2 * n - 1 - self.at])
        elif self.at == 2 * n:
            self.at, self.keep, self.recv = self.at + 1, (keep, recv), [swap(piece, "blk", 1) for piece in (keep, recv)]
            return keep, recv
        else:
            self.result, self.recv = (*keep, *recv), None
            return ()
        self.at += 1
        return send, self.keep


class Small:
    def __init__(self, value):
        count = lax.axis_size("rows") * lax.axis_size("blk")
        self.recv, self.result, self.sent = jnp.broadcast_to(value[None], (count, *value.shape)), None, False

    def step(self, recv):
        if not self.sent:
            self.recv, self.sent = lax.all_to_all(recv, ("rows", "blk"), 0, 0), True
            return (recv,)
        self.result, self.recv = jnp.sum(recv, axis=0), None
        return (self.result,)


class Home:
    def __init__(self, pieces):
        self.recv, self.result, self.sent = pieces, None, False

    def step(self, recv):
        if not self.sent:
            self.recv, self.sent = lax.all_to_all(recv, "blk", 0, 0), True
        else:
            self.result, self.recv = recv, None
        return (recv,)


def block_turns(steps):
    core = side("blk", 1)
    turns = []
    for c in range(2):
        turn = 0
        for step in steps:
            turn = turn * 2 + side(*step[c])
        turns.append(turn)
    first, second = jnp.where(core == 0, turns[0], turns[1]), jnp.where(core == 0, turns[1], turns[0])
    return core.astype(jnp.int32).reshape(1), jnp.stack([first, second]).astype(jnp.int32), 1 << len(steps)


def local_rows(
    inputs,
    image_index,
    keep_mask,
    first_gain,
    first_shift,
    input_weight,
    input_bias,
    output_weight,
    output_bias,
    second_gain,
    second_shift,
    up_weight,
    up_bias,
    down_weight,
    down_bias,
    cotangent,
):
    blocks, span, width = inputs.shape
    ff = up_weight.shape[1]
    me = lax.axis_index("blk")

    def row_piece(array, s):
        return lax.dynamic_index_in_dim(array, me ^ s, 0, keepdims=False)

    xs_send = [row_piece(inputs, s) for s in range(blocks)]
    xs_in = xs_send[:1] + [swap(xs_send[s], "blk", s) for s in range(1, blocks)]
    ids = [row_piece(image_index, 0)] + [
        swap(row_piece(after(image_index, *xs_send), s), "blk", s) for s in range(1, blocks)
    ]
    cots = [row_piece(cotangent, 0)] + [
        swap(after(row_piece(cotangent, s), *xs_in), "blk", s) for s in range(1, blocks)
    ]
    ids = jnp.concatenate(ids)
    image = jnp.where(ids < 0, 4, ids)
    order_key = image * ids.shape[0] + jnp.arange(ids.shape[0], dtype=jnp.int32)
    less = (order_key[None, :] < order_key[:, None]).astype(jnp.int32)
    rank = jnp.sum(less, axis=1)
    starts = jnp.sum((image[None, :] < jnp.arange(6, dtype=jnp.int32)[:, None]).astype(jnp.int32), axis=1)
    keep = lax.dynamic_index_in_dim(keep_mask, me, 0, keepdims=False).astype(F32) / keep_rate
    rank_row, rank_col = rank[None, :], rank[:, None]

    bias = jnp.stack([input_bias[0], jnp.zeros_like(input_bias[0]), input_bias[1]])
    xs, normed, qkv = qkv_call(rank_row, xs_in, first_gain[None], first_shift[None], input_weight, bias)
    attended, stat = forward_call(starts, qkv)
    vectors = jnp.stack([output_bias, second_gain, second_shift, down_bias])
    core = side("blk", 1).astype(jnp.int32).reshape(1)
    cot, att_low, middle, normed2, mlp_grad, sums_mid = middle_call(
        keep, rank_row, cots, attended, xs, output_weight, vectors
    )
    (up_send, up_keep, down_send, down_keep, up_sums, result, middle_grad, branch, att_grad, sums2) = mlp_call(
        core, keep, normed2, mlp_grad, middle, cot, att_low, output_weight, vectors, up_weight, up_bias[None], down_weight
    )

    y, x, z = axis_bits("blk")[1], axis_bits("rows")[0], axis_bits("rows")[1:]
    far = [(d, d) for d in z[1:]]
    xy = [(x, y), (y, x), (z[0], z[0])] + far
    zx = [(z[0], z[0]), (x, y), (y, x)] + far
    order = Order()
    order.done(att_grad)
    up_chain, down_chain = Chain(zx, up_send, up_keep), Chain(xy, down_send, down_keep)

    order.advance(down_chain, up_chain)
    result_home = Home(order.done(unsort_call(me.reshape(1), rank_col, blocks, order.hold(result))))
    order.advance(down_chain, up_chain, result_home)
    grads, bias_sums = backward_call(starts, qkv, order.hold(att_grad), attended, stat, 0, PAIRS)
    order.done(grads)
    order.advance(down_chain, up_chain, result_home)
    input_chain = Chain(
        xy, *order.done(*input_weights_call(core, order.hold(normed), grads, bias_sums, sums2, sums_mid, up_sums))
    )
    order.advance(down_chain, up_chain, input_chain)
    inputs_grad, sums1 = order.done(*input_call(grads, input_weight, xs, order.hold(middle_grad), first_gain[None]))
    small = Small(sums1[:2])
    order.advance(down_chain, up_chain, input_chain, small)
    home = Home(order.done(unsort_call(me.reshape(1), rank_col, blocks, order.hold(inputs_grad))))
    order.advance(down_chain, up_chain, input_chain, small, home)
    order.advance(down_chain, up_chain, input_chain)
    order.advance(down_chain, up_chain, input_chain, home)
    while down_chain.at < 2 * len(xy):
        order.advance(down_chain, up_chain, input_chain)
    result_out = order.done(copy_call(order.hold(result_home.result)))
    inputs_out = order.done(copy_call(order.hold(home.result)))
    order.advance(down_chain, up_chain, input_chain)
    order.advance(down_chain, up_chain, input_chain)
    up_total = order.done(up_final(*block_turns(zx), (order.hold(up_chain.result[0]), *up_chain.result[1:])))
    order.advance(input_chain)
    down_total, out_total = order.done(
        *down_final(*block_turns(xy), (order.hold(down_chain.result[0]), *down_chain.result[1:]), ff)
    )
    while input_chain.result is None:
        order.advance(input_chain)
    input_total, sums = input_final(*block_turns(xy), input_chain.result)
    sums = jnp.concatenate([small.result, sums[:, :16].T])

    return (
        result_out,
        inputs_out,
        sums[0],
        sums[1],
        input_total,
        jnp.stack([sums[2], sums[4]]),
        out_total,
        sums[7],
        sums[5],
        sums[6],
        up_total,
        sums[9:13].reshape(ff),
        down_total,
        sums[8],
    )


def solution(mesh):
    blocks, groups = mesh.shape["blk"], mesh.shape["rows"]

    def run(*args):
        whole_rows = args[0].shape[0] // groups == blocks == 4 and groups in (4, 8, 16)
        return jax.shard_map(
            local_rows if whole_rows else local,
            mesh=mesh,
            in_specs=(P("rows", "blk", None), P("rows", "blk"), P("rows", None)) + (P(),) * 12 + (P("rows", "blk", None),),
            out_specs=(P("rows", "blk", None),) * 2 + (P(),) * 12,
            check_vma=False,
        )(*args)

    return run
```

```python
import functools

import jax
import jax.numpy as jnp
from jax import lax
from jax.experimental import pallas as pl
from jax.experimental.pallas import tpu as pltpu
from jax.sharding import PartitionSpec as P

HEADS = 12
HEAD_DIM = 64
PAIR = 2 * HEAD_DIM
PAIRS = HEADS // 2
eps_norm = 1e-06
keep_rate = 0.9
F32 = jnp.float32
BF16 = jnp.bfloat16
NEG = -1e30
VMEM = 62 * 1024 * 1024
QUICK = pl.CostEstimate(flops=1 << 20, bytes_accessed=1 << 16, transcendentals=0)


def dot(a, b):
    return jnp.dot(a, b, preferred_element_type=F32)


def dot_nt(a, b):
    return lax.dot_general(a, b, (((1,), (1,)), ((), ())), preferred_element_type=F32)


def dot_tn(a, b):
    return lax.dot_general(a, b, (((0,), (0,)), ((), ())), preferred_element_type=F32)


def whole(shape):
    return pl.BlockSpec(shape, lambda *g: (0,) * len(shape), pipeline_mode=pl.Buffered(1))


def centre_scale(values):
    centre = values - jnp.mean(values, axis=-1, keepdims=True)
    spread = jnp.mean(centre * centre, axis=-1, keepdims=True)
    inv = lax.rsqrt(spread + eps_norm)
    return centre * inv, inv


def norm_back(grad_hat, hat, inv):
    first = jnp.mean(grad_hat, axis=-1, keepdims=True)
    second = jnp.mean(grad_hat * hat, axis=-1, keepdims=True)
    return (grad_hat - first - hat * second) * inv


def gather_pieces(step, pieces, row):
    @pl.when(step == 0)
    def _():
        span = pieces[0].shape[0]
        for i, piece in enumerate(pieces):
            row[i * span : (i + 1) * span, :] = piece[...]


def sort_tile(rank_row, tile, step, row):
    place = step * tile + lax.broadcasted_iota(jnp.int32, (tile, row.shape[0]), 0)
    return dot((rank_row == place).astype(BF16), row[...])


def qkv_kernel(n, tile, *refs):
    rank, *pieces = refs[: n + 1]
    gain, shift, weight, bias, xs_out, normed_out, qkv_out, row = refs[n + 1 :]
    gather_pieces(pl.program_id(0), pieces, row)
    xs = sort_tile(rank[...], tile, pl.program_id(0), row)
    xs_out[...] = xs.astype(BF16)
    hat, _ = centre_scale(xs)
    normed = (hat * gain[...] + shift[...]).astype(BF16)
    normed_out[...] = normed
    width = normed.shape[1]
    for j in range(3):
        cols = slice(j * width, (j + 1) * width)
        mixed = (dot(normed, weight[:, cols]) + bias[j : j + 1, :]).astype(BF16)
        qkv_out[j] = mixed * BF16(HEAD_DIM**-0.5) if j == 0 else mixed


def qkv_call(rank, pieces, gain, shift, weight, bias, tile=288):
    n = len(pieces)
    span, width = pieces[0].shape
    count = n * span
    return pl.pallas_call(
        functools.partial(qkv_kernel, n, tile),
        grid=(count // tile,),
        in_specs=[whole((1, count))]
        + [whole((span, width))] * n
        + [whole((1, width)), whole((1, width)), whole(weight.shape), whole(bias.shape)],
        out_specs=[
            pl.BlockSpec((tile, width), lambda i: (i, 0)),
            pl.BlockSpec((tile, width), lambda i: (i, 0)),
            pl.BlockSpec((3, tile, width), lambda i: (0, i, 0)),
        ],
        out_shape=[
            jax.ShapeDtypeStruct((count, width), BF16),
            jax.ShapeDtypeStruct((count, width), BF16),
            jax.ShapeDtypeStruct((3, count, width), BF16),
        ],
        scratch_shapes=[pltpu.VMEM((count, width), BF16)],
        compiler_params=pltpu.CompilerParams(vmem_limit_bytes=VMEM),
        cost_estimate=QUICK,
        name="sort_qkv",
    )(rank, *pieces, gain, shift, weight, bias)


SMALL = 304
LARGE = 384


def windows(starts, seg, length):
    first, last = starts[seg], starts[seg + 1]
    aligned = first // 16 * 16
    small = SMALL if seg < 4 else LARGE
    at_small = pl.multiple_of(jnp.minimum(aligned, length - small), 16)
    at_large = pl.multiple_of(jnp.minimum(aligned, length - LARGE), 16)
    return first, last, small, at_small, at_large


def inside(at, size, lanes, first, last):
    place = at + lax.broadcasted_iota(jnp.int32, (size, lanes), 0)
    return (place >= first) & (place < last)


def forward_kernel(starts, qkv, out, stat):
    length = qkv.shape[1]
    for seg in range(5):
        first, last, small, at_q, at_k = windows(starts, seg, length)
        rows_q = pl.ds(at_q, small)
        q = qkv[0, rows_q, :]
        k = qkv[1, pl.ds(at_k, LARGE), :]
        v = qkv[2, pl.ds(at_k, LARGE), :]
        lane = lax.broadcasted_iota(jnp.int32, (LARGE, PAIR), 1)
        lane_q = lax.broadcasted_iota(jnp.int32, (small, PAIR), 1)
        low = lane < HEAD_DIM
        seen = inside(at_k, LARGE, PAIR, first, last)
        zero = jnp.zeros((LARGE, PAIR), BF16)
        one = jnp.ones((LARGE, PAIR), BF16)
        bias = jnp.where((lane == 0) & ~seen, NEG, 0.0).astype(BF16)
        q_ext = jnp.concatenate([q, (lane_q == 0).astype(BF16)], axis=1)
        halves = (low, ~low)
        k_ext = [jnp.concatenate([jnp.where(half, k, zero), bias], axis=1) for half in halves]
        mixes = [
            jnp.concatenate([jnp.where(half, v, zero), jnp.where(half, one, zero)], axis=1) for half in halves
        ]
        pair = dot_nt(q_ext, jnp.concatenate(k_ext, axis=0))
        tops, weights = [], []
        for h in range(2):
            scores = pair[:, h * LARGE : (h + 1) * LARGE]
            top = jnp.max(scores, axis=-1, keepdims=True)
            tops.append(top)
            weights.append(jnp.exp(scores - top).astype(BF16))
        both = dot(jnp.concatenate(weights, axis=1), jnp.concatenate(mixes, axis=0))
        total = both[:, PAIR:]
        peak = jnp.where(lane_q < HEAD_DIM, tops[0], tops[1])
        mine = inside(at_q, small, PAIR, first, last)
        out[rows_q, :] = jnp.where(mine, both[:, :PAIR] / total, out[rows_q, :])
        stat[rows_q, :] = jnp.where(mine, peak + jnp.log(total), stat[rows_q, :])


def forward_call(starts, qkv):
    _, count, wide = qkv.shape
    pairs = wide // PAIR
    return pl.pallas_call(
        forward_kernel,
        grid_spec=pltpu.PrefetchScalarGridSpec(
            num_scalar_prefetch=1,
            grid=(pairs,),
            in_specs=[pl.BlockSpec((3, count, PAIR), lambda p, s: (0, 0, p))],
            out_specs=[
                pl.BlockSpec((count, PAIR), lambda p, s: (0, p)),
                pl.BlockSpec((count, PAIR), lambda p, s: (0, p)),
            ],
        ),
        out_shape=[jax.ShapeDtypeStruct((count, pairs * PAIR), F32)] * 2,
        compiler_params=pltpu.CompilerParams(vmem_limit_bytes=VMEM),
        cost_estimate=QUICK,
        name="attention_forward",
    )(starts, qkv)


def split3(value):
    high = value.astype(BF16)
    rest = value - high.astype(F32)
    mid = rest.astype(BF16)
    return high, mid, (rest - mid.astype(F32)).astype(BF16)


def backward_kernel(starts, qkv, grad, att, stat, *refs):
    out, sums = refs[-2:]
    length = qkv.shape[1]
    third = lax.broadcasted_iota(jnp.int32, (PAIR, PAIR), 0) // HEAD_DIM
    block = (third == lax.broadcasted_iota(jnp.int32, (PAIR, PAIR), 1) // HEAD_DIM).astype(BF16)
    for seg in range(5):
        first, last, small, at_k, at_q = windows(starts, seg, length)
        rows_q, rows_k = pl.ds(at_q, LARGE), pl.ds(at_k, small)
        lane_q = lax.broadcasted_iota(jnp.int32, (LARGE, PAIR), 1)
        lane_k = lax.broadcasted_iota(jnp.int32, (small, PAIR), 1)
        spot_q, spot_k = lane_q % HEAD_DIM, lane_k % HEAD_DIM
        mine_q = inside(at_q, LARGE, PAIR, first, last)
        mine_k = inside(at_k, small, PAIR, first, last)
        zero_q = jnp.zeros((LARGE, PAIR), BF16)
        zero_k = jnp.zeros((small, PAIR), BF16)
        q = qkv[0, rows_q, :]
        k = jnp.where(mine_k, qkv[1, rows_k, :], zero_k)
        v = qkv[2, rows_k, :]
        g = jnp.where(mine_q, grad[rows_q, :], zero_q)
        prod = g.astype(F32) * jnp.where(mine_q, att[rows_q, :], 0.0)
        p_high = prod.astype(BF16)
        p_low = (prod - p_high.astype(F32)).astype(BF16)
        inner = dot(p_high, block) + dot(p_low, block)
        logs = jnp.where(mine_q, stat[rows_q, :], 0.0)

        def spread(value, fifth):
            a, b, c = split3(value)
            return jnp.where(
                spot_q == 0, a, jnp.where(spot_q == 1, b, jnp.where(spot_q == 2, c, fifth))
            )

        query_bias = jnp.where(mine_q, 0.0, NEG).astype(BF16)
        unit = jnp.ones((LARGE, PAIR), BF16)
        q_tail = spread(logs, jnp.where(spot_q == 3, unit, jnp.where(spot_q == 4, query_bias, zero_q)))
        g_tail = spread(inner, zero_q)
        key_bias = jnp.where(mine_k, 0.0, NEG).astype(BF16)
        minus = jnp.where(spot_k < 3, -1.0, 0.0).astype(BF16)
        k_tail = jnp.where(
            spot_k == 3, key_bias, jnp.where(spot_k == 4, jnp.ones((small, PAIR), BF16), minus)
        )
        heads_q = [lane_q // HEAD_DIM == h for h in range(2)]
        qs = [jnp.where(head, q, zero_q) for head in heads_q]
        gs = [jnp.where(head, g, zero_q) for head in heads_q]
        q_both = [jnp.concatenate([x, jnp.where(head, q_tail, zero_q)], axis=1) for x, head in zip(qs, heads_q)]
        g_both = [jnp.concatenate([x, jnp.where(head, g_tail, zero_q)], axis=1) for x, head in zip(gs, heads_q)]
        prob = jnp.exp(dot_nt(jnp.concatenate([k, k_tail], axis=1), jnp.concatenate(q_both, axis=0)))
        prob_grad = dot_nt(jnp.concatenate([v, minus], axis=1), jnp.concatenate(g_both, axis=0))
        score_grad = (prob * prob_grad).astype(BF16)
        value_grad = dot(prob.astype(BF16), jnp.concatenate(gs, axis=0))
        key_grad = dot(score_grad, jnp.concatenate(qs, axis=0))
        stacked = jnp.concatenate([score_grad[:, :LARGE], score_grad[:, LARGE:]], axis=0)
        ks = [jnp.where(lane_k // HEAD_DIM == h, k, zero_k) for h in range(2)]
        query_grad = dot_tn(stacked, jnp.concatenate(ks, axis=0))
        query_grad = (query_grad * HEAD_DIM**-0.5).astype(BF16)
        out[0, rows_q, :] = jnp.where(mine_q, query_grad, out[0, rows_q, :])
        out[1, rows_k, :] = jnp.where(mine_k, key_grad.astype(BF16), out[1, rows_k, :])
        out[2, rows_k, :] = jnp.where(mine_k, value_grad.astype(BF16), out[2, rows_k, :])
    for j in range(3):
        sums[j : j + 1, :] = jnp.sum(out[j].astype(F32), axis=0, keepdims=True)


def backward_call(starts, qkv, grad, att, stat, first_pair, pairs, before=None):
    _, count, width = qkv.shape
    held = [] if before is None else list(before)
    return pl.pallas_call(
        backward_kernel,
        grid_spec=pltpu.PrefetchScalarGridSpec(
            num_scalar_prefetch=1,
            grid=(pairs,),
            in_specs=[pl.BlockSpec((3, count, PAIR), lambda p, s: (0, 0, p + first_pair))]
            + [pl.BlockSpec((count, PAIR), lambda p, s: (0, p + first_pair))] * 3
            + [pl.BlockSpec(memory_space=pl.ANY)] * len(held),
            out_specs=[
                pl.BlockSpec((3, count, PAIR), lambda p, s: (0, 0, p + first_pair)),
                pl.BlockSpec((8, PAIR), lambda p, s: (0, p + first_pair)),
            ],
        ),
        out_shape=[
            jax.ShapeDtypeStruct((3, count, width), BF16),
            jax.ShapeDtypeStruct((8, width), F32),
        ],
        input_output_aliases={5: 0, 6: 1} if held else {},
        compiler_params=pltpu.CompilerParams(vmem_limit_bytes=VMEM),
        cost_estimate=QUICK,
        name="attention_backward",
    )(starts, qkv, grad, att, stat, *held)


ERF = (0.254829592, -0.284496736, 1.421413741, -1.453152027, 1.061405429)


def gelu_pair(u):
    size = jnp.abs(u)
    t = 1.0 / (1.0 + (0.3275911 * 0.5**0.5) * size)
    bell = jnp.exp(u * u * -0.5)
    poly = ERF[4] * t + ERF[3]
    for c in (ERF[2], ERF[1], ERF[0]):
        poly = poly * t + c
    tail = 0.5 * poly * t * bell
    phi = jnp.where(u < 0, tail, 1.0 - tail)
    return u * phi, phi + u * bell * 0.3989422804014327


def middle_kernel(n, tile, *refs):
    keep, rank, *pieces = refs[: n + 2]
    att, xs, out_w, vectors, cot_out, att_low_out, middle_out, normed_out, mlp_out, sums, row = refs[n + 2 :]
    step = pl.program_id(0)
    gather_pieces(step, pieces, row)
    cot = sort_tile(rank[...], tile, step, row)
    cot_out[...] = cot.astype(BF16)
    mlp_grad = (cot * keep[1]).astype(BF16)
    mlp_out[...] = mlp_grad
    att_low = att[...].astype(BF16)
    att_low_out[...] = att_low
    middle = xs[...].astype(F32) + keep[0] * (dot(att_low, out_w[...]) + vectors[0:1, :])
    middle_out[...] = middle
    hat, _ = centre_scale(middle)
    normed_out[...] = (hat * vectors[1:2, :] + vectors[2:3, :]).astype(BF16)

    @pl.when(step == 0)
    def _():
        sums[...] = jnp.zeros_like(sums)

    sums[0:1, :] += jnp.sum(mlp_grad.astype(F32), axis=0, keepdims=True)


def middle_call(keep, rank, pieces, att, xs, out_w, vectors, tile=384):
    n = len(pieces)
    span, width = pieces[0].shape
    count = n * span
    rows = pl.BlockSpec((tile, width), lambda i: (i, 0))
    low, full = jax.ShapeDtypeStruct((count, width), BF16), jax.ShapeDtypeStruct((count, width), F32)
    return pl.pallas_call(
        functools.partial(middle_kernel, n, tile),
        grid=(count // tile,),
        in_specs=[pl.BlockSpec(memory_space=pltpu.SMEM), whole((1, count))]
        + [whole((span, width))] * n
        + [rows, rows, whole(out_w.shape), whole(vectors.shape)],
        out_specs=[rows] * 5 + [pl.BlockSpec((8, width), lambda i: (0, 0))],
        out_shape=[low, low, full, low, low, jax.ShapeDtypeStruct((8, width), F32)],
        scratch_shapes=[pltpu.VMEM((count, width), BF16)],
        compiler_params=pltpu.CompilerParams(vmem_limit_bytes=VMEM),
        cost_estimate=QUICK,
        name="middle",
    )(keep, rank, *pieces, att, xs, out_w, vectors)


def mlp_kernel(parts, core, keep, normed, mlp_grad, middle, cot, att, out_w, vectors, up_w, up_b, down_w, *refs):
    (
        up_send, up_keep, down_send, down_keep, up_sums, result, middle_grad_out, branch_out, att_grad_out, sums,
        lift, back, act_all, hidden_all,
    ) = refs
    step, half = pl.program_id(0), pl.num_programs(0) // 2
    count, width = normed.shape
    cuts = [slice(i * (count // parts), (i + 1) * (count // parts)) for i in range(parts)]

    @pl.when(step == 0)
    def _():
        lift[...] = jnp.zeros_like(lift)
        back[...] = jnp.zeros_like(back)

    @pl.when(step < 2 * half)
    def _():
        total = jnp.zeros(up_sums.shape, F32)
        ready = None
        for rows in cuts + [None]:
            fresh = None
            if rows is not None:
                u = dot(normed[rows, :], up_w[...]) + up_b[...]
                fresh = (rows, u, dot_nt(mlp_grad[rows, :], down_w[...]))
            if ready is not None:
                past, u, act_grad = ready
                act, slope = gelu_pair(u)
                act_all[past, :] = act.astype(BF16)
                hidden = (act_grad * slope).astype(BF16)
                hidden_all[past, :] = hidden
                total = total + jnp.sum(hidden.astype(F32), axis=0, keepdims=True)
            ready = fresh
        lift[...] += dot(act_all[...], down_w[...])
        back[...] += dot_nt(hidden_all[...], up_w[...])
        up_sums[...] = total
        up_part = dot_tn(normed[...], hidden_all[...]).astype(BF16)
        down_part = dot_tn(act_all[...], mlp_grad[...]).astype(BF16)

        @pl.when(step < half)
        def _():
            up_send[...] = up_part
            down_send[...] = down_part

        @pl.when(step >= half)
        def _():
            up_keep[...] = up_part
            down_keep[...] = down_part

    @pl.when(step == 2 * half)
    def _():
        gain, down_b = vectors[1:2, :], vectors[3:4, :]
        sums[...] = jnp.zeros_like(sums)
        for rows in cuts:
            mid, grad = middle[rows, :], back[rows, :]
            hat, inv = centre_scale(mid)
            result[rows, :] = (mid + keep[1] * (lift[rows, :] + down_b)).astype(BF16)
            middle_grad = cot[rows, :].astype(F32) + norm_back(grad * gain, hat, inv)
            middle_grad_out[rows, :] = middle_grad
            branch = (keep[0] * middle_grad).astype(BF16)
            branch_out[rows, :] = branch
            att_grad_out[rows, :] = dot_nt(branch, out_w[...]).astype(BF16)
            sums[0:1, :] += jnp.sum(grad * hat, axis=0, keepdims=True)
            sums[1:2, :] += jnp.sum(grad, axis=0, keepdims=True)
            sums[2:3, :] += jnp.sum(branch.astype(F32), axis=0, keepdims=True)
        for out, c in ((down_send, 1 - core[0]), (down_keep, core[0])):
            cols = pl.ds(pl.multiple_of(c * (width // 2), 128), width // 2)
            out[: width // 2, :] = dot_tn(att[:, cols], branch_out[...]).astype(BF16)
            out[width // 2 :, :] = jnp.zeros((out.shape[0] - width // 2, width), BF16)


def mlp_call(core, keep, normed, mlp_grad, middle, cot, att, out_w, vectors, up_w, up_b, down_w, chunk=512, parts=4):
    count, width = normed.shape
    ff = up_w.shape[1]
    half = ff // 2 // chunk

    def place(i, c):
        i = jnp.minimum(i, 2 * half - 1)
        return jnp.where(i < half, (1 - c[0]) * half + i, c[0] * half + i - half)

    def first(i):
        return jnp.minimum(i, half - 1)

    def second(i):
        return jnp.clip(i - half, 0, half - 1)

    def extra(i, index):
        return jnp.where(i == 2 * half, half, index)

    low, full = jax.ShapeDtypeStruct((count, width), BF16), jax.ShapeDtypeStruct((count, width), F32)
    return pl.pallas_call(
        functools.partial(mlp_kernel, parts),
        grid_spec=pltpu.PrefetchScalarGridSpec(
            num_scalar_prefetch=1,
            grid=(2 * half + 1,),
            in_specs=[pl.BlockSpec(memory_space=pltpu.SMEM)]
            + [whole((count, width))] * 5
            + [
                whole(out_w.shape),
                whole(vectors.shape),
                pl.BlockSpec((width, chunk), lambda i, c: (0, place(i, c))),
                pl.BlockSpec((1, chunk), lambda i, c: (0, place(i, c))),
                pl.BlockSpec((chunk, width), lambda i, c: (place(i, c), 0)),
            ],
            out_specs=[
                pl.BlockSpec((width, chunk), lambda i, c: (0, first(i))),
                pl.BlockSpec((width, chunk), lambda i, c: (0, second(i))),
                pl.BlockSpec((chunk, width), lambda i, c: (extra(i, first(i)), 0)),
                pl.BlockSpec((chunk, width), lambda i, c: (extra(i, second(i)), 0)),
                pl.BlockSpec((1, chunk), lambda i, c: (0, place(i, c))),
            ]
            + [whole((count, width))] * 4
            + [whole((8, width))],
            scratch_shapes=[pltpu.VMEM((count, width), F32)] * 2 + [pltpu.VMEM((count, chunk), BF16)] * 2,
        ),
        out_shape=[jax.ShapeDtypeStruct((width, ff // 2), BF16)] * 2
        + [jax.ShapeDtypeStruct((ff // 2 + chunk, width), BF16)] * 2
        + [jax.ShapeDtypeStruct((1, ff), F32), low, full, low, low, jax.ShapeDtypeStruct((8, width), F32)],
        compiler_params=pltpu.CompilerParams(vmem_limit_bytes=VMEM),
        cost_estimate=QUICK,
        name="mlp",
    )(core, keep, normed, mlp_grad, middle, cot, att, out_w, vectors, up_w, up_b, down_w)


def input_kernel(grads, weight, xs, middle_grad, gain, out, sums):
    span = xs.shape[1]
    back = None
    for j in range(3):
        part = dot_nt(grads[j], weight[:, j * span : (j + 1) * span])
        back = part if back is None else back + part
    hat, inv = centre_scale(xs[...].astype(F32))
    out[...] = (middle_grad[...] + norm_back(back * gain[...], hat, inv)).astype(BF16)

    @pl.when(pl.program_id(0) == 0)
    def _():
        sums[...] = jnp.zeros_like(sums)

    sums[0:1, :] += jnp.sum(back * hat, axis=0, keepdims=True)
    sums[1:2, :] += jnp.sum(back, axis=0, keepdims=True)


def input_call(grads, weight, xs, middle_grad, gain, tile=288):
    count, width = xs.shape
    return pl.pallas_call(
        input_kernel,
        grid=(count // tile,),
        in_specs=[pl.BlockSpec((3, tile, width), lambda i: (0, i, 0))]
        + [
            whole(weight.shape),
            pl.BlockSpec((tile, width), lambda i: (i, 0)),
            pl.BlockSpec((tile, width), lambda i: (i, 0)),
            whole((1, width)),
        ],
        out_specs=[pl.BlockSpec((tile, width), lambda i: (i, 0)), pl.BlockSpec((8, width), lambda i: (0, 0))],
        out_shape=[jax.ShapeDtypeStruct((count, width), BF16), jax.ShapeDtypeStruct((8, width), F32)],
        compiler_params=pltpu.CompilerParams(vmem_limit_bytes=VMEM),
        cost_estimate=QUICK,
        name="input_backward",
    )(grads, weight, xs, middle_grad, gain)


def unsort_kernel(me, rank, source, out):
    count, span = source.shape[0], rank.shape[0]
    place = lax.broadcasted_iota(jnp.int32, (span, count), 1)
    out[0] = dot((rank[...] == place).astype(BF16), source[...]).astype(BF16)


def unsort_call(me, rank_col, n, array):
    count, width = array.shape
    span = count // n
    return pl.pallas_call(
        unsort_kernel,
        grid_spec=pltpu.PrefetchScalarGridSpec(
            num_scalar_prefetch=1,
            grid=(n,),
            in_specs=[pl.BlockSpec((span, 1), lambda i, m: (i, 0)), whole((count, width))],
            out_specs=pl.BlockSpec((1, span, width), lambda i, m: (m[0] ^ i, 0, 0)),
        ),
        out_shape=jax.ShapeDtypeStruct((n, span, width), BF16),
        compiler_params=pltpu.CompilerParams(vmem_limit_bytes=VMEM),
        cost_estimate=QUICK,
        name="unsort",
    )(me, rank_col, array)


VECTORS = 128


def input_weights_kernel(core, normed, grads, first, second, third, up_sums, send, keep):
    mid, width = normed.shape[1], grads.shape[2]
    h = core[0] ^ 1 ^ pl.program_id(0)

    def write(out):
        for j in range(3):
            out[:, j * width : (j + 1) * width] = dot_tn(normed[...], grads[j]).astype(BF16)
        rows = [first[0:3, :], second[0:3, :], third[0:1, :]]
        for i in range(up_sums.shape[1] // width):
            rows.append(up_sums[:, pl.ds(pl.multiple_of(i * width + h * mid, 128), mid)])
        count = sum(row.shape[0] for row in rows)
        rows.append(jnp.zeros((VECTORS - count, mid), F32))
        out[:, 3 * width :] = jnp.concatenate(rows, axis=0).T.astype(BF16)

    pl.when(pl.program_id(0) == 0)(lambda: write(send))
    pl.when(pl.program_id(0) == 1)(lambda: write(keep))


def input_weights_call(core, normed, grads, first, second, third, up_sums):
    count, width = normed.shape
    half = jax.ShapeDtypeStruct((width // 2, 3 * width + VECTORS), BF16)
    rows = pl.BlockSpec((count, width // 2), lambda i, c: (0, c[0] ^ 1 ^ i))
    vector = pl.BlockSpec((8, width // 2), lambda i, c: (0, c[0] ^ 1 ^ i))
    return pl.pallas_call(
        input_weights_kernel,
        grid_spec=pltpu.PrefetchScalarGridSpec(
            num_scalar_prefetch=1,
            grid=(2,),
            in_specs=[rows, whole(grads.shape), vector, vector, vector, whole(up_sums.shape)],
            out_specs=[whole(half.shape)] * 2,
        ),
        out_shape=[half] * 2,
        compiler_params=pltpu.CompilerParams(vmem_limit_bytes=VMEM),
        cost_estimate=QUICK,
        name="input_weights",
    )(core, normed, grads, first, second, third, up_sums)


GROUPS = 4


def final_call(core, turns, blocks, groups, pieces, name, spread, outs):
    size = blocks // groups
    rows = pieces[0].shape[0] // (blocks // 2)
    whole_tile = 1 if rows % 16 == 0 else 2

    def kernel(c, t, *refs):
        h, g = pl.program_id(0), pl.program_id(1)
        active = (h * groups + g) // (groups // 2)
        turn = t[h]
        place = g ^ (turn // size)

        def write(source):
            for j in range(0, size, whole_tile):
                part = source[j * rows : (j + whole_tile) * rows, :].astype(F32)
                for i in range(whole_tile):
                    spread(part[i * rows : (i + 1) * rows], (j + i) ^ (turn % size), place, refs[4:])

        for q in range(4):
            pl.when(active == q)(functools.partial(write, refs[q]))

    def in_spec(q):
        def index(h, g, c, t):
            return jnp.clip(h * groups + g - q * (groups // 2), 0, groups // 2 - 1), 0

        return pl.BlockSpec((size * rows, pieces[q].shape[1]), index)

    def out_spec(block, index):
        return pl.BlockSpec(block, lambda h, g, c, t: index(h ^ c[0], g, lambda n: n ^ (t[h] // size)))

    return pl.pallas_call(
        kernel,
        grid_spec=pltpu.PrefetchScalarGridSpec(
            num_scalar_prefetch=2,
            grid=(2, groups),
            in_specs=[in_spec(q) for q in range(4)],
            out_specs=[out_spec(block, index) for _, block, index in outs],
        ),
        out_shape=[jax.ShapeDtypeStruct(shape, F32) for shape, _, _ in outs],
        compiler_params=pltpu.CompilerParams(vmem_limit_bytes=VMEM),
        cost_estimate=QUICK,
        name=name,
    )(core, turns, *pieces)


def rows_at(ref, place, value):
    rows = value.shape[0]
    ref[pl.ds(pl.multiple_of(place * rows, 8), rows), :] = value


def down_final(core, turns, blocks, pieces, ff):
    rows, width = pieces[0].shape[0] // (blocks // 2), pieces[0].shape[1]
    size = blocks // GROUPS * rows

    def spread(block, j, place, refs):
        @pl.when(place < GROUPS - 1)
        def _():
            rows_at(refs[0], j, block)

        @pl.when((place == GROUPS - 1) & (j * rows < width // 2))
        def _():
            rows_at(refs[1], j, block)

    def down_index(h, g, place):
        at = place(g)
        near = place(jnp.where(g == 0, 1, g - 1))
        return h * (GROUPS - 1) + jnp.where(at == GROUPS - 1, near, at), 0

    outs = [
        ((ff, width), (size, width), down_index),
        ((width, width), (width // 2, width), lambda h, g, place: (h, 0)),
    ]
    return final_call(core, turns, blocks, GROUPS, pieces, "down_final", spread, outs)


def up_final(core, turns, blocks, pieces):
    rows, cols = pieces[0].shape[0] * 2, pieces[0].shape[1]

    def spread(block, j, place, refs):
        rows_at(refs[0], j, block)

    outs = [((rows, 2 * cols), (rows // 2, cols), lambda h, g, place: (place(g), h))]
    return final_call(core, turns, blocks, 2, pieces, "up_final", spread, outs)[0]


def input_final(core, turns, blocks, pieces):
    width, cols = pieces[0].shape[0] * 4, pieces[0].shape[1]

    def spread(block, j, place, refs):
        rows_at(refs[0], j, block[:, : 3 * width])
        rows_at(refs[1], j, block[:, 3 * width :])

    outs = [
        ((width, n), (width // 4, n), lambda h, g, place: (h * 2 + place(g), 0))
        for n in (3 * width, cols - 3 * width)
    ]
    return final_call(core, turns, blocks, 2, pieces, "input_final", spread, outs)


def copy_kernel(source, out):
    out[...] = source[...]


def copy_call(array):
    spec = pl.BlockSpec((1, *array.shape[1:]), lambda i: (i, 0, 0))
    return pl.pallas_call(
        copy_kernel,
        grid=(array.shape[0],),
        in_specs=[spec],
        out_specs=spec,
        out_shape=jax.ShapeDtypeStruct(array.shape, array.dtype),
        compiler_params=pltpu.CompilerParams(vmem_limit_bytes=VMEM),
        cost_estimate=QUICK,
        name="copy",
    )(array)


MICRO = 2


def from_behind(value, axis, steps):
    count = lax.axis_size(axis)
    pairs = [(source, (source + steps) % count) for source in range(count)]
    return lax.ppermute(value, axis, pairs)


def norm_rows(values, gain, shift):
    centre = values - jnp.mean(values, axis=-1, keepdims=True)
    spread = jnp.mean(centre * centre, axis=-1, keepdims=True)
    return centre * lax.rsqrt(spread + eps_norm) * gain + shift


def gelu_exact(values):
    return jax.nn.gelu(values, approximate=False)


def split_heads(block):
    return block.reshape(block.shape[0], block.shape[1], HEADS, HEAD_DIM)


def take_rows(array, first_row, count_rows):
    return lax.slice_in_dim(array, first_row, first_row + count_rows, axis=0)


def masked_scores(query, keys, ids_query, ids_keys):
    scores = jnp.einsum(
        "rqhd,rkhd->rhqk", split_heads(query), split_heads(keys), preferred_element_type=jnp.float32
    ) * HEAD_DIM ** (-0.5)
    same = ids_query[:, None, :, None] == ids_keys[:, None, None, :]
    return jnp.where(same, scores, -jnp.inf)


def attend_piece(carry, query, ids_query, piece):
    keys, values, ids_keys = piece
    peak, total, accum = carry
    scores = masked_scores(query, keys, ids_query, ids_keys)
    top = jnp.maximum(peak, jnp.max(scores, axis=-1))
    weights = jnp.exp(scores - top[..., None])
    total = jnp.sum(weights, axis=-1)
    update = jnp.einsum(
        "rhqk,rkhd->rqhd",
        weights.astype(jnp.bfloat16),
        split_heads(values),
        preferred_element_type=jnp.float32,
    )
    return (top, total, update.reshape(accum.shape))


def attention_forward(query, keys, values, ids_query):
    rows_here, slots, width = query.shape
    start_state = (
        jnp.full((rows_here, HEADS, slots), -1e30, jnp.float32),
        jnp.zeros((rows_here, HEADS, slots), jnp.float32),
        jnp.zeros((rows_here, slots, width), jnp.float32),
    )
    carry = attend_piece(
        start_state,
        query,
        ids_query,
        (
            lax.all_gather(keys, "blk", axis=1, tiled=True),
            lax.all_gather(values, "blk", axis=1, tiled=True),
            lax.all_gather(ids_query, "blk", axis=1, tiled=True),
        ),
    )
    return (carry[0], carry[1], carry[2], None)


def attention_back(query, out_grad, ids_query, log_total, inner, piece):
    keys, values, ids_keys = piece
    scale = HEAD_DIM ** (-0.5)
    scores = masked_scores(query, keys, ids_query, ids_keys)
    probs = jnp.exp(scores - log_total[..., None])
    prob_grad = jnp.einsum(
        "rqhd,rkhd->rhqk",
        split_heads(out_grad),
        split_heads(values),
        preferred_element_type=jnp.float32,
    )
    score_grad = (probs * (prob_grad - inner[..., None])).astype(jnp.bfloat16)
    value_grad = jnp.einsum(
        "rhqk,rqhd->rkhd",
        probs.astype(jnp.bfloat16),
        split_heads(out_grad),
        preferred_element_type=jnp.float32,
    )
    key_grad = (
        jnp.einsum(
            "rhqk,rqhd->rkhd", score_grad, split_heads(query), preferred_element_type=jnp.float32
        )
        * scale
    )
    query_grad = (
        jnp.einsum(
            "rhqk,rkhd->rqhd", score_grad, split_heads(keys), preferred_element_type=jnp.float32
        )
        * scale
    )
    return (
        query_grad.reshape(query.shape),
        key_grad.reshape(keys.shape),
        value_grad.reshape(values.shape),
    )


def local(
    inputs,
    image_index,
    keep_mask,
    first_gain,
    first_shift,
    input_weight,
    input_bias,
    output_weight,
    output_bias,
    second_gain,
    second_shift,
    up_weight,
    up_bias,
    down_weight,
    down_bias,
    cotangent,
):
    rows_local, slots, width = inputs.shape
    rows_micro = rows_local // MICRO
    count = rows_micro * slots
    blocks = lax.axis_size("blk")
    params = (
        first_gain,
        first_shift,
        input_weight,
        input_bias,
        output_weight,
        output_bias,
        second_gain,
        second_shift,
        up_weight,
        up_bias,
        down_weight,
        down_bias,
    )
    sums = [jnp.zeros(item.shape, jnp.float32) for item in params]
    results = []
    input_grads = []
    for micro in range(MICRO):
        first_row = micro * rows_micro
        rows_in = take_rows(inputs, first_row, rows_micro).astype(jnp.float32).reshape(count, width)
        out_cot = (
            take_rows(cotangent, first_row, rows_micro).astype(jnp.float32).reshape(count, width)
        )
        ids_query = take_rows(image_index, first_row, rows_micro).astype(jnp.bfloat16)
        keep = take_rows(keep_mask, first_row, rows_micro).astype(jnp.float32) / keep_rate
        keep_attn = jnp.broadcast_to(keep[:, None, 0:1], (rows_micro, slots, 1)).reshape(count, 1)
        keep_mlp = jnp.broadcast_to(keep[:, None, 1:2], (rows_micro, slots, 1)).reshape(count, 1)
        normed = norm_rows(rows_in, first_gain, first_shift).astype(jnp.bfloat16)
        mixed = jnp.dot(normed, input_weight, preferred_element_type=jnp.float32)
        query = (
            (mixed[:, :width] + input_bias[0])
            .astype(jnp.bfloat16)
            .reshape(rows_micro, slots, width)
        )
        keys = mixed[:, width : 2 * width].astype(jnp.bfloat16).reshape(rows_micro, slots, width)
        values = (
            (mixed[:, 2 * width :] + input_bias[1])
            .astype(jnp.bfloat16)
            .reshape(rows_micro, slots, width)
        )
        top, total, accum, whole = attention_forward(query, keys, values, ids_query)
        attended = (split_heads(accum) / jnp.transpose(total, (0, 2, 1))[..., None]).reshape(
            count, width
        )
        log_total = top + jnp.log(total)
        attended_low = attended.astype(jnp.bfloat16)
        branch = (
            jnp.dot(attended_low, output_weight, preferred_element_type=jnp.float32) + output_bias
        )
        middle = rows_in + keep_attn * branch
        normed_second = norm_rows(middle, second_gain, second_shift).astype(jnp.bfloat16)
        hidden = jnp.dot(normed_second, up_weight, preferred_element_type=jnp.float32) + up_bias
        active = gelu_exact(hidden).astype(jnp.bfloat16)
        branch_second = jnp.dot(active, down_weight, preferred_element_type=jnp.float32) + down_bias
        results.append(
            (middle + keep_mlp * branch_second)
            .astype(jnp.bfloat16)
            .reshape(rows_micro, slots, width)
        )
        mlp_grad = (out_cot * keep_mlp).astype(jnp.bfloat16)
        sums[10] = sums[10] + jnp.dot(active.T, mlp_grad, preferred_element_type=jnp.float32)
        sums[11] = sums[11] + jnp.sum(mlp_grad.astype(jnp.float32), axis=0)
        active_grad = jnp.dot(mlp_grad, down_weight.T, preferred_element_type=jnp.float32)
        hidden_grad = jax.vjp(gelu_exact, hidden)[1](active_grad)[0].astype(jnp.bfloat16)
        sums[8] = sums[8] + jnp.dot(
            normed_second.T, hidden_grad, preferred_element_type=jnp.float32
        )
        sums[9] = sums[9] + jnp.sum(hidden_grad.astype(jnp.float32), axis=0)
        second_in_grad = jnp.dot(hidden_grad, up_weight.T, preferred_element_type=jnp.float32)
        middle_part, second_gain_part, second_shift_part = jax.vjp(
            norm_rows, middle, second_gain, second_shift
        )[1](second_in_grad)
        sums[6] = sums[6] + second_gain_part
        sums[7] = sums[7] + second_shift_part
        middle_grad = middle_part + out_cot
        branch_grad = (middle_grad * keep_attn).astype(jnp.bfloat16)
        sums[4] = sums[4] + jnp.dot(attended_low.T, branch_grad, preferred_element_type=jnp.float32)
        sums[5] = sums[5] + jnp.sum(branch_grad.astype(jnp.float32), axis=0)
        attended_grad = jnp.dot(
            branch_grad, output_weight.T, preferred_element_type=jnp.float32
        ).astype(jnp.bfloat16)
        out_grad = attended_grad.reshape(rows_micro, slots, width)
        inner = jnp.transpose(
            jnp.sum(
                split_heads(
                    (attended_grad.astype(jnp.float32) * attended).reshape(rows_micro, slots, width)
                ),
                axis=-1,
            ),
            (0, 2, 1),
        )
        query_grad = jnp.zeros((rows_micro, slots, width), jnp.float32)
        visiting = (keys, values, ids_query)
        key_grad = jnp.zeros((rows_micro, slots, width), jnp.float32)
        value_grad = jnp.zeros((rows_micro, slots, width), jnp.float32)
        for step in range(blocks):
            query_part, key_part, value_part = attention_back(
                query, out_grad, ids_query, log_total, inner, visiting
            )
            query_grad = query_grad + query_part
            key_grad, value_grad = (
                from_behind((key_grad + key_part).astype(jnp.bfloat16), "blk", 1).astype(
                    jnp.float32
                ),
                from_behind((value_grad + value_part).astype(jnp.bfloat16), "blk", 1).astype(
                    jnp.float32
                ),
            )
            if step + 1 < blocks:
                visiting = from_behind((visiting[0], visiting[1], visiting[2]), "blk", 1)
        joined_grad = (
            jnp.concatenate([query_grad, key_grad, value_grad], axis=-1)
            .astype(jnp.bfloat16)
            .reshape(count, 3 * width)
        )
        sums[2] = sums[2] + jnp.dot(normed.T, joined_grad, preferred_element_type=jnp.float32)
        joined_sums = jnp.sum(joined_grad.astype(jnp.float32), axis=0)
        sums[3] = sums[3] + jnp.stack([joined_sums[:width], joined_sums[2 * width :]])
        first_in_grad = jnp.dot(joined_grad, input_weight.T, preferred_element_type=jnp.float32)
        rows_part, first_gain_part, first_shift_part = jax.vjp(
            norm_rows, rows_in, first_gain, first_shift
        )[1](first_in_grad)
        sums[0] = sums[0] + first_gain_part
        sums[1] = sums[1] + first_shift_part
        input_grads.append(
            (rows_part + middle_grad).astype(jnp.bfloat16).reshape(rows_micro, slots, width)
        )
    totals = lax.psum(
        (
            sums[0],
            sums[1],
            sums[2],
            sums[3],
            sums[4],
            sums[5],
            sums[6],
            sums[7],
            sums[8],
            sums[9],
            sums[10],
            sums[11],
        ),
        ("rows", "blk"),
    )
    return (
        jnp.concatenate(results, axis=0),
        jnp.concatenate(input_grads, axis=0),
        totals[0],
        totals[1],
        totals[2],
        totals[3],
        totals[4],
        totals[5],
        totals[6],
        totals[7],
        totals[8],
        totals[9],
        totals[10],
        totals[11],
    )


def swap(value, axis, bit):
    return lax.ppermute(value, axis, [(i, i ^ bit) for i in range(lax.axis_size(axis))])


def side(axis, bit):
    return (lax.axis_index(axis) // bit) % 2


def after(value, *others):
    return lax.optimization_barrier((value, *others))[0]


def axis_bits(axis):
    bits, bit = [], 1
    while bit < lax.axis_size(axis):
        bits.append((axis, bit))
        bit *= 2
    return bits


def add_low(a, b):
    return (a.astype(F32) + b.astype(F32)).astype(BF16)


def swap_two(value, step):
    rows, blocks = lax.axis_size("rows"), lax.axis_size("blk")
    pairs = []
    for r in range(rows):
        for b in range(blocks):
            axis, bit = step[b % 2]
            other = (r ^ bit, b) if axis == "rows" else (r, b ^ bit)
            pairs.append((r * blocks + b, other[0] * blocks + other[1]))
    return lax.ppermute(value, ("rows", "blk"), pairs)


def side_two(step):
    return jnp.where(side("blk", 1) == 0, side(*step[0]), side(*step[1]))


class Order:
    def __init__(self):
        self.last = ()

    def hold(self, value):
        return after(value, *self.last) if self.last else value

    def advance(self, *parts):
        parts = [part for part in parts if part.result is None]
        if parts:
            held = lax.optimization_barrier(([part.recv for part in parts], self.last))[0]
            self.done(*[value for part, recv in zip(parts, held) for value in part.step(recv)])

    def done(self, *values):
        self.last = values
        return values[0] if len(values) == 1 else values


class Chain:
    def __init__(self, steps, send, keep):
        self.steps, self.at = steps, -1
        self.recv, self.keep, self.result = send, keep, None

    def step(self, recv):
        keep, n = self.keep, len(self.steps)
        if self.at < 0:
            send, self.recv = recv, swap(recv, "blk", 1)
        elif self.at < n:
            step = self.steps[self.at]
            half = keep.shape[0] // 2
            own = side_two(step)

            def part(which):
                return add_low(
                    lax.dynamic_slice_in_dim(keep, which * half, half, 0),
                    lax.dynamic_slice_in_dim(recv, which * half, half, 0),
                )

            send, self.keep = part(1 - own), part(own)
            self.recv = swap_two(send, step)
        elif self.at < 2 * n:
            send = add_low(keep, recv) if self.at == n else jnp.concatenate([keep, recv], axis=0)
            send = self.keep = lax.optimization_barrier(send)
            self.recv = swap_two(send, self.steps[2 * n - 1 - self.at])
        elif self.at == 2 * n:
            self.at, self.keep, self.recv = self.at + 1, (keep, recv), [swap(piece, "blk", 1) for piece in (keep, recv)]
            return keep, recv
        else:
            self.result, self.recv = (*keep, *recv), None
            return ()
        self.at += 1
        return send, self.keep


class Small:
    def __init__(self, value):
        count = lax.axis_size("rows") * lax.axis_size("blk")
        self.recv, self.result, self.sent = jnp.broadcast_to(value[None], (count, *value.shape)), None, False

    def step(self, recv):
        if not self.sent:
            self.recv, self.sent = lax.all_to_all(recv, ("rows", "blk"), 0, 0), True
            return (recv,)
        self.result, self.recv = jnp.sum(recv, axis=0), None
        return (self.result,)


class Home:
    def __init__(self, pieces):
        self.recv, self.result, self.sent = pieces, None, False

    def step(self, recv):
        if not self.sent:
            self.recv, self.sent = lax.all_to_all(recv, "blk", 0, 0), True
        else:
            self.result, self.recv = recv, None
        return (recv,)


def block_turns(steps):
    core = side("blk", 1)
    turns = []
    for c in range(2):
        turn = 0
        for step in steps:
            turn = turn * 2 + side(*step[c])
        turns.append(turn)
    first, second = jnp.where(core == 0, turns[0], turns[1]), jnp.where(core == 0, turns[1], turns[0])
    return core.astype(jnp.int32).reshape(1), jnp.stack([first, second]).astype(jnp.int32), 1 << len(steps)


def local_rows(
    inputs,
    image_index,
    keep_mask,
    first_gain,
    first_shift,
    input_weight,
    input_bias,
    output_weight,
    output_bias,
    second_gain,
    second_shift,
    up_weight,
    up_bias,
    down_weight,
    down_bias,
    cotangent,
):
    blocks, span, width = inputs.shape
    ff = up_weight.shape[1]
    me = lax.axis_index("blk")

    def row_piece(array, s):
        return lax.dynamic_index_in_dim(array, me ^ s, 0, keepdims=False)

    xs_send = [row_piece(inputs, s) for s in range(blocks)]
    xs_in = xs_send[:1] + [swap(xs_send[s], "blk", s) for s in range(1, blocks)]
    ids = [row_piece(image_index, 0)] + [
        swap(row_piece(after(image_index, *xs_send), s), "blk", s) for s in range(1, blocks)
    ]
    cots = [row_piece(cotangent, 0)] + [
        swap(after(row_piece(cotangent, s), *xs_in), "blk", s) for s in range(1, blocks)
    ]
    ids = jnp.concatenate(ids)
    image = jnp.where(ids < 0, 4, ids)
    order_key = image * ids.shape[0] + jnp.arange(ids.shape[0], dtype=jnp.int32)
    less = (order_key[None, :] < order_key[:, None]).astype(jnp.int32)
    rank = jnp.sum(less, axis=1)
    starts = jnp.sum((image[None, :] < jnp.arange(6, dtype=jnp.int32)[:, None]).astype(jnp.int32), axis=1)
    keep = lax.dynamic_index_in_dim(keep_mask, me, 0, keepdims=False).astype(F32) / keep_rate
    rank_row, rank_col = rank[None, :], rank[:, None]

    bias = jnp.stack([input_bias[0], jnp.zeros_like(input_bias[0]), input_bias[1]])
    xs, normed, qkv = qkv_call(rank_row, xs_in, first_gain[None], first_shift[None], input_weight, bias)
    attended, stat = forward_call(starts, qkv)
    vectors = jnp.stack([output_bias, second_gain, second_shift, down_bias])
    core = side("blk", 1).astype(jnp.int32).reshape(1)
    cot, att_low, middle, normed2, mlp_grad, sums_mid = middle_call(
        keep, rank_row, cots, attended, xs, output_weight, vectors
    )
    (up_send, up_keep, down_send, down_keep, up_sums, result, middle_grad, branch, att_grad, sums2) = mlp_call(
        core, keep, normed2, mlp_grad, middle, cot, att_low, output_weight, vectors, up_weight, up_bias[None], down_weight
    )

    y, x, z = axis_bits("blk")[1], axis_bits("rows")[0], axis_bits("rows")[1:]
    far = [(d, d) for d in z[1:]]
    xy = [(x, y), (y, x), (z[0], z[0])] + far
    zx = [(z[0], z[0]), (x, y), (y, x)] + far
    order = Order()
    order.done(att_grad)
    up_chain, down_chain = Chain(zx, up_send, up_keep), Chain(xy, down_send, down_keep)

    order.advance(down_chain, up_chain)
    result_home = Home(order.done(unsort_call(me.reshape(1), rank_col, blocks, order.hold(result))))
    order.advance(down_chain, up_chain, result_home)
    grads, bias_sums = backward_call(starts, qkv, order.hold(att_grad), attended, stat, 0, PAIRS)
    order.done(grads)
    order.advance(down_chain, up_chain, result_home)
    input_chain = Chain(
        xy, *order.done(*input_weights_call(core, order.hold(normed), grads, bias_sums, sums2, sums_mid, up_sums))
    )
    order.advance(down_chain, up_chain, input_chain)
    inputs_grad, sums1 = order.done(*input_call(grads, input_weight, xs, order.hold(middle_grad), first_gain[None]))
    small = Small(sums1[:2])
    order.advance(down_chain, up_chain, input_chain, small)
    home = Home(order.done(unsort_call(me.reshape(1), rank_col, blocks, order.hold(inputs_grad))))
    order.advance(down_chain, up_chain, input_chain, small, home)
    order.advance(down_chain, up_chain, input_chain)
    order.advance(down_chain, up_chain, input_chain, home)
    while down_chain.at < 2 * len(xy):
        order.advance(down_chain, up_chain, input_chain)
    result_out = order.done(copy_call(order.hold(result_home.result)))
    inputs_out = order.done(copy_call(order.hold(home.result)))
    order.advance(down_chain, up_chain, input_chain)
    order.advance(down_chain, up_chain, input_chain)
    up_total = order.done(up_final(*block_turns(zx), (order.hold(up_chain.result[0]), *up_chain.result[1:])))
    order.advance(input_chain)
    down_total, out_total = order.done(
        *down_final(*block_turns(xy), (order.hold(down_chain.result[0]), *down_chain.result[1:]), ff)
    )
    while input_chain.result is None:
        order.advance(input_chain)
    input_total, sums = input_final(*block_turns(xy), input_chain.result)
    sums = jnp.concatenate([small.result, sums[:, :16].T])

    return (
        result_out,
        inputs_out,
        sums[0],
        sums[1],
        input_total,
        jnp.stack([sums[2], sums[4]]),
        out_total,
        sums[7],
        sums[5],
        sums[6],
        up_total,
        sums[9:13].reshape(ff),
        down_total,
        sums[8],
    )


def solution(mesh):
    blocks, groups = mesh.shape["blk"], mesh.shape["rows"]

    def run(*args):
        whole_rows = args[0].shape[0] // groups == blocks == 4 and groups in (4, 8, 16)
        return jax.shard_map(
            local_rows if whole_rows else local,
            mesh=mesh,
            in_specs=(P("rows", "blk", None), P("rows", "blk"), P("rows", None)) + (P(),) * 12 + (P("rows", "blk", None),),
            out_specs=(P("rows", "blk", None),) * 2 + (P(),) * 12,
            check_vma=False,
        )(*args)

    return run
```

```python
import functools

import jax
import jax.numpy as jnp
from jax import lax
from jax.experimental import pallas as pl
from jax.experimental.pallas import tpu as pltpu
from jax.sharding import PartitionSpec as P

HEADS = 12
HEAD_DIM = 64
PAIR = 2 * HEAD_DIM
PAIRS = HEADS // 2
eps_norm = 1e-06
keep_rate = 0.9
F32 = jnp.float32
BF16 = jnp.bfloat16
NEG = -1e30
VMEM = 62 * 1024 * 1024
QUICK = pl.CostEstimate(flops=1 << 20, bytes_accessed=1 << 16, transcendentals=0)


def dot(a, b):
    return jnp.dot(a, b, preferred_element_type=F32)


def dot_nt(a, b):
    return lax.dot_general(a, b, (((1,), (1,)), ((), ())), preferred_element_type=F32)


def dot_tn(a, b):
    return lax.dot_general(a, b, (((0,), (0,)), ((), ())), preferred_element_type=F32)


def whole(shape):
    return pl.BlockSpec(shape, lambda *g: (0,) * len(shape), pipeline_mode=pl.Buffered(1))


def centre_scale(values):
    centre = values - jnp.mean(values, axis=-1, keepdims=True)
    spread = jnp.mean(centre * centre, axis=-1, keepdims=True)
    inv = lax.rsqrt(spread + eps_norm)
    return centre * inv, inv


def norm_back(grad_hat, hat, inv):
    first = jnp.mean(grad_hat, axis=-1, keepdims=True)
    second = jnp.mean(grad_hat * hat, axis=-1, keepdims=True)
    return (grad_hat - first - hat * second) * inv


def gather_pieces(step, pieces, row):
    @pl.when(step == 0)
    def _():
        span = pieces[0].shape[0]
        for i, piece in enumerate(pieces):
            row[i * span : (i + 1) * span, :] = piece[...]


def sort_tile(rank_row, tile, step, row):
    place = step * tile + lax.broadcasted_iota(jnp.int32, (tile, row.shape[0]), 0)
    return dot((rank_row == place).astype(BF16), row[...])


def qkv_kernel(n, tile, *refs):
    rank, *pieces = refs[: n + 1]
    gain, shift, weight, bias, xs_out, normed_out, qkv_out, row = refs[n + 1 :]
    gather_pieces(pl.program_id(0), pieces, row)
    xs = sort_tile(rank[...], tile, pl.program_id(0), row)
    xs_out[...] = xs.astype(BF16)
    hat, _ = centre_scale(xs)
    normed = (hat * gain[...] + shift[...]).astype(BF16)
    normed_out[...] = normed
    width = normed.shape[1]
    for j in range(3):
        cols = slice(j * width, (j + 1) * width)
        mixed = (dot(normed, weight[:, cols]) + bias[j : j + 1, :]).astype(BF16)
        qkv_out[j] = mixed * BF16(HEAD_DIM**-0.5) if j == 0 else mixed


def qkv_call(rank, pieces, gain, shift, weight, bias, tile=288):
    n = len(pieces)
    span, width = pieces[0].shape
    count = n * span
    return pl.pallas_call(
        functools.partial(qkv_kernel, n, tile),
        grid=(count // tile,),
        in_specs=[whole((1, count))]
        + [whole((span, width))] * n
        + [whole((1, width)), whole((1, width)), whole(weight.shape), whole(bias.shape)],
        out_specs=[
            pl.BlockSpec((tile, width), lambda i: (i, 0)),
            pl.BlockSpec((tile, width), lambda i: (i, 0)),
            pl.BlockSpec((3, tile, width), lambda i: (0, i, 0)),
        ],
        out_shape=[
            jax.ShapeDtypeStruct((count, width), BF16),
            jax.ShapeDtypeStruct((count, width), BF16),
            jax.ShapeDtypeStruct((3, count, width), BF16),
        ],
        scratch_shapes=[pltpu.VMEM((count, width), BF16)],
        compiler_params=pltpu.CompilerParams(vmem_limit_bytes=VMEM),
        cost_estimate=QUICK,
        name="sort_qkv",
    )(rank, *pieces, gain, shift, weight, bias)


SMALL = 304
LARGE = 384


def windows(starts, seg, length):
    first, last = starts[seg], starts[seg + 1]
    aligned = first // 16 * 16
    small = SMALL if seg < 4 else LARGE
    at_small = pl.multiple_of(jnp.minimum(aligned, length - small), 16)
    at_large = pl.multiple_of(jnp.minimum(aligned, length - LARGE), 16)
    return first, last, small, at_small, at_large


def inside(at, size, lanes, first, last):
    place = at + lax.broadcasted_iota(jnp.int32, (size, lanes), 0)
    return (place >= first) & (place < last)


def forward_kernel(starts, qkv, out, stat, low_out):
    length = qkv.shape[1]
    for seg in range(5):
        first, last, small, at_q, at_k = windows(starts, seg, length)
        rows_q = pl.ds(at_q, small)
        q = qkv[0, rows_q, :]
        k = qkv[1, pl.ds(at_k, LARGE), :]
        v = qkv[2, pl.ds(at_k, LARGE), :]
        lane = lax.broadcasted_iota(jnp.int32, (LARGE, PAIR), 1)
        lane_q = lax.broadcasted_iota(jnp.int32, (small, PAIR), 1)
        low = lane < HEAD_DIM
        seen = inside(at_k, LARGE, PAIR, first, last)
        zero = jnp.zeros((LARGE, PAIR), BF16)
        one = jnp.ones((LARGE, PAIR), BF16)
        bias = jnp.where((lane == 0) & ~seen, NEG, 0.0).astype(BF16)
        q_ext = jnp.concatenate([q, (lane_q == 0).astype(BF16)], axis=1)
        halves = (low, ~low)
        k_ext = [jnp.concatenate([jnp.where(half, k, zero), bias], axis=1) for half in halves]
        mixes = [
            jnp.concatenate([jnp.where(half, v, zero), jnp.where(half, one, zero)], axis=1) for half in halves
        ]
        pair = dot_nt(q_ext, jnp.concatenate(k_ext, axis=0))
        tops, weights = [], []
        for h in range(2):
            scores = pair[:, h * LARGE : (h + 1) * LARGE]
            top = jnp.max(scores, axis=-1, keepdims=True)
            tops.append(top)
            weights.append(jnp.exp(scores - top).astype(BF16))
        both = dot(jnp.concatenate(weights, axis=1), jnp.concatenate(mixes, axis=0))
        total = both[:, PAIR:]
        peak = jnp.where(lane_q < HEAD_DIM, tops[0], tops[1])
        mine = inside(at_q, small, PAIR, first, last)
        out[rows_q, :] = jnp.where(mine, both[:, :PAIR] / total, out[rows_q, :])
        stat[rows_q, :] = jnp.where(mine, peak + jnp.log(total), stat[rows_q, :])
    low_out[...] = out[...].astype(BF16)


def forward_call(starts, qkv):
    _, count, wide = qkv.shape
    pairs = wide // PAIR
    return pl.pallas_call(
        forward_kernel,
        grid_spec=pltpu.PrefetchScalarGridSpec(
            num_scalar_prefetch=1,
            grid=(pairs,),
            in_specs=[pl.BlockSpec((3, count, PAIR), lambda p, s: (0, 0, p))],
            out_specs=[pl.BlockSpec((count, PAIR), lambda p, s: (0, p))] * 3,
        ),
        out_shape=[jax.ShapeDtypeStruct((count, pairs * PAIR), dtype) for dtype in (F32, F32, BF16)],
        compiler_params=pltpu.CompilerParams(vmem_limit_bytes=VMEM),
        cost_estimate=QUICK,
        name="attention_forward",
    )(starts, qkv)


def split3(value):
    high = value.astype(BF16)
    rest = value - high.astype(F32)
    mid = rest.astype(BF16)
    return high, mid, (rest - mid.astype(F32)).astype(BF16)


def backward_kernel(starts, qkv, grad, att, stat, *refs):
    out, sums = refs[-2:]
    length = qkv.shape[1]
    third = lax.broadcasted_iota(jnp.int32, (PAIR, PAIR), 0) // HEAD_DIM
    block = (third == lax.broadcasted_iota(jnp.int32, (PAIR, PAIR), 1) // HEAD_DIM).astype(BF16)
    for seg in range(5):
        first, last, small, at_k, at_q = windows(starts, seg, length)
        rows_q, rows_k = pl.ds(at_q, LARGE), pl.ds(at_k, small)
        lane_q = lax.broadcasted_iota(jnp.int32, (LARGE, PAIR), 1)
        lane_k = lax.broadcasted_iota(jnp.int32, (small, PAIR), 1)
        spot_q, spot_k = lane_q % HEAD_DIM, lane_k % HEAD_DIM
        mine_q = inside(at_q, LARGE, PAIR, first, last)
        mine_k = inside(at_k, small, PAIR, first, last)
        zero_q = jnp.zeros((LARGE, PAIR), BF16)
        zero_k = jnp.zeros((small, PAIR), BF16)
        q = qkv[0, rows_q, :]
        k = jnp.where(mine_k, qkv[1, rows_k, :], zero_k)
        v = qkv[2, rows_k, :]
        g = jnp.where(mine_q, grad[rows_q, :], zero_q)
        prod = g.astype(F32) * jnp.where(mine_q, att[rows_q, :], 0.0)
        p_high = prod.astype(BF16)
        p_low = (prod - p_high.astype(F32)).astype(BF16)
        inner = dot(p_high, block) + dot(p_low, block)
        logs = jnp.where(mine_q, stat[rows_q, :], 0.0)

        def spread(value, fifth):
            a, b, c = split3(value)
            return jnp.where(
                spot_q == 0, a, jnp.where(spot_q == 1, b, jnp.where(spot_q == 2, c, fifth))
            )

        query_bias = jnp.where(mine_q, 0.0, NEG).astype(BF16)
        unit = jnp.ones((LARGE, PAIR), BF16)
        q_tail = spread(logs, jnp.where(spot_q == 3, unit, jnp.where(spot_q == 4, query_bias, zero_q)))
        g_tail = spread(inner, zero_q)
        key_bias = jnp.where(mine_k, 0.0, NEG).astype(BF16)
        minus = jnp.where(spot_k < 3, -1.0, 0.0).astype(BF16)
        k_tail = jnp.where(
            spot_k == 3, key_bias, jnp.where(spot_k == 4, jnp.ones((small, PAIR), BF16), minus)
        )
        heads_q = [lane_q // HEAD_DIM == h for h in range(2)]
        qs = [jnp.where(head, q, zero_q) for head in heads_q]
        gs = [jnp.where(head, g, zero_q) for head in heads_q]
        q_both = [jnp.concatenate([x, jnp.where(head, q_tail, zero_q)], axis=1) for x, head in zip(qs, heads_q)]
        g_both = [jnp.concatenate([x, jnp.where(head, g_tail, zero_q)], axis=1) for x, head in zip(gs, heads_q)]
        prob = jnp.exp(dot_nt(jnp.concatenate([k, k_tail], axis=1), jnp.concatenate(q_both, axis=0)))
        prob_grad = dot_nt(jnp.concatenate([v, minus], axis=1), jnp.concatenate(g_both, axis=0))
        score_grad = (prob * prob_grad).astype(BF16)
        value_grad = dot(prob.astype(BF16), jnp.concatenate(gs, axis=0))
        key_grad = dot(score_grad, jnp.concatenate(qs, axis=0))
        stacked = jnp.concatenate([score_grad[:, :LARGE], score_grad[:, LARGE:]], axis=0)
        ks = [jnp.where(lane_k // HEAD_DIM == h, k, zero_k) for h in range(2)]
        query_grad = dot_tn(stacked, jnp.concatenate(ks, axis=0))
        query_grad = (query_grad * HEAD_DIM**-0.5).astype(BF16)
        out[0, rows_q, :] = jnp.where(mine_q, query_grad, out[0, rows_q, :])
        out[1, rows_k, :] = jnp.where(mine_k, key_grad.astype(BF16), out[1, rows_k, :])
        out[2, rows_k, :] = jnp.where(mine_k, value_grad.astype(BF16), out[2, rows_k, :])
    for j in range(3):
        sums[j : j + 1, :] = jnp.sum(out[j].astype(F32), axis=0, keepdims=True)


def backward_call(starts, qkv, grad, att, stat, first_pair, pairs, before=None):
    _, count, width = qkv.shape
    held = [] if before is None else list(before)
    return pl.pallas_call(
        backward_kernel,
        grid_spec=pltpu.PrefetchScalarGridSpec(
            num_scalar_prefetch=1,
            grid=(pairs,),
            in_specs=[pl.BlockSpec((3, count, PAIR), lambda p, s: (0, 0, p + first_pair))]
            + [pl.BlockSpec((count, PAIR), lambda p, s: (0, p + first_pair))] * 3
            + [pl.BlockSpec(memory_space=pl.ANY)] * len(held),
            out_specs=[
                pl.BlockSpec((3, count, PAIR), lambda p, s: (0, 0, p + first_pair)),
                pl.BlockSpec((8, PAIR), lambda p, s: (0, p + first_pair)),
            ],
        ),
        out_shape=[
            jax.ShapeDtypeStruct((3, count, width), BF16),
            jax.ShapeDtypeStruct((8, width), F32),
        ],
        input_output_aliases={5: 0, 6: 1} if held else {},
        compiler_params=pltpu.CompilerParams(vmem_limit_bytes=VMEM),
        cost_estimate=QUICK,
        name="attention_backward",
    )(starts, qkv, grad, att, stat, *held)


HALF_ERF = tuple(0.5 * c for c in (0.254829592, -0.284496736, 1.421413741, -1.453152027, 1.061405429))
LOG2_E = 1.4426950408889634


def gelu_pair(u):
    size = jnp.abs(u)
    t = 1.0 / (1.0 + (0.3275911 * 0.5**0.5) * size)
    bell = jnp.exp2(u * u * (-0.5 * LOG2_E))
    poly = HALF_ERF[4] * t + HALF_ERF[3]
    for c in (HALF_ERF[2], HALF_ERF[1], HALF_ERF[0]):
        poly = poly * t + c
    tail = poly * t * bell
    phi = jnp.where(u < 0, tail, 1.0 - tail)
    return u * phi, phi + u * bell * 0.3989422804014327


def middle_kernel(n, tile, *refs):
    keep, rank, *pieces = refs[: n + 2]
    att, xs, out_w, vectors, cot_out, middle_out, normed_out, mlp_out, sums, row = refs[n + 2 :]
    step = pl.program_id(0)
    gather_pieces(step, pieces, row)
    cot = sort_tile(rank[...], tile, step, row)
    cot_out[...] = cot.astype(BF16)
    mlp_grad = (cot * keep[1]).astype(BF16)
    mlp_out[...] = mlp_grad
    middle = xs[...].astype(F32) + keep[0] * (dot(att[...], out_w[...]) + vectors[0:1, :])
    middle_out[...] = middle
    hat, _ = centre_scale(middle)
    normed_out[...] = (hat * vectors[1:2, :] + vectors[2:3, :]).astype(BF16)

    @pl.when(step == 0)
    def _():
        sums[...] = jnp.zeros_like(sums)

    sums[0:1, :] += jnp.sum(mlp_grad.astype(F32), axis=0, keepdims=True)


def middle_call(keep, rank, pieces, att, xs, out_w, vectors, tile=384):
    n = len(pieces)
    span, width = pieces[0].shape
    count = n * span
    rows = pl.BlockSpec((tile, width), lambda i: (i, 0))
    low, full = jax.ShapeDtypeStruct((count, width), BF16), jax.ShapeDtypeStruct((count, width), F32)
    return pl.pallas_call(
        functools.partial(middle_kernel, n, tile),
        grid=(count // tile,),
        in_specs=[pl.BlockSpec(memory_space=pltpu.SMEM), whole((1, count))]
        + [whole((span, width))] * n
        + [rows, rows, whole(out_w.shape), whole(vectors.shape)],
        out_specs=[rows] * 4 + [pl.BlockSpec((8, width), lambda i: (0, 0))],
        out_shape=[low, full, low, low, jax.ShapeDtypeStruct((8, width), F32)],
        scratch_shapes=[pltpu.VMEM((count, width), BF16)],
        compiler_params=pltpu.CompilerParams(vmem_limit_bytes=VMEM),
        cost_estimate=QUICK,
        name="middle",
    )(keep, rank, *pieces, att, xs, out_w, vectors)


def mlp_kernel(parts, core, keep, normed, mlp_grad, middle, cot, att, out_w, vectors, up_w, up_b, down_w, *refs):
    (
        up_send, up_keep, down_send, down_keep, up_sums, result, middle_grad_out, branch_out, att_grad_out, sums,
        lift, back, act_all, hidden_all,
    ) = refs
    step, half = pl.program_id(0), pl.num_programs(0) // 2
    count, width = normed.shape
    cuts = [slice(i * (count // parts), (i + 1) * (count // parts)) for i in range(parts)]

    @pl.when(step == 0)
    def _():
        lift[...] = jnp.zeros_like(lift)
        back[...] = jnp.zeros_like(back)

    @pl.when(step < 2 * half)
    def _():
        total = jnp.zeros(up_sums.shape, F32)
        ready = None
        for rows in cuts + [None]:
            fresh = None
            if rows is not None:
                u = dot(normed[rows, :], up_w[...]) + up_b[...]
                fresh = (rows, u, dot_nt(mlp_grad[rows, :], down_w[...]))
            if ready is not None:
                past, u, act_grad = ready
                act, slope = gelu_pair(u)
                act_all[past, :] = act.astype(BF16)
                hidden = (act_grad * slope).astype(BF16)
                hidden_all[past, :] = hidden
                total = total + jnp.sum(hidden.astype(F32), axis=0, keepdims=True)
            ready = fresh
        lift[...] += dot(act_all[...], down_w[...])
        back[...] += dot_nt(hidden_all[...], up_w[...])
        up_sums[...] = total
        up_part = dot_tn(normed[...], hidden_all[...]).astype(BF16)
        down_part = dot_tn(act_all[...], mlp_grad[...]).astype(BF16)

        @pl.when(step < half)
        def _():
            up_send[...] = up_part
            down_send[...] = down_part

        @pl.when(step >= half)
        def _():
            up_keep[...] = up_part
            down_keep[...] = down_part

    @pl.when(step == 2 * half)
    def _():
        gain, down_b = vectors[1:2, :], vectors[3:4, :]
        sums[...] = jnp.zeros_like(sums)
        for rows in cuts:
            mid, grad = middle[rows, :], back[rows, :]
            hat, inv = centre_scale(mid)
            result[rows, :] = (mid + keep[1] * (lift[rows, :] + down_b)).astype(BF16)
            middle_grad = cot[rows, :].astype(F32) + norm_back(grad * gain, hat, inv)
            middle_grad_out[rows, :] = middle_grad
            branch = (keep[0] * middle_grad).astype(BF16)
            branch_out[rows, :] = branch
            att_grad_out[rows, :] = dot_nt(branch, out_w[...]).astype(BF16)
            sums[0:1, :] += jnp.sum(grad * hat, axis=0, keepdims=True)
            sums[1:2, :] += jnp.sum(grad, axis=0, keepdims=True)
            sums[2:3, :] += jnp.sum(branch.astype(F32), axis=0, keepdims=True)
        for out, c in ((down_send, 1 - core[0]), (down_keep, core[0])):
            cols = pl.ds(pl.multiple_of(c * (width // 2), 128), width // 2)
            out[: width // 2, :] = dot_tn(att[:, cols], branch_out[...]).astype(BF16)
            out[width // 2 :, :] = jnp.zeros((out.shape[0] - width // 2, width), BF16)


def mlp_call(core, keep, normed, mlp_grad, middle, cot, att, out_w, vectors, up_w, up_b, down_w, chunk=512, parts=4):
    count, width = normed.shape
    ff = up_w.shape[1]
    half = ff // 2 // chunk

    def place(i, c):
        i = jnp.minimum(i, 2 * half - 1)
        return jnp.where(i < half, (1 - c[0]) * half + i, c[0] * half + i - half)

    def first(i):
        return jnp.minimum(i, half - 1)

    def second(i):
        return jnp.clip(i - half, 0, half - 1)

    def extra(i, index):
        return jnp.where(i == 2 * half, half, index)

    low, full = jax.ShapeDtypeStruct((count, width), BF16), jax.ShapeDtypeStruct((count, width), F32)
    return pl.pallas_call(
        functools.partial(mlp_kernel, parts),
        grid_spec=pltpu.PrefetchScalarGridSpec(
            num_scalar_prefetch=1,
            grid=(2 * half + 1,),
            in_specs=[pl.BlockSpec(memory_space=pltpu.SMEM)]
            + [whole((count, width))] * 5
            + [
                whole(out_w.shape),
                whole(vectors.shape),
                pl.BlockSpec((width, chunk), lambda i, c: (0, place(i, c))),
                pl.BlockSpec((1, chunk), lambda i, c: (0, place(i, c))),
                pl.BlockSpec((chunk, width), lambda i, c: (place(i, c), 0)),
            ],
            out_specs=[
                pl.BlockSpec((width, chunk), lambda i, c: (0, first(i))),
                pl.BlockSpec((width, chunk), lambda i, c: (0, second(i))),
                pl.BlockSpec((chunk, width), lambda i, c: (extra(i, first(i)), 0)),
                pl.BlockSpec((chunk, width), lambda i, c: (extra(i, second(i)), 0)),
                pl.BlockSpec((1, chunk), lambda i, c: (0, place(i, c))),
            ]
            + [whole((count, width))] * 4
            + [whole((8, width))],
            scratch_shapes=[pltpu.VMEM((count, width), F32)] * 2 + [pltpu.VMEM((count, chunk), BF16)] * 2,
        ),
        out_shape=[jax.ShapeDtypeStruct((width, ff // 2), BF16)] * 2
        + [jax.ShapeDtypeStruct((ff // 2 + chunk, width), BF16)] * 2
        + [jax.ShapeDtypeStruct((1, ff), F32), low, full, low, low, jax.ShapeDtypeStruct((8, width), F32)],
        compiler_params=pltpu.CompilerParams(vmem_limit_bytes=VMEM),
        cost_estimate=QUICK,
        name="mlp",
    )(core, keep, normed, mlp_grad, middle, cot, att, out_w, vectors, up_w, up_b, down_w)


def input_kernel(grads, weight, xs, middle_grad, gain, out, sums):
    span = xs.shape[1]
    back = None
    for j in range(3):
        part = dot_nt(grads[j], weight[:, j * span : (j + 1) * span])
        back = part if back is None else back + part
    hat, inv = centre_scale(xs[...].astype(F32))
    out[...] = (middle_grad[...] + norm_back(back * gain[...], hat, inv)).astype(BF16)

    @pl.when(pl.program_id(0) == 0)
    def _():
        sums[...] = jnp.zeros_like(sums)

    sums[0:1, :] += jnp.sum(back * hat, axis=0, keepdims=True)
    sums[1:2, :] += jnp.sum(back, axis=0, keepdims=True)


def input_call(grads, weight, xs, middle_grad, gain, tile=288):
    count, width = xs.shape
    return pl.pallas_call(
        input_kernel,
        grid=(count // tile,),
        in_specs=[pl.BlockSpec((3, tile, width), lambda i: (0, i, 0))]
        + [
            whole(weight.shape),
            pl.BlockSpec((tile, width), lambda i: (i, 0)),
            pl.BlockSpec((tile, width), lambda i: (i, 0)),
            whole((1, width)),
        ],
        out_specs=[pl.BlockSpec((tile, width), lambda i: (i, 0)), pl.BlockSpec((8, width), lambda i: (0, 0))],
        out_shape=[jax.ShapeDtypeStruct((count, width), BF16), jax.ShapeDtypeStruct((8, width), F32)],
        compiler_params=pltpu.CompilerParams(vmem_limit_bytes=VMEM),
        cost_estimate=QUICK,
        name="input_backward",
    )(grads, weight, xs, middle_grad, gain)


def unsort_kernel(me, rank, source, out):
    count, span = source.shape[0], rank.shape[0]
    place = lax.broadcasted_iota(jnp.int32, (span, count), 1)
    out[0] = dot((rank[...] == place).astype(BF16), source[...]).astype(BF16)


def unsort_call(me, rank_col, n, array):
    count, width = array.shape
    span = count // n
    return pl.pallas_call(
        unsort_kernel,
        grid_spec=pltpu.PrefetchScalarGridSpec(
            num_scalar_prefetch=1,
            grid=(n,),
            in_specs=[pl.BlockSpec((span, 1), lambda i, m: (i, 0)), whole((count, width))],
            out_specs=pl.BlockSpec((1, span, width), lambda i, m: (m[0] ^ i, 0, 0)),
        ),
        out_shape=jax.ShapeDtypeStruct((n, span, width), BF16),
        compiler_params=pltpu.CompilerParams(vmem_limit_bytes=VMEM),
        cost_estimate=QUICK,
        name="unsort",
    )(me, rank_col, array)


VECTORS = 128


def input_weights_kernel(core, normed, grads, first, second, third, up_sums, send, keep):
    mid, width = normed.shape[1], grads.shape[2]
    h = core[0] ^ 1 ^ pl.program_id(0)

    def write(out):
        for j in range(3):
            out[:, j * width : (j + 1) * width] = dot_tn(normed[...], grads[j]).astype(BF16)
        rows = [first[0:3, :], second[0:3, :], third[0:1, :]]
        for i in range(up_sums.shape[1] // width):
            rows.append(up_sums[:, pl.ds(pl.multiple_of(i * width + h * mid, 128), mid)])
        count = sum(row.shape[0] for row in rows)
        rows.append(jnp.zeros((VECTORS - count, mid), F32))
        out[:, 3 * width :] = jnp.concatenate(rows, axis=0).T.astype(BF16)

    pl.when(pl.program_id(0) == 0)(lambda: write(send))
    pl.when(pl.program_id(0) == 1)(lambda: write(keep))


def input_weights_call(core, normed, grads, first, second, third, up_sums):
    count, width = normed.shape
    half = jax.ShapeDtypeStruct((width // 2, 3 * width + VECTORS), BF16)
    rows = pl.BlockSpec((count, width // 2), lambda i, c: (0, c[0] ^ 1 ^ i))
    vector = pl.BlockSpec((8, width // 2), lambda i, c: (0, c[0] ^ 1 ^ i))
    return pl.pallas_call(
        input_weights_kernel,
        grid_spec=pltpu.PrefetchScalarGridSpec(
            num_scalar_prefetch=1,
            grid=(2,),
            in_specs=[rows, whole(grads.shape), vector, vector, vector, whole(up_sums.shape)],
            out_specs=[whole(half.shape)] * 2,
        ),
        out_shape=[half] * 2,
        compiler_params=pltpu.CompilerParams(vmem_limit_bytes=VMEM),
        cost_estimate=QUICK,
        name="input_weights",
    )(core, normed, grads, first, second, third, up_sums)


GROUPS = 4


def final_call(core, turns, blocks, groups, pieces, name, spread, outs):
    size = blocks // groups
    rows = pieces[0].shape[0] // (blocks // 2)
    whole_tile = 1 if rows % 16 == 0 else 2

    def kernel(c, t, *refs):
        h, g = pl.program_id(0), pl.program_id(1)
        active = (h * groups + g) // (groups // 2)
        turn = t[h]
        place = g ^ (turn // size)

        def write(source):
            for j in range(0, size, whole_tile):
                part = source[j * rows : (j + whole_tile) * rows, :].astype(F32)
                for i in range(whole_tile):
                    spread(part[i * rows : (i + 1) * rows], (j + i) ^ (turn % size), place, refs[4:])

        for q in range(4):
            pl.when(active == q)(functools.partial(write, refs[q]))

    def in_spec(q):
        def index(h, g, c, t):
            return jnp.clip(h * groups + g - q * (groups // 2), 0, groups // 2 - 1), 0

        return pl.BlockSpec((size * rows, pieces[q].shape[1]), index)

    def out_spec(block, index):
        return pl.BlockSpec(block, lambda h, g, c, t: index(h ^ c[0], g, lambda n: n ^ (t[h] // size)))

    return pl.pallas_call(
        kernel,
        grid_spec=pltpu.PrefetchScalarGridSpec(
            num_scalar_prefetch=2,
            grid=(2, groups),
            in_specs=[in_spec(q) for q in range(4)],
            out_specs=[out_spec(block, index) for _, block, index in outs],
        ),
        out_shape=[jax.ShapeDtypeStruct(shape, F32) for shape, _, _ in outs],
        compiler_params=pltpu.CompilerParams(vmem_limit_bytes=VMEM),
        cost_estimate=QUICK,
        name=name,
    )(core, turns, *pieces)


def rows_at(ref, place, value):
    rows = value.shape[0]
    ref[pl.ds(pl.multiple_of(place * rows, 8), rows), :] = value


def down_final(core, turns, blocks, pieces, ff):
    rows, width = pieces[0].shape[0] // (blocks // 2), pieces[0].shape[1]
    size = blocks // GROUPS * rows

    def spread(block, j, place, refs):
        @pl.when(place < GROUPS - 1)
        def _():
            rows_at(refs[0], j, block)

        @pl.when((place == GROUPS - 1) & (j * rows < width // 2))
        def _():
            rows_at(refs[1], j, block)

    def down_index(h, g, place):
        at = place(g)
        near = place(jnp.where(g == 0, 1, g - 1))
        return h * (GROUPS - 1) + jnp.where(at == GROUPS - 1, near, at), 0

    outs = [
        ((ff, width), (size, width), down_index),
        ((width, width), (width // 2, width), lambda h, g, place: (h, 0)),
    ]
    return final_call(core, turns, blocks, GROUPS, pieces, "down_final", spread, outs)


def up_final(core, turns, blocks, pieces):
    rows, cols = pieces[0].shape[0] * 2, pieces[0].shape[1]

    def spread(block, j, place, refs):
        rows_at(refs[0], j, block)

    outs = [((rows, 2 * cols), (rows // 2, cols), lambda h, g, place: (place(g), h))]
    return final_call(core, turns, blocks, 2, pieces, "up_final", spread, outs)[0]


def input_final(core, turns, blocks, pieces):
    width, cols = pieces[0].shape[0] * 4, pieces[0].shape[1]

    def spread(block, j, place, refs):
        rows_at(refs[0], j, block[:, : 3 * width])
        rows_at(refs[1], j, block[:, 3 * width :])

    outs = [
        ((width, n), (width // 4, n), lambda h, g, place: (h * 2 + place(g), 0))
        for n in (3 * width, cols - 3 * width)
    ]
    return final_call(core, turns, blocks, 2, pieces, "input_final", spread, outs)


def copy_kernel(source, out):
    out[...] = source[...]


def copy_call(array):
    spec = pl.BlockSpec((1, *array.shape[1:]), lambda i: (i, 0, 0))
    return pl.pallas_call(
        copy_kernel,
        grid=(array.shape[0],),
        in_specs=[spec],
        out_specs=spec,
        out_shape=jax.ShapeDtypeStruct(array.shape, array.dtype),
        compiler_params=pltpu.CompilerParams(vmem_limit_bytes=VMEM),
        cost_estimate=QUICK,
        name="copy",
    )(array)


MICRO = 2


def from_behind(value, axis, steps):
    count = lax.axis_size(axis)
    pairs = [(source, (source + steps) % count) for source in range(count)]
    return lax.ppermute(value, axis, pairs)


def norm_rows(values, gain, shift):
    centre = values - jnp.mean(values, axis=-1, keepdims=True)
    spread = jnp.mean(centre * centre, axis=-1, keepdims=True)
    return centre * lax.rsqrt(spread + eps_norm) * gain + shift


def gelu_exact(values):
    return jax.nn.gelu(values, approximate=False)


def split_heads(block):
    return block.reshape(block.shape[0], block.shape[1], HEADS, HEAD_DIM)


def take_rows(array, first_row, count_rows):
    return lax.slice_in_dim(array, first_row, first_row + count_rows, axis=0)


def masked_scores(query, keys, ids_query, ids_keys):
    scores = jnp.einsum(
        "rqhd,rkhd->rhqk", split_heads(query), split_heads(keys), preferred_element_type=jnp.float32
    ) * HEAD_DIM ** (-0.5)
    same = ids_query[:, None, :, None] == ids_keys[:, None, None, :]
    return jnp.where(same, scores, -jnp.inf)


def attend_piece(carry, query, ids_query, piece):
    keys, values, ids_keys = piece
    peak, total, accum = carry
    scores = masked_scores(query, keys, ids_query, ids_keys)
    top = jnp.maximum(peak, jnp.max(scores, axis=-1))
    weights = jnp.exp(scores - top[..., None])
    total = jnp.sum(weights, axis=-1)
    update = jnp.einsum(
        "rhqk,rkhd->rqhd",
        weights.astype(jnp.bfloat16),
        split_heads(values),
        preferred_element_type=jnp.float32,
    )
    return (top, total, update.reshape(accum.shape))


def attention_forward(query, keys, values, ids_query):
    rows_here, slots, width = query.shape
    start_state = (
        jnp.full((rows_here, HEADS, slots), -1e30, jnp.float32),
        jnp.zeros((rows_here, HEADS, slots), jnp.float32),
        jnp.zeros((rows_here, slots, width), jnp.float32),
    )
    carry = attend_piece(
        start_state,
        query,
        ids_query,
        (
            lax.all_gather(keys, "blk", axis=1, tiled=True),
            lax.all_gather(values, "blk", axis=1, tiled=True),
            lax.all_gather(ids_query, "blk", axis=1, tiled=True),
        ),
    )
    return (carry[0], carry[1], carry[2], None)


def attention_back(query, out_grad, ids_query, log_total, inner, piece):
    keys, values, ids_keys = piece
    scale = HEAD_DIM ** (-0.5)
    scores = masked_scores(query, keys, ids_query, ids_keys)
    probs = jnp.exp(scores - log_total[..., None])
    prob_grad = jnp.einsum(
        "rqhd,rkhd->rhqk",
        split_heads(out_grad),
        split_heads(values),
        preferred_element_type=jnp.float32,
    )
    score_grad = (probs * (prob_grad - inner[..., None])).astype(jnp.bfloat16)
    value_grad = jnp.einsum(
        "rhqk,rqhd->rkhd",
        probs.astype(jnp.bfloat16),
        split_heads(out_grad),
        preferred_element_type=jnp.float32,
    )
    key_grad = (
        jnp.einsum(
            "rhqk,rqhd->rkhd", score_grad, split_heads(query), preferred_element_type=jnp.float32
        )
        * scale
    )
    query_grad = (
        jnp.einsum(
            "rhqk,rkhd->rqhd", score_grad, split_heads(keys), preferred_element_type=jnp.float32
        )
        * scale
    )
    return (
        query_grad.reshape(query.shape),
        key_grad.reshape(keys.shape),
        value_grad.reshape(values.shape),
    )


def local(
    inputs,
    image_index,
    keep_mask,
    first_gain,
    first_shift,
    input_weight,
    input_bias,
    output_weight,
    output_bias,
    second_gain,
    second_shift,
    up_weight,
    up_bias,
    down_weight,
    down_bias,
    cotangent,
):
    rows_local, slots, width = inputs.shape
    rows_micro = rows_local // MICRO
    count = rows_micro * slots
    blocks = lax.axis_size("blk")
    params = (
        first_gain,
        first_shift,
        input_weight,
        input_bias,
        output_weight,
        output_bias,
        second_gain,
        second_shift,
        up_weight,
        up_bias,
        down_weight,
        down_bias,
    )
    sums = [jnp.zeros(item.shape, jnp.float32) for item in params]
    results = []
    input_grads = []
    for micro in range(MICRO):
        first_row = micro * rows_micro
        rows_in = take_rows(inputs, first_row, rows_micro).astype(jnp.float32).reshape(count, width)
        out_cot = (
            take_rows(cotangent, first_row, rows_micro).astype(jnp.float32).reshape(count, width)
        )
        ids_query = take_rows(image_index, first_row, rows_micro).astype(jnp.bfloat16)
        keep = take_rows(keep_mask, first_row, rows_micro).astype(jnp.float32) / keep_rate
        keep_attn = jnp.broadcast_to(keep[:, None, 0:1], (rows_micro, slots, 1)).reshape(count, 1)
        keep_mlp = jnp.broadcast_to(keep[:, None, 1:2], (rows_micro, slots, 1)).reshape(count, 1)
        normed = norm_rows(rows_in, first_gain, first_shift).astype(jnp.bfloat16)
        mixed = jnp.dot(normed, input_weight, preferred_element_type=jnp.float32)
        query = (
            (mixed[:, :width] + input_bias[0])
            .astype(jnp.bfloat16)
            .reshape(rows_micro, slots, width)
        )
        keys = mixed[:, width : 2 * width].astype(jnp.bfloat16).reshape(rows_micro, slots, width)
        values = (
            (mixed[:, 2 * width :] + input_bias[1])
            .astype(jnp.bfloat16)
            .reshape(rows_micro, slots, width)
        )
        top, total, accum, whole = attention_forward(query, keys, values, ids_query)
        attended = (split_heads(accum) / jnp.transpose(total, (0, 2, 1))[..., None]).reshape(
            count, width
        )
        log_total = top + jnp.log(total)
        attended_low = attended.astype(jnp.bfloat16)
        branch = (
            jnp.dot(attended_low, output_weight, preferred_element_type=jnp.float32) + output_bias
        )
        middle = rows_in + keep_attn * branch
        normed_second = norm_rows(middle, second_gain, second_shift).astype(jnp.bfloat16)
        hidden = jnp.dot(normed_second, up_weight, preferred_element_type=jnp.float32) + up_bias
        active = gelu_exact(hidden).astype(jnp.bfloat16)
        branch_second = jnp.dot(active, down_weight, preferred_element_type=jnp.float32) + down_bias
        results.append(
            (middle + keep_mlp * branch_second)
            .astype(jnp.bfloat16)
            .reshape(rows_micro, slots, width)
        )
        mlp_grad = (out_cot * keep_mlp).astype(jnp.bfloat16)
        sums[10] = sums[10] + jnp.dot(active.T, mlp_grad, preferred_element_type=jnp.float32)
        sums[11] = sums[11] + jnp.sum(mlp_grad.astype(jnp.float32), axis=0)
        active_grad = jnp.dot(mlp_grad, down_weight.T, preferred_element_type=jnp.float32)
        hidden_grad = jax.vjp(gelu_exact, hidden)[1](active_grad)[0].astype(jnp.bfloat16)
        sums[8] = sums[8] + jnp.dot(
            normed_second.T, hidden_grad, preferred_element_type=jnp.float32
        )
        sums[9] = sums[9] + jnp.sum(hidden_grad.astype(jnp.float32), axis=0)
        second_in_grad = jnp.dot(hidden_grad, up_weight.T, preferred_element_type=jnp.float32)
        middle_part, second_gain_part, second_shift_part = jax.vjp(
            norm_rows, middle, second_gain, second_shift
        )[1](second_in_grad)
        sums[6] = sums[6] + second_gain_part
        sums[7] = sums[7] + second_shift_part
        middle_grad = middle_part + out_cot
        branch_grad = (middle_grad * keep_attn).astype(jnp.bfloat16)
        sums[4] = sums[4] + jnp.dot(attended_low.T, branch_grad, preferred_element_type=jnp.float32)
        sums[5] = sums[5] + jnp.sum(branch_grad.astype(jnp.float32), axis=0)
        attended_grad = jnp.dot(
            branch_grad, output_weight.T, preferred_element_type=jnp.float32
        ).astype(jnp.bfloat16)
        out_grad = attended_grad.reshape(rows_micro, slots, width)
        inner = jnp.transpose(
            jnp.sum(
                split_heads(
                    (attended_grad.astype(jnp.float32) * attended).reshape(rows_micro, slots, width)
                ),
                axis=-1,
            ),
            (0, 2, 1),
        )
        query_grad = jnp.zeros((rows_micro, slots, width), jnp.float32)
        visiting = (keys, values, ids_query)
        key_grad = jnp.zeros((rows_micro, slots, width), jnp.float32)
        value_grad = jnp.zeros((rows_micro, slots, width), jnp.float32)
        for step in range(blocks):
            query_part, key_part, value_part = attention_back(
                query, out_grad, ids_query, log_total, inner, visiting
            )
            query_grad = query_grad + query_part
            key_grad, value_grad = (
                from_behind((key_grad + key_part).astype(jnp.bfloat16), "blk", 1).astype(
                    jnp.float32
                ),
                from_behind((value_grad + value_part).astype(jnp.bfloat16), "blk", 1).astype(
                    jnp.float32
                ),
            )
            if step + 1 < blocks:
                visiting = from_behind((visiting[0], visiting[1], visiting[2]), "blk", 1)
        joined_grad = (
            jnp.concatenate([query_grad, key_grad, value_grad], axis=-1)
            .astype(jnp.bfloat16)
            .reshape(count, 3 * width)
        )
        sums[2] = sums[2] + jnp.dot(normed.T, joined_grad, preferred_element_type=jnp.float32)
        joined_sums = jnp.sum(joined_grad.astype(jnp.float32), axis=0)
        sums[3] = sums[3] + jnp.stack([joined_sums[:width], joined_sums[2 * width :]])
        first_in_grad = jnp.dot(joined_grad, input_weight.T, preferred_element_type=jnp.float32)
        rows_part, first_gain_part, first_shift_part = jax.vjp(
            norm_rows, rows_in, first_gain, first_shift
        )[1](first_in_grad)
        sums[0] = sums[0] + first_gain_part
        sums[1] = sums[1] + first_shift_part
        input_grads.append(
            (rows_part + middle_grad).astype(jnp.bfloat16).reshape(rows_micro, slots, width)
        )
    totals = lax.psum(
        (
            sums[0],
            sums[1],
            sums[2],
            sums[3],
            sums[4],
            sums[5],
            sums[6],
            sums[7],
            sums[8],
            sums[9],
            sums[10],
            sums[11],
        ),
        ("rows", "blk"),
    )
    return (
        jnp.concatenate(results, axis=0),
        jnp.concatenate(input_grads, axis=0),
        totals[0],
        totals[1],
        totals[2],
        totals[3],
        totals[4],
        totals[5],
        totals[6],
        totals[7],
        totals[8],
        totals[9],
        totals[10],
        totals[11],
    )


def swap(value, axis, bit):
    return lax.ppermute(value, axis, [(i, i ^ bit) for i in range(lax.axis_size(axis))])


def side(axis, bit):
    return (lax.axis_index(axis) // bit) % 2


def after(value, *others):
    return lax.optimization_barrier((value, *others))[0]


def axis_bits(axis):
    bits, bit = [], 1
    while bit < lax.axis_size(axis):
        bits.append((axis, bit))
        bit *= 2
    return bits


def add_low(a, b):
    return (a.astype(F32) + b.astype(F32)).astype(BF16)


def swap_two(value, step):
    rows, blocks = lax.axis_size("rows"), lax.axis_size("blk")
    pairs = []
    for r in range(rows):
        for b in range(blocks):
            axis, bit = step[b % 2]
            other = (r ^ bit, b) if axis == "rows" else (r, b ^ bit)
            pairs.append((r * blocks + b, other[0] * blocks + other[1]))
    return lax.ppermute(value, ("rows", "blk"), pairs)


def side_two(step):
    return jnp.where(side("blk", 1) == 0, side(*step[0]), side(*step[1]))


class Order:
    def __init__(self):
        self.last = ()

    def hold(self, value):
        return after(value, *self.last) if self.last else value

    def advance(self, *parts):
        parts = [part for part in parts if part.result is None]
        if parts:
            held = lax.optimization_barrier(([part.recv for part in parts], self.last))[0]
            self.done(*[value for part, recv in zip(parts, held) for value in part.step(recv)])

    def done(self, *values):
        self.last = values
        return values[0] if len(values) == 1 else values


class Chain:
    def __init__(self, steps, send, keep):
        self.steps, self.at = steps, -1
        self.recv, self.keep, self.result = send, keep, None

    def step(self, recv):
        keep, n = self.keep, len(self.steps)
        if self.at < 0:
            send, self.recv = recv, swap(recv, "blk", 1)
        elif self.at < n:
            step = self.steps[self.at]
            half = keep.shape[0] // 2
            own = side_two(step)

            def part(which):
                return add_low(
                    lax.dynamic_slice_in_dim(keep, which * half, half, 0),
                    lax.dynamic_slice_in_dim(recv, which * half, half, 0),
                )

            send, self.keep = part(1 - own), part(own)
            self.recv = swap_two(send, step)
        elif self.at < 2 * n:
            send = add_low(keep, recv) if self.at == n else jnp.concatenate([keep, recv], axis=0)
            send = self.keep = lax.optimization_barrier(send)
            self.recv = swap_two(send, self.steps[2 * n - 1 - self.at])
        elif self.at == 2 * n:
            self.at, self.keep, self.recv = self.at + 1, (keep, recv), [swap(piece, "blk", 1) for piece in (keep, recv)]
            return keep, recv
        else:
            self.result, self.recv = (*keep, *recv), None
            return ()
        self.at += 1
        return send, self.keep


class Small:
    def __init__(self, value):
        count = lax.axis_size("rows") * lax.axis_size("blk")
        self.recv, self.result, self.sent = jnp.broadcast_to(value[None], (count, *value.shape)), None, False

    def step(self, recv):
        if not self.sent:
            self.recv, self.sent = lax.all_to_all(recv, ("rows", "blk"), 0, 0), True
            return (recv,)
        self.result, self.recv = jnp.sum(recv, axis=0), None
        return (self.result,)


class Home:
    def __init__(self, pieces):
        self.recv, self.result, self.sent = pieces, None, False

    def step(self, recv):
        if not self.sent:
            self.recv, self.sent = lax.all_to_all(recv, "blk", 0, 0), True
        else:
            self.result, self.recv = recv, None
        return (recv,)


def block_turns(steps):
    core = side("blk", 1)
    turns = []
    for c in range(2):
        turn = 0
        for step in steps:
            turn = turn * 2 + side(*step[c])
        turns.append(turn)
    first, second = jnp.where(core == 0, turns[0], turns[1]), jnp.where(core == 0, turns[1], turns[0])
    return core.astype(jnp.int32).reshape(1), jnp.stack([first, second]).astype(jnp.int32), 1 << len(steps)


def local_rows(
    inputs,
    image_index,
    keep_mask,
    first_gain,
    first_shift,
    input_weight,
    input_bias,
    output_weight,
    output_bias,
    second_gain,
    second_shift,
    up_weight,
    up_bias,
    down_weight,
    down_bias,
    cotangent,
):
    blocks, span, width = inputs.shape
    ff = up_weight.shape[1]
    me = lax.axis_index("blk")

    def row_piece(array, s):
        return lax.dynamic_index_in_dim(array, me ^ s, 0, keepdims=False)

    xs_send = [row_piece(inputs, s) for s in range(blocks)]
    xs_in = xs_send[:1] + [swap(xs_send[s], "blk", s) for s in range(1, blocks)]
    ids = [row_piece(image_index, 0)] + [
        swap(row_piece(after(image_index, *xs_send), s), "blk", s) for s in range(1, blocks)
    ]
    cots = [row_piece(cotangent, 0)] + [
        swap(after(row_piece(cotangent, s), *xs_send), "blk", s) for s in range(1, blocks)
    ]
    ids = jnp.concatenate(ids)
    image = jnp.where(ids < 0, 4, ids)
    order_key = image * ids.shape[0] + jnp.arange(ids.shape[0], dtype=jnp.int32)
    less = (order_key[None, :] < order_key[:, None]).astype(jnp.int32)
    rank = jnp.sum(less, axis=1)
    starts = jnp.sum((image[None, :] < jnp.arange(6, dtype=jnp.int32)[:, None]).astype(jnp.int32), axis=1)
    keep = lax.dynamic_index_in_dim(keep_mask, me, 0, keepdims=False).astype(F32) / keep_rate
    rank_row, rank_col = rank[None, :], rank[:, None]

    bias = jnp.stack([input_bias[0], jnp.zeros_like(input_bias[0]), input_bias[1]])
    xs, normed, qkv = qkv_call(rank_row, xs_in, first_gain[None], first_shift[None], input_weight, bias)
    attended, stat, att_low = forward_call(starts, qkv)
    vectors = jnp.stack([output_bias, second_gain, second_shift, down_bias])
    core = side("blk", 1).astype(jnp.int32).reshape(1)
    cot, middle, normed2, mlp_grad, sums_mid = middle_call(
        keep, rank_row, cots, att_low, xs, output_weight, vectors
    )
    (up_send, up_keep, down_send, down_keep, up_sums, result, middle_grad, branch, att_grad, sums2) = mlp_call(
        core, keep, normed2, mlp_grad, middle, cot, att_low, output_weight, vectors, up_weight, up_bias[None], down_weight
    )

    y, x, z = axis_bits("blk")[1], axis_bits("rows")[0], axis_bits("rows")[1:]
    far = [(d, d) for d in z[1:]]
    xy = [(x, y), (y, x), (z[0], z[0])] + far
    zx = [(z[0], z[0]), (x, y), (y, x)] + far
    order = Order()
    order.done(att_grad)
    up_chain, down_chain = Chain(zx, up_send, up_keep), Chain(xy, down_send, down_keep)

    order.advance(down_chain, up_chain)
    result_home = Home(order.done(unsort_call(me.reshape(1), rank_col, blocks, order.hold(result))))
    order.advance(down_chain, up_chain, result_home)
    grads, bias_sums = backward_call(starts, qkv, order.hold(att_grad), attended, stat, 0, PAIRS)
    order.done(grads)
    order.advance(down_chain, up_chain, result_home)
    input_chain = Chain(
        xy, *order.done(*input_weights_call(core, order.hold(normed), grads, bias_sums, sums2, sums_mid, up_sums))
    )
    order.advance(down_chain, up_chain, input_chain)
    inputs_grad, sums1 = order.done(*input_call(grads, input_weight, xs, order.hold(middle_grad), first_gain[None]))
    small = Small(sums1[:2])
    order.advance(down_chain, up_chain, input_chain, small)
    home = Home(order.done(unsort_call(me.reshape(1), rank_col, blocks, order.hold(inputs_grad))))
    order.advance(down_chain, up_chain, input_chain, small, home)
    order.advance(down_chain, up_chain, input_chain)
    order.advance(down_chain, up_chain, input_chain, home)
    while down_chain.at < 2 * len(xy):
        order.advance(down_chain, up_chain, input_chain)
    result_out = order.done(copy_call(order.hold(result_home.result)))
    inputs_out = order.done(copy_call(order.hold(home.result)))
    order.advance(down_chain, up_chain, input_chain)
    order.advance(down_chain, up_chain, input_chain)
    up_total = order.done(up_final(*block_turns(zx), (order.hold(up_chain.result[0]), *up_chain.result[1:])))
    order.advance(input_chain)
    down_total, out_total = order.done(
        *down_final(*block_turns(xy), (order.hold(down_chain.result[0]), *down_chain.result[1:]), ff)
    )
    while input_chain.result is None:
        order.advance(input_chain)
    input_total, sums = input_final(*block_turns(xy), input_chain.result)
    sums = jnp.concatenate([small.result, sums[:, :16].T])

    return (
        result_out,
        inputs_out,
        sums[0],
        sums[1],
        input_total,
        jnp.stack([sums[2], sums[4]]),
        out_total,
        sums[7],
        sums[5],
        sums[6],
        up_total,
        sums[9:13].reshape(ff),
        down_total,
        sums[8],
    )


def solution(mesh):
    blocks, groups = mesh.shape["blk"], mesh.shape["rows"]

    def run(*args):
        whole_rows = args[0].shape[0] // groups == blocks == 4 and groups in (4, 8, 16)
        return jax.shard_map(
            local_rows if whole_rows else local,
            mesh=mesh,
            in_specs=(P("rows", "blk", None), P("rows", "blk"), P("rows", None)) + (P(),) * 12 + (P("rows", "blk", None),),
            out_specs=(P("rows", "blk", None),) * 2 + (P(),) * 12,
            check_vma=False,
        )(*args)

    return run
```

```python
import functools

import jax
import jax.numpy as jnp
from jax import lax
from jax.experimental import pallas as pl
from jax.experimental.pallas import tpu as pltpu
from jax.sharding import PartitionSpec as P

HEADS = 12
HEAD_DIM = 64
PAIR = 2 * HEAD_DIM
PAIRS = HEADS // 2
eps_norm = 1e-06
keep_rate = 0.9
F32 = jnp.float32
BF16 = jnp.bfloat16
NEG = -1e30
VMEM = 62 * 1024 * 1024
QUICK = pl.CostEstimate(flops=1 << 20, bytes_accessed=1 << 16, transcendentals=0)


def dot(a, b):
    return jnp.dot(a, b, preferred_element_type=F32)


def dot_nt(a, b):
    return lax.dot_general(a, b, (((1,), (1,)), ((), ())), preferred_element_type=F32)


def dot_tn(a, b):
    return lax.dot_general(a, b, (((0,), (0,)), ((), ())), preferred_element_type=F32)


def whole(shape):
    return pl.BlockSpec(shape, lambda *g: (0,) * len(shape), pipeline_mode=pl.Buffered(1))


def centre_scale(values):
    centre = values - jnp.mean(values, axis=-1, keepdims=True)
    spread = jnp.mean(centre * centre, axis=-1, keepdims=True)
    inv = lax.rsqrt(spread + eps_norm)
    return centre * inv, inv


def norm_back(grad_hat, hat, inv):
    first = jnp.mean(grad_hat, axis=-1, keepdims=True)
    second = jnp.mean(grad_hat * hat, axis=-1, keepdims=True)
    return (grad_hat - first - hat * second) * inv


def gather_pieces(step, pieces, row):
    @pl.when(step == 0)
    def _():
        span = pieces[0].shape[0]
        for i, piece in enumerate(pieces):
            row[i * span : (i + 1) * span, :] = piece[...]


def sort_tile(rank_row, tile, step, row):
    place = step * tile + lax.broadcasted_iota(jnp.int32, (tile, row.shape[0]), 0)
    return dot((rank_row == place).astype(BF16), row[...])


def qkv_kernel(n, tile, *refs):
    rank, *pieces = refs[: n + 1]
    gain, shift, weight, bias, xs_out, normed_out, qkv_out, row = refs[n + 1 :]
    gather_pieces(pl.program_id(0), pieces, row)
    xs = sort_tile(rank[...], tile, pl.program_id(0), row)
    xs_out[...] = xs.astype(BF16)
    hat, _ = centre_scale(xs)
    normed = (hat * gain[...] + shift[...]).astype(BF16)
    normed_out[...] = normed
    width = normed.shape[1]
    for j in range(3):
        cols = slice(j * width, (j + 1) * width)
        mixed = (dot(normed, weight[:, cols]) + bias[j : j + 1, :]).astype(BF16)
        qkv_out[j] = mixed * BF16(HEAD_DIM**-0.5) if j == 0 else mixed


def qkv_call(rank, pieces, gain, shift, weight, bias, tile=288):
    n = len(pieces)
    span, width = pieces[0].shape
    count = n * span
    return pl.pallas_call(
        functools.partial(qkv_kernel, n, tile),
        grid=(count // tile,),
        in_specs=[whole((1, count))]
        + [whole((span, width))] * n
        + [whole((1, width)), whole((1, width)), whole(weight.shape), whole(bias.shape)],
        out_specs=[
            pl.BlockSpec((tile, width), lambda i: (i, 0)),
            pl.BlockSpec((tile, width), lambda i: (i, 0)),
            pl.BlockSpec((3, tile, width), lambda i: (0, i, 0)),
        ],
        out_shape=[
            jax.ShapeDtypeStruct((count, width), BF16),
            jax.ShapeDtypeStruct((count, width), BF16),
            jax.ShapeDtypeStruct((3, count, width), BF16),
        ],
        scratch_shapes=[pltpu.VMEM((count, width), BF16)],
        compiler_params=pltpu.CompilerParams(vmem_limit_bytes=VMEM),
        cost_estimate=QUICK,
        name="sort_qkv",
    )(rank, *pieces, gain, shift, weight, bias)


SMALL = 304
LARGE = 384


def windows(starts, seg, length):
    first, last = starts[seg], starts[seg + 1]
    aligned = first // 16 * 16
    small = SMALL if seg < 4 else LARGE
    at_small = pl.multiple_of(jnp.minimum(aligned, length - small), 16)
    at_large = pl.multiple_of(jnp.minimum(aligned, length - LARGE), 16)
    return first, last, small, at_small, at_large


def inside(at, size, lanes, first, last):
    place = at + lax.broadcasted_iota(jnp.int32, (size, lanes), 0)
    return (place >= first) & (place < last)


def forward_kernel(starts, qkv, out, stat, low_out):
    length = qkv.shape[1]
    for seg in range(5):
        first, last, small, at_q, at_k = windows(starts, seg, length)
        rows_q = pl.ds(at_q, small)
        q = qkv[0, rows_q, :]
        k = qkv[1, pl.ds(at_k, LARGE), :]
        v = qkv[2, pl.ds(at_k, LARGE), :]
        lane = lax.broadcasted_iota(jnp.int32, (LARGE, PAIR), 1)
        lane_q = lax.broadcasted_iota(jnp.int32, (small, PAIR), 1)
        low = lane < HEAD_DIM
        seen = inside(at_k, LARGE, PAIR, first, last)
        zero = jnp.zeros((LARGE, PAIR), BF16)
        one = jnp.ones((LARGE, PAIR), BF16)
        bias = jnp.where((lane == 0) & ~seen, NEG, 0.0).astype(BF16)
        q_ext = jnp.concatenate([q, (lane_q == 0).astype(BF16)], axis=1)
        halves = (low, ~low)
        k_ext = [jnp.concatenate([jnp.where(half, k, zero), bias], axis=1) for half in halves]
        mixes = [
            jnp.concatenate([jnp.where(half, v, zero), jnp.where(half, one, zero)], axis=1) for half in halves
        ]
        pair = dot_nt(q_ext, jnp.concatenate(k_ext, axis=0))
        tops, weights = [], []
        for h in range(2):
            scores = pair[:, h * LARGE : (h + 1) * LARGE]
            top = jnp.max(scores, axis=-1, keepdims=True)
            tops.append(top)
            weights.append(jnp.exp(scores - top).astype(BF16))
        both = dot(jnp.concatenate(weights, axis=1), jnp.concatenate(mixes, axis=0))
        total = both[:, PAIR:]
        peak = jnp.where(lane_q < HEAD_DIM, tops[0], tops[1])
        mine = inside(at_q, small, PAIR, first, last)
        out[rows_q, :] = jnp.where(mine, both[:, :PAIR] / total, out[rows_q, :])
        stat[rows_q, :] = jnp.where(mine, peak + jnp.log(total), stat[rows_q, :])
    low_out[...] = out[...].astype(BF16)


def forward_call(starts, qkv):
    _, count, wide = qkv.shape
    pairs = wide // PAIR
    return pl.pallas_call(
        forward_kernel,
        grid_spec=pltpu.PrefetchScalarGridSpec(
            num_scalar_prefetch=1,
            grid=(pairs,),
            in_specs=[pl.BlockSpec((3, count, PAIR), lambda p, s: (0, 0, p))],
            out_specs=[pl.BlockSpec((count, PAIR), lambda p, s: (0, p))] * 3,
        ),
        out_shape=[jax.ShapeDtypeStruct((count, pairs * PAIR), dtype) for dtype in (F32, F32, BF16)],
        compiler_params=pltpu.CompilerParams(vmem_limit_bytes=VMEM),
        cost_estimate=QUICK,
        name="attention_forward",
    )(starts, qkv)


def split3(value):
    high = value.astype(BF16)
    rest = value - high.astype(F32)
    mid = rest.astype(BF16)
    return high, mid, (rest - mid.astype(F32)).astype(BF16)


def backward_kernel(starts, qkv, grad, att, stat, *refs):
    out, sums = refs[-2:]
    length = qkv.shape[1]
    third = lax.broadcasted_iota(jnp.int32, (PAIR, PAIR), 0) // HEAD_DIM
    block = (third == lax.broadcasted_iota(jnp.int32, (PAIR, PAIR), 1) // HEAD_DIM).astype(BF16)
    for seg in range(5):
        first, last, small, at_k, at_q = windows(starts, seg, length)
        rows_q, rows_k = pl.ds(at_q, LARGE), pl.ds(at_k, small)
        lane_q = lax.broadcasted_iota(jnp.int32, (LARGE, PAIR), 1)
        lane_k = lax.broadcasted_iota(jnp.int32, (small, PAIR), 1)
        spot_q, spot_k = lane_q % HEAD_DIM, lane_k % HEAD_DIM
        mine_q = inside(at_q, LARGE, PAIR, first, last)
        mine_k = inside(at_k, small, PAIR, first, last)
        zero_q = jnp.zeros((LARGE, PAIR), BF16)
        zero_k = jnp.zeros((small, PAIR), BF16)
        q = qkv[0, rows_q, :]
        k = jnp.where(mine_k, qkv[1, rows_k, :], zero_k)
        v = qkv[2, rows_k, :]
        g = jnp.where(mine_q, grad[rows_q, :], zero_q)
        prod = g.astype(F32) * jnp.where(mine_q, att[rows_q, :], 0.0)
        p_high = prod.astype(BF16)
        p_low = (prod - p_high.astype(F32)).astype(BF16)
        inner = dot(p_high, block) + dot(p_low, block)
        logs = jnp.where(mine_q, stat[rows_q, :], 0.0)

        def spread(value, fifth):
            a, b, c = split3(value)
            return jnp.where(
                spot_q == 0, a, jnp.where(spot_q == 1, b, jnp.where(spot_q == 2, c, fifth))
            )

        query_bias = jnp.where(mine_q, 0.0, NEG).astype(BF16)
        unit = jnp.ones((LARGE, PAIR), BF16)
        q_tail = spread(logs, jnp.where(spot_q == 3, unit, jnp.where(spot_q == 4, query_bias, zero_q)))
        g_tail = spread(inner, zero_q)
        key_bias = jnp.where(mine_k, 0.0, NEG).astype(BF16)
        minus = jnp.where(spot_k < 3, -1.0, 0.0).astype(BF16)
        k_tail = jnp.where(
            spot_k == 3, key_bias, jnp.where(spot_k == 4, jnp.ones((small, PAIR), BF16), minus)
        )
        heads_q = [lane_q // HEAD_DIM == h for h in range(2)]
        qs = [jnp.where(head, q, zero_q) for head in heads_q]
        gs = [jnp.where(head, g, zero_q) for head in heads_q]
        q_both = [jnp.concatenate([x, jnp.where(head, q_tail, zero_q)], axis=1) for x, head in zip(qs, heads_q)]
        g_both = [jnp.concatenate([x, jnp.where(head, g_tail, zero_q)], axis=1) for x, head in zip(gs, heads_q)]
        prob = jnp.exp(dot_nt(jnp.concatenate([k, k_tail], axis=1), jnp.concatenate(q_both, axis=0)))
        prob_grad = dot_nt(jnp.concatenate([v, minus], axis=1), jnp.concatenate(g_both, axis=0))
        score_grad = (prob * prob_grad).astype(BF16)
        value_grad = dot(prob.astype(BF16), jnp.concatenate(gs, axis=0))
        key_grad = dot(score_grad, jnp.concatenate(qs, axis=0))
        stacked = jnp.concatenate([score_grad[:, :LARGE], score_grad[:, LARGE:]], axis=0)
        ks = [jnp.where(lane_k // HEAD_DIM == h, k, zero_k) for h in range(2)]
        query_grad = dot_tn(stacked, jnp.concatenate(ks, axis=0))
        query_grad = (query_grad * HEAD_DIM**-0.5).astype(BF16)
        out[0, rows_q, :] = jnp.where(mine_q, query_grad, out[0, rows_q, :])
        out[1, rows_k, :] = jnp.where(mine_k, key_grad.astype(BF16), out[1, rows_k, :])
        out[2, rows_k, :] = jnp.where(mine_k, value_grad.astype(BF16), out[2, rows_k, :])
    for j in range(3):
        sums[j : j + 1, :] = jnp.sum(out[j].astype(F32), axis=0, keepdims=True)


def backward_call(starts, qkv, grad, att, stat, first_pair, pairs, before=None):
    _, count, width = qkv.shape
    held = [] if before is None else list(before)
    return pl.pallas_call(
        backward_kernel,
        grid_spec=pltpu.PrefetchScalarGridSpec(
            num_scalar_prefetch=1,
            grid=(pairs,),
            in_specs=[pl.BlockSpec((3, count, PAIR), lambda p, s: (0, 0, p + first_pair))]
            + [pl.BlockSpec((count, PAIR), lambda p, s: (0, p + first_pair))] * 3
            + [pl.BlockSpec(memory_space=pl.ANY)] * len(held),
            out_specs=[
                pl.BlockSpec((3, count, PAIR), lambda p, s: (0, 0, p + first_pair)),
                pl.BlockSpec((8, PAIR), lambda p, s: (0, p + first_pair)),
            ],
        ),
        out_shape=[
            jax.ShapeDtypeStruct((3, count, width), BF16),
            jax.ShapeDtypeStruct((8, width), F32),
        ],
        input_output_aliases={5: 0, 6: 1} if held else {},
        compiler_params=pltpu.CompilerParams(vmem_limit_bytes=VMEM),
        cost_estimate=QUICK,
        name="attention_backward",
    )(starts, qkv, grad, att, stat, *held)


HALF_ERF = tuple(0.5 * c for c in (0.254829592, -0.284496736, 1.421413741, -1.453152027, 1.061405429))
LOG2_E = 1.4426950408889634


def gelu_pair(u):
    size = jnp.abs(u)
    t = 1.0 / (1.0 + (0.3275911 * 0.5**0.5) * size)
    bell = jnp.exp2(u * u * (-0.5 * LOG2_E))
    poly = HALF_ERF[4] * t + HALF_ERF[3]
    for c in (HALF_ERF[2], HALF_ERF[1], HALF_ERF[0]):
        poly = poly * t + c
    tail = poly * t * bell
    phi = jnp.where(u < 0, tail, 1.0 - tail)
    return u * phi, phi + u * bell * 0.3989422804014327


def middle_kernel(n, tile, *refs):
    keep, rank, *pieces = refs[: n + 2]
    att, xs, out_w, vectors, cot_out, middle_out, normed_out, mlp_out, sums, row = refs[n + 2 :]
    step = pl.program_id(0)
    gather_pieces(step, pieces, row)
    cot = sort_tile(rank[...], tile, step, row)
    cot_out[...] = cot.astype(BF16)
    mlp_grad = (cot * keep[1]).astype(BF16)
    mlp_out[...] = mlp_grad
    middle = xs[...].astype(F32) + keep[0] * (dot(att[...], out_w[...]) + vectors[0:1, :])
    middle_out[...] = middle
    hat, _ = centre_scale(middle)
    normed_out[...] = (hat * vectors[1:2, :] + vectors[2:3, :]).astype(BF16)

    @pl.when(step == 0)
    def _():
        sums[...] = jnp.zeros_like(sums)

    sums[0:1, :] += jnp.sum(mlp_grad.astype(F32), axis=0, keepdims=True)


def middle_call(keep, rank, pieces, att, xs, out_w, vectors, tile=384):
    n = len(pieces)
    span, width = pieces[0].shape
    count = n * span
    rows = pl.BlockSpec((tile, width), lambda i: (i, 0))
    low, full = jax.ShapeDtypeStruct((count, width), BF16), jax.ShapeDtypeStruct((count, width), F32)
    return pl.pallas_call(
        functools.partial(middle_kernel, n, tile),
        grid=(count // tile,),
        in_specs=[pl.BlockSpec(memory_space=pltpu.SMEM), whole((1, count))]
        + [whole((span, width))] * n
        + [rows, rows, whole(out_w.shape), whole(vectors.shape)],
        out_specs=[rows] * 4 + [pl.BlockSpec((8, width), lambda i: (0, 0))],
        out_shape=[low, full, low, low, jax.ShapeDtypeStruct((8, width), F32)],
        scratch_shapes=[pltpu.VMEM((count, width), BF16)],
        compiler_params=pltpu.CompilerParams(vmem_limit_bytes=VMEM),
        cost_estimate=QUICK,
        name="middle",
    )(keep, rank, *pieces, att, xs, out_w, vectors)


def mlp_kernel(parts, core, keep, normed, mlp_grad, middle, cot, att, out_w, vectors, up_w, up_b, down_w, *refs):
    (
        up_send, up_keep, down_send, down_keep, up_sums, result, middle_grad_out, branch_out, att_grad_out, sums,
        lift, back, act_all, hidden_all,
    ) = refs
    step, half = pl.program_id(0), pl.num_programs(0) // 2
    count, width = normed.shape
    cuts = [slice(i * (count // parts), (i + 1) * (count // parts)) for i in range(parts)]

    @pl.when(step == 0)
    def _():
        lift[...] = jnp.zeros_like(lift)
        back[...] = jnp.zeros_like(back)

    @pl.when(step < 2 * half)
    def _():
        total = jnp.zeros(up_sums.shape, F32)
        ready = None
        for rows in cuts + [None]:
            fresh = None
            if rows is not None:
                u = dot(normed[rows, :], up_w[...]) + up_b[...]
                fresh = (rows, u, dot_nt(mlp_grad[rows, :], down_w[...]))
            if ready is not None:
                past, u, act_grad = ready
                act, slope = gelu_pair(u)
                act_all[past, :] = act.astype(BF16)
                hidden = (act_grad * slope).astype(BF16)
                hidden_all[past, :] = hidden
                total = total + jnp.sum(hidden.astype(F32), axis=0, keepdims=True)
            ready = fresh
        lift[...] += dot(act_all[...], down_w[...])
        back[...] += dot_nt(hidden_all[...], up_w[...])
        up_sums[...] = total
        up_part = dot_tn(normed[...], hidden_all[...]).astype(BF16)
        down_part = dot_tn(act_all[...], mlp_grad[...]).astype(BF16)

        @pl.when(step < half)
        def _():
            up_send[...] = up_part
            down_send[...] = down_part

        @pl.when(step >= half)
        def _():
            up_keep[...] = up_part
            down_keep[...] = down_part

    @pl.when(step == 2 * half)
    def _():
        gain, down_b = vectors[1:2, :], vectors[3:4, :]
        sums[...] = jnp.zeros_like(sums)
        for rows in cuts:
            mid, grad = middle[rows, :], back[rows, :]
            hat, inv = centre_scale(mid)
            result[rows, :] = (mid + keep[1] * (lift[rows, :] + down_b)).astype(BF16)
            middle_grad = cot[rows, :].astype(F32) + norm_back(grad * gain, hat, inv)
            middle_grad_out[rows, :] = middle_grad
            branch = (keep[0] * middle_grad).astype(BF16)
            branch_out[rows, :] = branch
            att_grad_out[rows, :] = dot_nt(branch, out_w[...]).astype(BF16)
            sums[0:1, :] += jnp.sum(grad * hat, axis=0, keepdims=True)
            sums[1:2, :] += jnp.sum(grad, axis=0, keepdims=True)
            sums[2:3, :] += jnp.sum(branch.astype(F32), axis=0, keepdims=True)
        for out, c in ((down_send, 1 - core[0]), (down_keep, core[0])):
            cols = pl.ds(pl.multiple_of(c * (width // 2), 128), width // 2)
            out[: width // 2, :] = dot_tn(att[:, cols], branch_out[...]).astype(BF16)
            out[width // 2 :, :] = jnp.zeros((out.shape[0] - width // 2, width), BF16)


def mlp_call(core, keep, normed, mlp_grad, middle, cot, att, out_w, vectors, up_w, up_b, down_w, chunk=512, parts=4):
    count, width = normed.shape
    ff = up_w.shape[1]
    half = ff // 2 // chunk

    def place(i, c):
        i = jnp.minimum(i, 2 * half - 1)
        return jnp.where(i < half, (1 - c[0]) * half + i, c[0] * half + i - half)

    def first(i):
        return jnp.minimum(i, half - 1)

    def second(i):
        return jnp.clip(i - half, 0, half - 1)

    def extra(i, index):
        return jnp.where(i == 2 * half, half, index)

    low, full = jax.ShapeDtypeStruct((count, width), BF16), jax.ShapeDtypeStruct((count, width), F32)
    return pl.pallas_call(
        functools.partial(mlp_kernel, parts),
        grid_spec=pltpu.PrefetchScalarGridSpec(
            num_scalar_prefetch=1,
            grid=(2 * half + 1,),
            in_specs=[pl.BlockSpec(memory_space=pltpu.SMEM)]
            + [whole((count, width))] * 5
            + [
                whole(out_w.shape),
                whole(vectors.shape),
                pl.BlockSpec((width, chunk), lambda i, c: (0, place(i, c))),
                pl.BlockSpec((1, chunk), lambda i, c: (0, place(i, c))),
                pl.BlockSpec((chunk, width), lambda i, c: (place(i, c), 0)),
            ],
            out_specs=[
                pl.BlockSpec((width, chunk), lambda i, c: (0, first(i))),
                pl.BlockSpec((width, chunk), lambda i, c: (0, second(i))),
                pl.BlockSpec((chunk, width), lambda i, c: (extra(i, first(i)), 0)),
                pl.BlockSpec((chunk, width), lambda i, c: (extra(i, second(i)), 0)),
                pl.BlockSpec((1, chunk), lambda i, c: (0, place(i, c))),
            ]
            + [whole((count, width))] * 4
            + [whole((8, width))],
            scratch_shapes=[pltpu.VMEM((count, width), F32)] * 2 + [pltpu.VMEM((count, chunk), BF16)] * 2,
        ),
        out_shape=[jax.ShapeDtypeStruct((width, ff // 2), BF16)] * 2
        + [jax.ShapeDtypeStruct((ff // 2 + chunk, width), BF16)] * 2
        + [jax.ShapeDtypeStruct((1, ff), F32), low, full, low, low, jax.ShapeDtypeStruct((8, width), F32)],
        compiler_params=pltpu.CompilerParams(vmem_limit_bytes=VMEM),
        cost_estimate=QUICK,
        name="mlp",
    )(core, keep, normed, mlp_grad, middle, cot, att, out_w, vectors, up_w, up_b, down_w)


def input_kernel(grads, weight, xs, middle_grad, gain, out, sums):
    span = xs.shape[1]
    back = None
    for j in range(3):
        part = dot_nt(grads[j], weight[:, j * span : (j + 1) * span])
        back = part if back is None else back + part
    hat, inv = centre_scale(xs[...].astype(F32))
    out[...] = (middle_grad[...] + norm_back(back * gain[...], hat, inv)).astype(BF16)

    @pl.when(pl.program_id(0) == 0)
    def _():
        sums[...] = jnp.zeros_like(sums)

    sums[0:1, :] += jnp.sum(back * hat, axis=0, keepdims=True)
    sums[1:2, :] += jnp.sum(back, axis=0, keepdims=True)


def input_call(grads, weight, xs, middle_grad, gain, tile=288):
    count, width = xs.shape
    return pl.pallas_call(
        input_kernel,
        grid=(count // tile,),
        in_specs=[pl.BlockSpec((3, tile, width), lambda i: (0, i, 0))]
        + [
            whole(weight.shape),
            pl.BlockSpec((tile, width), lambda i: (i, 0)),
            pl.BlockSpec((tile, width), lambda i: (i, 0)),
            whole((1, width)),
        ],
        out_specs=[pl.BlockSpec((tile, width), lambda i: (i, 0)), pl.BlockSpec((8, width), lambda i: (0, 0))],
        out_shape=[jax.ShapeDtypeStruct((count, width), BF16), jax.ShapeDtypeStruct((8, width), F32)],
        compiler_params=pltpu.CompilerParams(vmem_limit_bytes=VMEM),
        cost_estimate=QUICK,
        name="input_backward",
    )(grads, weight, xs, middle_grad, gain)


def unsort_kernel(me, rank, source, out):
    count, span = source.shape[0], rank.shape[0]
    place = lax.broadcasted_iota(jnp.int32, (span, count), 1)
    out[0] = dot((rank[...] == place).astype(BF16), source[...]).astype(BF16)


def unsort_call(me, rank_col, n, array):
    count, width = array.shape
    span = count // n
    return pl.pallas_call(
        unsort_kernel,
        grid_spec=pltpu.PrefetchScalarGridSpec(
            num_scalar_prefetch=1,
            grid=(n,),
            in_specs=[pl.BlockSpec((span, 1), lambda i, m: (i, 0)), whole((count, width))],
            out_specs=pl.BlockSpec((1, span, width), lambda i, m: (m[0] ^ i, 0, 0)),
        ),
        out_shape=jax.ShapeDtypeStruct((n, span, width), BF16),
        compiler_params=pltpu.CompilerParams(vmem_limit_bytes=VMEM),
        cost_estimate=QUICK,
        name="unsort",
    )(me, rank_col, array)


VECTORS = 128


def input_weights_kernel(core, normed, grads, first, second, third, up_sums, send, keep):
    mid, width = normed.shape[1], grads.shape[2]
    h = core[0] ^ 1 ^ pl.program_id(0)

    def write(out):
        for j in range(3):
            out[:, j * width : (j + 1) * width] = dot_tn(normed[...], grads[j]).astype(BF16)
        rows = [first[0:3, :], second[0:3, :], third[0:1, :]]
        for i in range(up_sums.shape[1] // width):
            rows.append(up_sums[:, pl.ds(pl.multiple_of(i * width + h * mid, 128), mid)])
        count = sum(row.shape[0] for row in rows)
        rows.append(jnp.zeros((VECTORS - count, mid), F32))
        out[:, 3 * width :] = jnp.concatenate(rows, axis=0).T.astype(BF16)

    pl.when(pl.program_id(0) == 0)(lambda: write(send))
    pl.when(pl.program_id(0) == 1)(lambda: write(keep))


def input_weights_call(core, normed, grads, first, second, third, up_sums):
    count, width = normed.shape
    half = jax.ShapeDtypeStruct((width // 2, 3 * width + VECTORS), BF16)
    rows = pl.BlockSpec((count, width // 2), lambda i, c: (0, c[0] ^ 1 ^ i))
    vector = pl.BlockSpec((8, width // 2), lambda i, c: (0, c[0] ^ 1 ^ i))
    return pl.pallas_call(
        input_weights_kernel,
        grid_spec=pltpu.PrefetchScalarGridSpec(
            num_scalar_prefetch=1,
            grid=(2,),
            in_specs=[rows, whole(grads.shape), vector, vector, vector, whole(up_sums.shape)],
            out_specs=[whole(half.shape)] * 2,
        ),
        out_shape=[half] * 2,
        compiler_params=pltpu.CompilerParams(vmem_limit_bytes=VMEM),
        cost_estimate=QUICK,
        name="input_weights",
    )(core, normed, grads, first, second, third, up_sums)


GROUPS = 4


def final_call(core, turns, blocks, groups, pieces, name, spread, outs, scratch=(), finish=None):
    size = blocks // groups
    rows = pieces[0].shape[0] // (blocks // 2)
    whole_tile = 1 if rows % 16 == 0 else 2

    def kernel(c, t, *refs):
        h, g = pl.program_id(0), pl.program_id(1)
        active = (h * groups + g) // (groups // 2)
        turn = t[h]
        place = g ^ (turn // size)

        def write(source):
            for j in range(0, size, whole_tile):
                part = source[j * rows : (j + whole_tile) * rows, :].astype(F32)
                for i in range(whole_tile):
                    spread(part[i * rows : (i + 1) * rows], (j + i) ^ (turn % size), place, refs[4:])

        for q in range(4):
            pl.when(active == q)(functools.partial(write, refs[q]))
        if finish is not None:
            pl.when(g == groups - 1)(lambda: finish(refs[4:]))

    def in_spec(q):
        def index(h, g, c, t):
            return jnp.clip(h * groups + g - q * (groups // 2), 0, groups // 2 - 1), 0

        return pl.BlockSpec((size * rows, pieces[q].shape[1]), index)

    def out_spec(block, index):
        return pl.BlockSpec(block, lambda h, g, c, t: index(h ^ c[0], g, lambda n: n ^ (t[h] // size)))

    return pl.pallas_call(
        kernel,
        grid_spec=pltpu.PrefetchScalarGridSpec(
            num_scalar_prefetch=2,
            grid=(2, groups),
            in_specs=[in_spec(q) for q in range(4)],
            out_specs=[out_spec(block, index) for _, block, index in outs],
            scratch_shapes=list(scratch),
        ),
        out_shape=[jax.ShapeDtypeStruct(shape, F32) for shape, _, _ in outs],
        compiler_params=pltpu.CompilerParams(vmem_limit_bytes=VMEM),
        cost_estimate=QUICK,
        name=name,
    )(core, turns, *pieces)


def rows_at(ref, place, value):
    rows = value.shape[0]
    ref[pl.ds(pl.multiple_of(place * rows, 8), rows), :] = value


def down_final(core, turns, blocks, pieces, ff):
    rows, width = pieces[0].shape[0] // (blocks // 2), pieces[0].shape[1]
    size = blocks // GROUPS * rows

    def spread(block, j, place, refs):
        @pl.when(place < GROUPS - 1)
        def _():
            rows_at(refs[0], j, block)

        @pl.when((place == GROUPS - 1) & (j * rows < width // 2))
        def _():
            rows_at(refs[1], j, block)

    def down_index(h, g, place):
        at = place(g)
        near = place(jnp.where(g == 0, 1, g - 1))
        return h * (GROUPS - 1) + jnp.where(at == GROUPS - 1, near, at), 0

    outs = [
        ((ff, width), (size, width), down_index),
        ((width, width), (width // 2, width), lambda h, g, place: (h, 0)),
    ]
    return final_call(core, turns, blocks, GROUPS, pieces, "down_final", spread, outs)


def up_final(core, turns, blocks, pieces):
    rows, cols = pieces[0].shape[0] * 2, pieces[0].shape[1]

    def spread(block, j, place, refs):
        rows_at(refs[0], j, block)

    outs = [((rows, 2 * cols), (rows // 2, cols), lambda h, g, place: (place(g), h))]
    return final_call(core, turns, blocks, 2, pieces, "up_final", spread, outs)[0]


def input_final(core, turns, blocks, pieces):
    width, cols = pieces[0].shape[0] * 4, pieces[0].shape[1]
    n, half = cols - 3 * width, width // 2

    def spread(block, j, place, refs):
        rows_at(refs[0], j, block[:, : 3 * width])
        rows_at(refs[2], place * (blocks // 2) + j, block[:, 3 * width :])

    def finish(refs):
        refs[1][...] = refs[2][...].T

    outs = [
        ((width, 3 * width), (half // 2, 3 * width), lambda h, g, place: (h * 2 + place(g), 0)),
        ((n, width), (n, half), lambda h, g, place: (0, h)),
    ]
    scratch = [pltpu.VMEM((half, n), F32)]
    return final_call(core, turns, blocks, 2, pieces, "input_final", spread, outs, scratch, finish)


def copy_kernel(source, out):
    out[...] = source[...]


def copy_call(array):
    spec = pl.BlockSpec((1, *array.shape[1:]), lambda i: (i, 0, 0))
    return pl.pallas_call(
        copy_kernel,
        grid=(array.shape[0],),
        in_specs=[spec],
        out_specs=spec,
        out_shape=jax.ShapeDtypeStruct(array.shape, array.dtype),
        compiler_params=pltpu.CompilerParams(vmem_limit_bytes=VMEM),
        cost_estimate=QUICK,
        name="copy",
    )(array)


MICRO = 2


def from_behind(value, axis, steps):
    count = lax.axis_size(axis)
    pairs = [(source, (source + steps) % count) for source in range(count)]
    return lax.ppermute(value, axis, pairs)


def norm_rows(values, gain, shift):
    centre = values - jnp.mean(values, axis=-1, keepdims=True)
    spread = jnp.mean(centre * centre, axis=-1, keepdims=True)
    return centre * lax.rsqrt(spread + eps_norm) * gain + shift


def gelu_exact(values):
    return jax.nn.gelu(values, approximate=False)


def split_heads(block):
    return block.reshape(block.shape[0], block.shape[1], HEADS, HEAD_DIM)


def take_rows(array, first_row, count_rows):
    return lax.slice_in_dim(array, first_row, first_row + count_rows, axis=0)


def masked_scores(query, keys, ids_query, ids_keys):
    scores = jnp.einsum(
        "rqhd,rkhd->rhqk", split_heads(query), split_heads(keys), preferred_element_type=jnp.float32
    ) * HEAD_DIM ** (-0.5)
    same = ids_query[:, None, :, None] == ids_keys[:, None, None, :]
    return jnp.where(same, scores, -jnp.inf)


def attend_piece(carry, query, ids_query, piece):
    keys, values, ids_keys = piece
    peak, total, accum = carry
    scores = masked_scores(query, keys, ids_query, ids_keys)
    top = jnp.maximum(peak, jnp.max(scores, axis=-1))
    weights = jnp.exp(scores - top[..., None])
    total = jnp.sum(weights, axis=-1)
    update = jnp.einsum(
        "rhqk,rkhd->rqhd",
        weights.astype(jnp.bfloat16),
        split_heads(values),
        preferred_element_type=jnp.float32,
    )
    return (top, total, update.reshape(accum.shape))


def attention_forward(query, keys, values, ids_query):
    rows_here, slots, width = query.shape
    start_state = (
        jnp.full((rows_here, HEADS, slots), -1e30, jnp.float32),
        jnp.zeros((rows_here, HEADS, slots), jnp.float32),
        jnp.zeros((rows_here, slots, width), jnp.float32),
    )
    carry = attend_piece(
        start_state,
        query,
        ids_query,
        (
            lax.all_gather(keys, "blk", axis=1, tiled=True),
            lax.all_gather(values, "blk", axis=1, tiled=True),
            lax.all_gather(ids_query, "blk", axis=1, tiled=True),
        ),
    )
    return (carry[0], carry[1], carry[2], None)


def attention_back(query, out_grad, ids_query, log_total, inner, piece):
    keys, values, ids_keys = piece
    scale = HEAD_DIM ** (-0.5)
    scores = masked_scores(query, keys, ids_query, ids_keys)
    probs = jnp.exp(scores - log_total[..., None])
    prob_grad = jnp.einsum(
        "rqhd,rkhd->rhqk",
        split_heads(out_grad),
        split_heads(values),
        preferred_element_type=jnp.float32,
    )
    score_grad = (probs * (prob_grad - inner[..., None])).astype(jnp.bfloat16)
    value_grad = jnp.einsum(
        "rhqk,rqhd->rkhd",
        probs.astype(jnp.bfloat16),
        split_heads(out_grad),
        preferred_element_type=jnp.float32,
    )
    key_grad = (
        jnp.einsum(
            "rhqk,rqhd->rkhd", score_grad, split_heads(query), preferred_element_type=jnp.float32
        )
        * scale
    )
    query_grad = (
        jnp.einsum(
            "rhqk,rkhd->rqhd", score_grad, split_heads(keys), preferred_element_type=jnp.float32
        )
        * scale
    )
    return (
        query_grad.reshape(query.shape),
        key_grad.reshape(keys.shape),
        value_grad.reshape(values.shape),
    )


def local(
    inputs,
    image_index,
    keep_mask,
    first_gain,
    first_shift,
    input_weight,
    input_bias,
    output_weight,
    output_bias,
    second_gain,
    second_shift,
    up_weight,
    up_bias,
    down_weight,
    down_bias,
    cotangent,
):
    rows_local, slots, width = inputs.shape
    rows_micro = rows_local // MICRO
    count = rows_micro * slots
    blocks = lax.axis_size("blk")
    params = (
        first_gain,
        first_shift,
        input_weight,
        input_bias,
        output_weight,
        output_bias,
        second_gain,
        second_shift,
        up_weight,
        up_bias,
        down_weight,
        down_bias,
    )
    sums = [jnp.zeros(item.shape, jnp.float32) for item in params]
    results = []
    input_grads = []
    for micro in range(MICRO):
        first_row = micro * rows_micro
        rows_in = take_rows(inputs, first_row, rows_micro).astype(jnp.float32).reshape(count, width)
        out_cot = (
            take_rows(cotangent, first_row, rows_micro).astype(jnp.float32).reshape(count, width)
        )
        ids_query = take_rows(image_index, first_row, rows_micro).astype(jnp.bfloat16)
        keep = take_rows(keep_mask, first_row, rows_micro).astype(jnp.float32) / keep_rate
        keep_attn = jnp.broadcast_to(keep[:, None, 0:1], (rows_micro, slots, 1)).reshape(count, 1)
        keep_mlp = jnp.broadcast_to(keep[:, None, 1:2], (rows_micro, slots, 1)).reshape(count, 1)
        normed = norm_rows(rows_in, first_gain, first_shift).astype(jnp.bfloat16)
        mixed = jnp.dot(normed, input_weight, preferred_element_type=jnp.float32)
        query = (
            (mixed[:, :width] + input_bias[0])
            .astype(jnp.bfloat16)
            .reshape(rows_micro, slots, width)
        )
        keys = mixed[:, width : 2 * width].astype(jnp.bfloat16).reshape(rows_micro, slots, width)
        values = (
            (mixed[:, 2 * width :] + input_bias[1])
            .astype(jnp.bfloat16)
            .reshape(rows_micro, slots, width)
        )
        top, total, accum, whole = attention_forward(query, keys, values, ids_query)
        attended = (split_heads(accum) / jnp.transpose(total, (0, 2, 1))[..., None]).reshape(
            count, width
        )
        log_total = top + jnp.log(total)
        attended_low = attended.astype(jnp.bfloat16)
        branch = (
            jnp.dot(attended_low, output_weight, preferred_element_type=jnp.float32) + output_bias
        )
        middle = rows_in + keep_attn * branch
        normed_second = norm_rows(middle, second_gain, second_shift).astype(jnp.bfloat16)
        hidden = jnp.dot(normed_second, up_weight, preferred_element_type=jnp.float32) + up_bias
        active = gelu_exact(hidden).astype(jnp.bfloat16)
        branch_second = jnp.dot(active, down_weight, preferred_element_type=jnp.float32) + down_bias
        results.append(
            (middle + keep_mlp * branch_second)
            .astype(jnp.bfloat16)
            .reshape(rows_micro, slots, width)
        )
        mlp_grad = (out_cot * keep_mlp).astype(jnp.bfloat16)
        sums[10] = sums[10] + jnp.dot(active.T, mlp_grad, preferred_element_type=jnp.float32)
        sums[11] = sums[11] + jnp.sum(mlp_grad.astype(jnp.float32), axis=0)
        active_grad = jnp.dot(mlp_grad, down_weight.T, preferred_element_type=jnp.float32)
        hidden_grad = jax.vjp(gelu_exact, hidden)[1](active_grad)[0].astype(jnp.bfloat16)
        sums[8] = sums[8] + jnp.dot(
            normed_second.T, hidden_grad, preferred_element_type=jnp.float32
        )
        sums[9] = sums[9] + jnp.sum(hidden_grad.astype(jnp.float32), axis=0)
        second_in_grad = jnp.dot(hidden_grad, up_weight.T, preferred_element_type=jnp.float32)
        middle_part, second_gain_part, second_shift_part = jax.vjp(
            norm_rows, middle, second_gain, second_shift
        )[1](second_in_grad)
        sums[6] = sums[6] + second_gain_part
        sums[7] = sums[7] + second_shift_part
        middle_grad = middle_part + out_cot
        branch_grad = (middle_grad * keep_attn).astype(jnp.bfloat16)
        sums[4] = sums[4] + jnp.dot(attended_low.T, branch_grad, preferred_element_type=jnp.float32)
        sums[5] = sums[5] + jnp.sum(branch_grad.astype(jnp.float32), axis=0)
        attended_grad = jnp.dot(
            branch_grad, output_weight.T, preferred_element_type=jnp.float32
        ).astype(jnp.bfloat16)
        out_grad = attended_grad.reshape(rows_micro, slots, width)
        inner = jnp.transpose(
            jnp.sum(
                split_heads(
                    (attended_grad.astype(jnp.float32) * attended).reshape(rows_micro, slots, width)
                ),
                axis=-1,
            ),
            (0, 2, 1),
        )
        query_grad = jnp.zeros((rows_micro, slots, width), jnp.float32)
        visiting = (keys, values, ids_query)
        key_grad = jnp.zeros((rows_micro, slots, width), jnp.float32)
        value_grad = jnp.zeros((rows_micro, slots, width), jnp.float32)
        for step in range(blocks):
            query_part, key_part, value_part = attention_back(
                query, out_grad, ids_query, log_total, inner, visiting
            )
            query_grad = query_grad + query_part
            key_grad, value_grad = (
                from_behind((key_grad + key_part).astype(jnp.bfloat16), "blk", 1).astype(
                    jnp.float32
                ),
                from_behind((value_grad + value_part).astype(jnp.bfloat16), "blk", 1).astype(
                    jnp.float32
                ),
            )
            if step + 1 < blocks:
                visiting = from_behind((visiting[0], visiting[1], visiting[2]), "blk", 1)
        joined_grad = (
            jnp.concatenate([query_grad, key_grad, value_grad], axis=-1)
            .astype(jnp.bfloat16)
            .reshape(count, 3 * width)
        )
        sums[2] = sums[2] + jnp.dot(normed.T, joined_grad, preferred_element_type=jnp.float32)
        joined_sums = jnp.sum(joined_grad.astype(jnp.float32), axis=0)
        sums[3] = sums[3] + jnp.stack([joined_sums[:width], joined_sums[2 * width :]])
        first_in_grad = jnp.dot(joined_grad, input_weight.T, preferred_element_type=jnp.float32)
        rows_part, first_gain_part, first_shift_part = jax.vjp(
            norm_rows, rows_in, first_gain, first_shift
        )[1](first_in_grad)
        sums[0] = sums[0] + first_gain_part
        sums[1] = sums[1] + first_shift_part
        input_grads.append(
            (rows_part + middle_grad).astype(jnp.bfloat16).reshape(rows_micro, slots, width)
        )
    totals = lax.psum(
        (
            sums[0],
            sums[1],
            sums[2],
            sums[3],
            sums[4],
            sums[5],
            sums[6],
            sums[7],
            sums[8],
            sums[9],
            sums[10],
            sums[11],
        ),
        ("rows", "blk"),
    )
    return (
        jnp.concatenate(results, axis=0),
        jnp.concatenate(input_grads, axis=0),
        totals[0],
        totals[1],
        totals[2],
        totals[3],
        totals[4],
        totals[5],
        totals[6],
        totals[7],
        totals[8],
        totals[9],
        totals[10],
        totals[11],
    )


def swap(value, axis, bit):
    return lax.ppermute(value, axis, [(i, i ^ bit) for i in range(lax.axis_size(axis))])


def side(axis, bit):
    return (lax.axis_index(axis) // bit) % 2


def after(value, *others):
    return lax.optimization_barrier((value, *others))[0]


def axis_bits(axis):
    bits, bit = [], 1
    while bit < lax.axis_size(axis):
        bits.append((axis, bit))
        bit *= 2
    return bits


def add_low(a, b):
    return (a.astype(F32) + b.astype(F32)).astype(BF16)


def swap_two(value, step):
    rows, blocks = lax.axis_size("rows"), lax.axis_size("blk")
    pairs = []
    for r in range(rows):
        for b in range(blocks):
            axis, bit = step[b % 2]
            other = (r ^ bit, b) if axis == "rows" else (r, b ^ bit)
            pairs.append((r * blocks + b, other[0] * blocks + other[1]))
    return lax.ppermute(value, ("rows", "blk"), pairs)


def side_two(step):
    return jnp.where(side("blk", 1) == 0, side(*step[0]), side(*step[1]))


class Order:
    def __init__(self):
        self.last = ()

    def hold(self, value):
        return after(value, *self.last) if self.last else value

    def advance(self, *parts):
        parts = [part for part in parts if part.result is None]
        if parts:
            held = lax.optimization_barrier(([part.recv for part in parts], self.last))[0]
            self.done(*[value for part, recv in zip(parts, held) for value in part.step(recv)])

    def done(self, *values):
        self.last = values
        return values[0] if len(values) == 1 else values


class Chain:
    def __init__(self, steps, send, keep):
        self.steps, self.at = steps, -1
        self.recv, self.keep, self.result = send, keep, None

    def step(self, recv):
        keep, n = self.keep, len(self.steps)
        if self.at < 0:
            send, self.recv = recv, swap(recv, "blk", 1)
        elif self.at < n:
            step = self.steps[self.at]
            half = keep.shape[0] // 2
            own = side_two(step)

            def part(which):
                return add_low(
                    lax.dynamic_slice_in_dim(keep, which * half, half, 0),
                    lax.dynamic_slice_in_dim(recv, which * half, half, 0),
                )

            send, self.keep = part(1 - own), part(own)
            self.recv = swap_two(send, step)
        elif self.at < 2 * n:
            send = add_low(keep, recv) if self.at == n else jnp.concatenate([keep, recv], axis=0)
            send = self.keep = lax.optimization_barrier(send)
            self.recv = swap_two(send, self.steps[2 * n - 1 - self.at])
        elif self.at == 2 * n:
            self.at, self.keep, self.recv = self.at + 1, (keep, recv), [swap(piece, "blk", 1) for piece in (keep, recv)]
            return keep, recv
        else:
            self.result, self.recv = (*keep, *recv), None
            return ()
        self.at += 1
        return send, self.keep


class Small:
    def __init__(self, value):
        count = lax.axis_size("rows") * lax.axis_size("blk")
        self.recv, self.result, self.sent = jnp.broadcast_to(value[None], (count, *value.shape)), None, False

    def step(self, recv):
        if not self.sent:
            self.recv, self.sent = lax.all_to_all(recv, ("rows", "blk"), 0, 0), True
            return (recv,)
        self.result, self.recv = jnp.sum(recv, axis=0), None
        return (self.result,)


class Home:
    def __init__(self, pieces):
        self.recv, self.result, self.sent = pieces, None, False

    def step(self, recv):
        if not self.sent:
            self.recv, self.sent = lax.all_to_all(recv, "blk", 0, 0), True
        else:
            self.result, self.recv = recv, None
        return (recv,)


def block_turns(steps):
    core = side("blk", 1)
    turns = []
    for c in range(2):
        turn = 0
        for step in steps:
            turn = turn * 2 + side(*step[c])
        turns.append(turn)
    first, second = jnp.where(core == 0, turns[0], turns[1]), jnp.where(core == 0, turns[1], turns[0])
    return core.astype(jnp.int32).reshape(1), jnp.stack([first, second]).astype(jnp.int32), 1 << len(steps)


def local_rows(
    inputs,
    image_index,
    keep_mask,
    first_gain,
    first_shift,
    input_weight,
    input_bias,
    output_weight,
    output_bias,
    second_gain,
    second_shift,
    up_weight,
    up_bias,
    down_weight,
    down_bias,
    cotangent,
):
    blocks, span, width = inputs.shape
    ff = up_weight.shape[1]
    me = lax.axis_index("blk")

    def row_piece(array, s):
        return lax.dynamic_index_in_dim(array, me ^ s, 0, keepdims=False)

    xs_send = [row_piece(inputs, s) for s in range(1, blocks)]
    xs_in = [row_piece(after(inputs, *xs_send), 0)] + [swap(x, "blk", s + 1) for s, x in enumerate(xs_send)]
    ids = [row_piece(image_index, 0)] + [
        swap(row_piece(after(image_index, *xs_send), s), "blk", s) for s in range(1, blocks)
    ]
    cots = [row_piece(cotangent, 0)] + [
        swap(after(row_piece(cotangent, s), *xs_send), "blk", s) for s in range(1, blocks)
    ]
    ids = jnp.concatenate(ids)
    image = jnp.where(ids < 0, 4, ids)
    order_key = image * ids.shape[0] + jnp.arange(ids.shape[0], dtype=jnp.int32)
    less = (order_key[None, :] < order_key[:, None]).astype(jnp.int32)
    rank = jnp.sum(less, axis=1)
    starts = jnp.sum((image[None, :] < jnp.arange(6, dtype=jnp.int32)[:, None]).astype(jnp.int32), axis=1)
    keep = lax.dynamic_index_in_dim(keep_mask, me, 0, keepdims=False).astype(F32) / keep_rate
    rank_row, rank_col = rank[None, :], rank[:, None]

    bias = jnp.stack([input_bias[0], jnp.zeros_like(input_bias[0]), input_bias[1]])
    xs, normed, qkv = qkv_call(rank_row, xs_in, first_gain[None], first_shift[None], input_weight, bias)
    attended, stat, att_low = forward_call(starts, qkv)
    vectors = jnp.stack([output_bias, second_gain, second_shift, down_bias])
    core = side("blk", 1).astype(jnp.int32).reshape(1)
    cot, middle, normed2, mlp_grad, sums_mid = middle_call(
        keep, rank_row, cots, att_low, xs, output_weight, vectors
    )
    (up_send, up_keep, down_send, down_keep, up_sums, result, middle_grad, branch, att_grad, sums2) = mlp_call(
        core, keep, normed2, mlp_grad, middle, cot, att_low, output_weight, vectors, up_weight, up_bias[None], down_weight
    )

    y, x, z = axis_bits("blk")[1], axis_bits("rows")[0], axis_bits("rows")[1:]
    far = [(d, d) for d in z[1:]]
    xy = [(x, y), (y, x), (z[0], z[0])] + far
    zx = [(z[0], z[0]), (x, y), (y, x)] + far
    order = Order()
    order.done(att_grad)
    up_chain, down_chain = Chain(zx, up_send, up_keep), Chain(xy, down_send, down_keep)

    order.advance(up_chain, down_chain)
    result_home = Home(order.done(unsort_call(me.reshape(1), rank_col, blocks, order.hold(result))))
    order.advance(up_chain, down_chain, result_home)
    grads, bias_sums = backward_call(starts, qkv, order.hold(att_grad), attended, stat, 0, PAIRS)
    order.done(grads)
    order.advance(up_chain, down_chain, result_home)
    input_chain = Chain(
        xy, *order.done(*input_weights_call(core, order.hold(normed), grads, bias_sums, sums2, sums_mid, up_sums))
    )
    order.advance(input_chain, up_chain, down_chain)
    inputs_grad, sums1 = order.done(*input_call(grads, input_weight, xs, order.hold(middle_grad), first_gain[None]))
    small = Small(sums1[:2])
    order.advance(input_chain, up_chain, down_chain, small)
    home = Home(order.done(unsort_call(me.reshape(1), rank_col, blocks, order.hold(inputs_grad))))
    order.advance(input_chain, up_chain, down_chain, small, home)
    order.advance(input_chain, up_chain, down_chain)
    order.advance(input_chain, up_chain, down_chain, home)
    while down_chain.at < 2 * len(xy):
        order.advance(input_chain, up_chain, down_chain)
    result_out = order.done(copy_call(order.hold(result_home.result)))
    inputs_out = order.done(copy_call(order.hold(home.result)))
    order.advance(input_chain, up_chain, down_chain)
    order.advance(input_chain, up_chain, down_chain)
    up_total = order.done(up_final(*block_turns(zx), (order.hold(up_chain.result[0]), *up_chain.result[1:])))
    order.advance(input_chain)
    down_total, out_total = order.done(
        *down_final(*block_turns(xy), (order.hold(down_chain.result[0]), *down_chain.result[1:]), ff)
    )
    while input_chain.result is None:
        order.advance(input_chain)
    input_total, sums = input_final(*block_turns(xy), input_chain.result)
    sums = jnp.concatenate([small.result, sums[:16]])

    return (
        result_out,
        inputs_out,
        sums[0],
        sums[1],
        input_total,
        jnp.stack([sums[2], sums[4]]),
        out_total,
        sums[7],
        sums[5],
        sums[6],
        up_total,
        sums[9:13].reshape(ff),
        down_total,
        sums[8],
    )


def solution(mesh):
    blocks, groups = mesh.shape["blk"], mesh.shape["rows"]

    def run(*args):
        whole_rows = args[0].shape[0] // groups == blocks == 4 and groups in (4, 8, 16)
        return jax.shard_map(
            local_rows if whole_rows else local,
            mesh=mesh,
            in_specs=(P("rows", "blk", None), P("rows", "blk"), P("rows", None)) + (P(),) * 12 + (P("rows", "blk", None),),
            out_specs=(P("rows", "blk", None),) * 2 + (P(),) * 12,
            check_vma=False,
        )(*args)

    return run
```

```python
import functools

import jax
import jax.numpy as jnp
from jax import lax
from jax.experimental import pallas as pl
from jax.experimental.pallas import tpu as pltpu
from jax.sharding import PartitionSpec as P

HEADS = 12
HEAD_DIM = 64
PAIR = 2 * HEAD_DIM
PAIRS = HEADS // 2
eps_norm = 1e-06
keep_rate = 0.9
F32 = jnp.float32
BF16 = jnp.bfloat16
NEG = -1e30
VMEM = 62 * 1024 * 1024
QUICK = pl.CostEstimate(flops=1 << 20, bytes_accessed=1 << 16, transcendentals=0)


def dot(a, b):
    return jnp.dot(a, b, preferred_element_type=F32)


def dot_nt(a, b):
    return lax.dot_general(a, b, (((1,), (1,)), ((), ())), preferred_element_type=F32)


def dot_tn(a, b):
    return lax.dot_general(a, b, (((0,), (0,)), ((), ())), preferred_element_type=F32)


def whole(shape):
    return pl.BlockSpec(shape, lambda *g: (0,) * len(shape), pipeline_mode=pl.Buffered(1))


def centre_scale(values):
    centre = values - jnp.mean(values, axis=-1, keepdims=True)
    spread = jnp.mean(centre * centre, axis=-1, keepdims=True)
    inv = lax.rsqrt(spread + eps_norm)
    return centre * inv, inv


def norm_back(grad_hat, hat, inv):
    first = jnp.mean(grad_hat, axis=-1, keepdims=True)
    second = jnp.mean(grad_hat * hat, axis=-1, keepdims=True)
    return (grad_hat - first - hat * second) * inv


def gather_pieces(step, pieces, row):
    @pl.when(step == 0)
    def _():
        span = pieces[0].shape[0]
        for i, piece in enumerate(pieces):
            row[i * span : (i + 1) * span, :] = piece[...]


def sort_tile(rank_row, tile, step, row):
    place = step * tile + lax.broadcasted_iota(jnp.int32, (tile, row.shape[0]), 0)
    return dot((rank_row == place).astype(BF16), row[...])


def qkv_kernel(n, tile, *refs):
    rank, *pieces = refs[: n + 1]
    gain, shift, weight, bias, xs_out, normed_out, qkv_out, row = refs[n + 1 :]
    gather_pieces(pl.program_id(0), pieces, row)
    xs = sort_tile(rank[...], tile, pl.program_id(0), row)
    xs_out[...] = xs.astype(BF16)
    hat, _ = centre_scale(xs)
    normed = (hat * gain[...] + shift[...]).astype(BF16)
    normed_out[...] = normed
    width = normed.shape[1]
    for j in range(3):
        cols = slice(j * width, (j + 1) * width)
        mixed = (dot(normed, weight[:, cols]) + bias[j : j + 1, :]).astype(BF16)
        qkv_out[j] = mixed * BF16(HEAD_DIM**-0.5) if j == 0 else mixed


def qkv_call(rank, pieces, gain, shift, weight, bias, tile=384):
    n = len(pieces)
    span, width = pieces[0].shape
    count = n * span
    return pl.pallas_call(
        functools.partial(qkv_kernel, n, tile),
        grid=(count // tile,),
        in_specs=[whole((1, count))]
        + [whole((span, width))] * n
        + [whole((1, width)), whole((1, width)), whole(weight.shape), whole(bias.shape)],
        out_specs=[
            pl.BlockSpec((tile, width), lambda i: (i, 0)),
            pl.BlockSpec((tile, width), lambda i: (i, 0)),
            pl.BlockSpec((3, tile, width), lambda i: (0, i, 0)),
        ],
        out_shape=[
            jax.ShapeDtypeStruct((count, width), BF16),
            jax.ShapeDtypeStruct((count, width), BF16),
            jax.ShapeDtypeStruct((3, count, width), BF16),
        ],
        scratch_shapes=[pltpu.VMEM((count, width), BF16)],
        compiler_params=pltpu.CompilerParams(vmem_limit_bytes=VMEM),
        cost_estimate=QUICK,
        name="sort_qkv",
    )(rank, *pieces, gain, shift, weight, bias)


SMALL = 304
LARGE = 384


def windows(starts, seg, length):
    first, last = starts[seg], starts[seg + 1]
    aligned = first // 16 * 16
    small = SMALL if seg < 4 else LARGE
    at_small = pl.multiple_of(jnp.minimum(aligned, length - small), 16)
    at_large = pl.multiple_of(jnp.minimum(aligned, length - LARGE), 16)
    return first, last, small, at_small, at_large


def inside(at, size, lanes, first, last):
    place = at + lax.broadcasted_iota(jnp.int32, (size, lanes), 0)
    return (place >= first) & (place < last)


def forward_kernel(starts, qkv, out, stat, low_out):
    length = qkv.shape[1]
    for seg in range(5):
        first, last, small, at_q, at_k = windows(starts, seg, length)
        rows_q = pl.ds(at_q, small)
        q = qkv[0, rows_q, :]
        k = qkv[1, pl.ds(at_k, LARGE), :]
        v = qkv[2, pl.ds(at_k, LARGE), :]
        lane = lax.broadcasted_iota(jnp.int32, (LARGE, PAIR), 1)
        lane_q = lax.broadcasted_iota(jnp.int32, (small, PAIR), 1)
        low = lane < HEAD_DIM
        seen = inside(at_k, LARGE, PAIR, first, last)
        zero = jnp.zeros((LARGE, PAIR), BF16)
        one = jnp.ones((LARGE, PAIR), BF16)
        bias = jnp.where((lane == 0) & ~seen, NEG, 0.0).astype(BF16)
        q_ext = jnp.concatenate([q, (lane_q == 0).astype(BF16)], axis=1)
        halves = (low, ~low)
        k_ext = [jnp.concatenate([jnp.where(half, k, zero), bias], axis=1) for half in halves]
        mixes = [
            jnp.concatenate([jnp.where(half, v, zero), jnp.where(half, one, zero)], axis=1) for half in halves
        ]
        pair = dot_nt(q_ext, jnp.concatenate(k_ext, axis=0))
        tops, weights = [], []
        for h in range(2):
            scores = pair[:, h * LARGE : (h + 1) * LARGE]
            top = jnp.max(scores, axis=-1, keepdims=True)
            tops.append(top)
            weights.append(jnp.exp(scores - top).astype(BF16))
        both = dot(jnp.concatenate(weights, axis=1), jnp.concatenate(mixes, axis=0))
        total = both[:, PAIR:]
        peak = jnp.where(lane_q < HEAD_DIM, tops[0], tops[1])
        mine = inside(at_q, small, PAIR, first, last)
        out[rows_q, :] = jnp.where(mine, both[:, :PAIR] / total, out[rows_q, :])
        stat[rows_q, :] = jnp.where(mine, peak + jnp.log(total), stat[rows_q, :])
    low_out[...] = out[...].astype(BF16)


def forward_call(starts, qkv):
    _, count, wide = qkv.shape
    pairs = wide // PAIR
    return pl.pallas_call(
        forward_kernel,
        grid_spec=pltpu.PrefetchScalarGridSpec(
            num_scalar_prefetch=1,
            grid=(pairs,),
            in_specs=[pl.BlockSpec((3, count, PAIR), lambda p, s: (0, 0, p))],
            out_specs=[pl.BlockSpec((count, PAIR), lambda p, s: (0, p))] * 3,
        ),
        out_shape=[jax.ShapeDtypeStruct((count, pairs * PAIR), dtype) for dtype in (F32, F32, BF16)],
        compiler_params=pltpu.CompilerParams(vmem_limit_bytes=VMEM),
        cost_estimate=QUICK,
        name="attention_forward",
    )(starts, qkv)


def split3(value):
    high = value.astype(BF16)
    rest = value - high.astype(F32)
    mid = rest.astype(BF16)
    return high, mid, (rest - mid.astype(F32)).astype(BF16)


def backward_kernel(starts, qkv, grad, att, stat, *refs):
    out, sums = refs[-2:]
    length = qkv.shape[1]
    third = lax.broadcasted_iota(jnp.int32, (PAIR, PAIR), 0) // HEAD_DIM
    block = (third == lax.broadcasted_iota(jnp.int32, (PAIR, PAIR), 1) // HEAD_DIM).astype(BF16)
    for seg in range(5):
        first, last, small, at_k, at_q = windows(starts, seg, length)
        rows_q, rows_k = pl.ds(at_q, LARGE), pl.ds(at_k, small)
        lane_q = lax.broadcasted_iota(jnp.int32, (LARGE, PAIR), 1)
        lane_k = lax.broadcasted_iota(jnp.int32, (small, PAIR), 1)
        spot_q, spot_k = lane_q % HEAD_DIM, lane_k % HEAD_DIM
        mine_q = inside(at_q, LARGE, PAIR, first, last)
        mine_k = inside(at_k, small, PAIR, first, last)
        zero_q = jnp.zeros((LARGE, PAIR), BF16)
        zero_k = jnp.zeros((small, PAIR), BF16)
        q = qkv[0, rows_q, :]
        k = jnp.where(mine_k, qkv[1, rows_k, :], zero_k)
        v = qkv[2, rows_k, :]
        g = jnp.where(mine_q, grad[rows_q, :], zero_q)
        prod = g.astype(F32) * jnp.where(mine_q, att[rows_q, :], 0.0)
        p_high = prod.astype(BF16)
        p_low = (prod - p_high.astype(F32)).astype(BF16)
        inner = dot(p_high, block) + dot(p_low, block)
        logs = jnp.where(mine_q, stat[rows_q, :], 0.0)

        def spread(value, fifth):
            a, b, c = split3(value)
            return jnp.where(
                spot_q == 0, a, jnp.where(spot_q == 1, b, jnp.where(spot_q == 2, c, fifth))
            )

        query_bias = jnp.where(mine_q, 0.0, NEG).astype(BF16)
        unit = jnp.ones((LARGE, PAIR), BF16)
        q_tail = spread(logs, jnp.where(spot_q == 3, unit, jnp.where(spot_q == 4, query_bias, zero_q)))
        g_tail = spread(inner, zero_q)
        key_bias = jnp.where(mine_k, 0.0, NEG).astype(BF16)
        minus = jnp.where(spot_k < 3, -1.0, 0.0).astype(BF16)
        k_tail = jnp.where(
            spot_k == 3, key_bias, jnp.where(spot_k == 4, jnp.ones((small, PAIR), BF16), minus)
        )
        heads_q = [lane_q // HEAD_DIM == h for h in range(2)]
        qs = [jnp.where(head, q, zero_q) for head in heads_q]
        gs = [jnp.where(head, g, zero_q) for head in heads_q]
        q_both = [jnp.concatenate([x, jnp.where(head, q_tail, zero_q)], axis=1) for x, head in zip(qs, heads_q)]
        g_both = [jnp.concatenate([x, jnp.where(head, g_tail, zero_q)], axis=1) for x, head in zip(gs, heads_q)]
        prob = jnp.exp(dot_nt(jnp.concatenate([k, k_tail], axis=1), jnp.concatenate(q_both, axis=0)))
        prob_grad = dot_nt(jnp.concatenate([v, minus], axis=1), jnp.concatenate(g_both, axis=0))
        score_grad = (prob * prob_grad).astype(BF16)
        value_grad = dot(prob.astype(BF16), jnp.concatenate(gs, axis=0))
        key_grad = dot(score_grad, jnp.concatenate(qs, axis=0))
        stacked = jnp.concatenate([score_grad[:, :LARGE], score_grad[:, LARGE:]], axis=0)
        ks = [jnp.where(lane_k // HEAD_DIM == h, k, zero_k) for h in range(2)]
        query_grad = dot_tn(stacked, jnp.concatenate(ks, axis=0))
        query_grad = (query_grad * HEAD_DIM**-0.5).astype(BF16)
        out[0, rows_q, :] = jnp.where(mine_q, query_grad, out[0, rows_q, :])
        out[1, rows_k, :] = jnp.where(mine_k, key_grad.astype(BF16), out[1, rows_k, :])
        out[2, rows_k, :] = jnp.where(mine_k, value_grad.astype(BF16), out[2, rows_k, :])
    for j in range(3):
        sums[j : j + 1, :] = jnp.sum(out[j].astype(F32), axis=0, keepdims=True)


def backward_call(starts, qkv, grad, att, stat, first_pair, pairs, before=None):
    _, count, width = qkv.shape
    held = [] if before is None else list(before)
    return pl.pallas_call(
        backward_kernel,
        grid_spec=pltpu.PrefetchScalarGridSpec(
            num_scalar_prefetch=1,
            grid=(pairs,),
            in_specs=[pl.BlockSpec((3, count, PAIR), lambda p, s: (0, 0, p + first_pair))]
            + [pl.BlockSpec((count, PAIR), lambda p, s: (0, p + first_pair))] * 3
            + [pl.BlockSpec(memory_space=pl.ANY)] * len(held),
            out_specs=[
                pl.BlockSpec((3, count, PAIR), lambda p, s: (0, 0, p + first_pair)),
                pl.BlockSpec((8, PAIR), lambda p, s: (0, p + first_pair)),
            ],
        ),
        out_shape=[
            jax.ShapeDtypeStruct((3, count, width), BF16),
            jax.ShapeDtypeStruct((8, width), F32),
        ],
        input_output_aliases={5: 0, 6: 1} if held else {},
        compiler_params=pltpu.CompilerParams(vmem_limit_bytes=VMEM),
        cost_estimate=QUICK,
        name="attention_backward",
    )(starts, qkv, grad, att, stat, *held)


HALF_ERF = tuple(0.5 * c for c in (0.254829592, -0.284496736, 1.421413741, -1.453152027, 1.061405429))
LOG2_E = 1.4426950408889634


def gelu_pair(u):
    size = jnp.abs(u)
    t = 1.0 / (1.0 + (0.3275911 * 0.5**0.5) * size)
    bell = jnp.exp2(u * u * (-0.5 * LOG2_E))
    poly = HALF_ERF[4] * t + HALF_ERF[3]
    for c in (HALF_ERF[2], HALF_ERF[1], HALF_ERF[0]):
        poly = poly * t + c
    tail = poly * t * bell
    phi = jnp.where(u < 0, tail, 1.0 - tail)
    return u * phi, phi + u * bell * 0.3989422804014327


def middle_kernel(n, tile, *refs):
    keep, rank, *pieces = refs[: n + 2]
    att, xs, out_w, vectors, cot_out, middle_out, normed_out, mlp_out, sums, row = refs[n + 2 :]
    step = pl.program_id(0)
    gather_pieces(step, pieces, row)
    cot = sort_tile(rank[...], tile, step, row)
    cot_out[...] = cot.astype(BF16)
    mlp_grad = (cot * keep[1]).astype(BF16)
    mlp_out[...] = mlp_grad
    middle = xs[...].astype(F32) + keep[0] * (dot(att[...], out_w[...]) + vectors[0:1, :])
    middle_out[...] = middle
    hat, _ = centre_scale(middle)
    normed_out[...] = (hat * vectors[1:2, :] + vectors[2:3, :]).astype(BF16)

    @pl.when(step == 0)
    def _():
        sums[...] = jnp.zeros_like(sums)

    sums[0:1, :] += jnp.sum(mlp_grad.astype(F32), axis=0, keepdims=True)


def middle_call(keep, rank, pieces, att, xs, out_w, vectors, tile=384):
    n = len(pieces)
    span, width = pieces[0].shape
    count = n * span
    rows = pl.BlockSpec((tile, width), lambda i: (i, 0))
    low, full = jax.ShapeDtypeStruct((count, width), BF16), jax.ShapeDtypeStruct((count, width), F32)
    return pl.pallas_call(
        functools.partial(middle_kernel, n, tile),
        grid=(count // tile,),
        in_specs=[pl.BlockSpec(memory_space=pltpu.SMEM), whole((1, count))]
        + [whole((span, width))] * n
        + [rows, rows, whole(out_w.shape), whole(vectors.shape)],
        out_specs=[rows] * 4 + [pl.BlockSpec((8, width), lambda i: (0, 0))],
        out_shape=[low, full, low, low, jax.ShapeDtypeStruct((8, width), F32)],
        scratch_shapes=[pltpu.VMEM((count, width), BF16)],
        compiler_params=pltpu.CompilerParams(vmem_limit_bytes=VMEM),
        cost_estimate=QUICK,
        name="middle",
    )(keep, rank, *pieces, att, xs, out_w, vectors)


def mlp_kernel(parts, core, keep, normed, mlp_grad, middle, cot, att, out_w, vectors, up_w, up_b, down_w, *refs):
    (
        up_send, up_keep, down_send, down_keep, up_sums, result, middle_grad_out, branch_out, att_grad_out, sums,
        lift, back, act_all, hidden_all,
    ) = refs
    step, half = pl.program_id(0), pl.num_programs(0) // 2
    count, width = normed.shape
    cuts = [slice(i * (count // parts), (i + 1) * (count // parts)) for i in range(parts)]

    @pl.when(step == 0)
    def _():
        lift[...] = jnp.zeros_like(lift)
        back[...] = jnp.zeros_like(back)

    @pl.when(step < 2 * half)
    def _():
        total = jnp.zeros(up_sums.shape, F32)
        ready = None
        for rows in cuts + [None]:
            fresh = None
            if rows is not None:
                u = dot(normed[rows, :], up_w[...]) + up_b[...]
                fresh = (rows, u, dot_nt(mlp_grad[rows, :], down_w[...]))
            if ready is not None:
                past, u, act_grad = ready
                act, slope = gelu_pair(u)
                act_all[past, :] = act.astype(BF16)
                hidden = (act_grad * slope).astype(BF16)
                hidden_all[past, :] = hidden
                total = total + jnp.sum(hidden.astype(F32), axis=0, keepdims=True)
            ready = fresh
        lift[...] += dot(act_all[...], down_w[...])
        back[...] += dot_nt(hidden_all[...], up_w[...])
        up_sums[...] = total
        up_part = dot_tn(normed[...], hidden_all[...]).astype(BF16)
        down_part = dot_tn(act_all[...], mlp_grad[...]).astype(BF16)

        @pl.when(step < half)
        def _():
            up_send[...] = up_part
            down_send[...] = down_part

        @pl.when(step >= half)
        def _():
            up_keep[...] = up_part
            down_keep[...] = down_part

    @pl.when(step == 2 * half)
    def _():
        gain, down_b = vectors[1:2, :], vectors[3:4, :]
        sums[...] = jnp.zeros_like(sums)
        for rows in cuts:
            mid, grad = middle[rows, :], back[rows, :]
            hat, inv = centre_scale(mid)
            result[rows, :] = (mid + keep[1] * (lift[rows, :] + down_b)).astype(BF16)
            middle_grad = cot[rows, :].astype(F32) + norm_back(grad * gain, hat, inv)
            middle_grad_out[rows, :] = middle_grad
            branch = (keep[0] * middle_grad).astype(BF16)
            branch_out[rows, :] = branch
            att_grad_out[rows, :] = dot_nt(branch, out_w[...]).astype(BF16)
            sums[0:1, :] += jnp.sum(grad * hat, axis=0, keepdims=True)
            sums[1:2, :] += jnp.sum(grad, axis=0, keepdims=True)
            sums[2:3, :] += jnp.sum(branch.astype(F32), axis=0, keepdims=True)
        for out, c in ((down_send, 1 - core[0]), (down_keep, core[0])):
            cols = pl.ds(pl.multiple_of(c * (width // 2), 128), width // 2)
            out[: width // 2, :] = dot_tn(att[:, cols], branch_out[...]).astype(BF16)
            out[width // 2 :, :] = jnp.zeros((out.shape[0] - width // 2, width), BF16)


def mlp_call(core, keep, normed, mlp_grad, middle, cot, att, out_w, vectors, up_w, up_b, down_w, chunk=512, parts=4):
    count, width = normed.shape
    ff = up_w.shape[1]
    half = ff // 2 // chunk

    def place(i, c):
        i = jnp.minimum(i, 2 * half - 1)
        return jnp.where(i < half, (1 - c[0]) * half + i, c[0] * half + i - half)

    def first(i):
        return jnp.minimum(i, half - 1)

    def second(i):
        return jnp.clip(i - half, 0, half - 1)

    def extra(i, index):
        return jnp.where(i == 2 * half, half, index)

    low, full = jax.ShapeDtypeStruct((count, width), BF16), jax.ShapeDtypeStruct((count, width), F32)
    return pl.pallas_call(
        functools.partial(mlp_kernel, parts),
        grid_spec=pltpu.PrefetchScalarGridSpec(
            num_scalar_prefetch=1,
            grid=(2 * half + 1,),
            in_specs=[pl.BlockSpec(memory_space=pltpu.SMEM)]
            + [whole((count, width))] * 5
            + [
                whole(out_w.shape),
                whole(vectors.shape),
                pl.BlockSpec((width, chunk), lambda i, c: (0, place(i, c))),
                pl.BlockSpec((1, chunk), lambda i, c: (0, place(i, c))),
                pl.BlockSpec((chunk, width), lambda i, c: (place(i, c), 0)),
            ],
            out_specs=[
                pl.BlockSpec((width, chunk), lambda i, c: (0, first(i))),
                pl.BlockSpec((width, chunk), lambda i, c: (0, second(i))),
                pl.BlockSpec((chunk, width), lambda i, c: (extra(i, first(i)), 0)),
                pl.BlockSpec((chunk, width), lambda i, c: (extra(i, second(i)), 0)),
                pl.BlockSpec((1, chunk), lambda i, c: (0, place(i, c))),
            ]
            + [whole((count, width))] * 4
            + [whole((8, width))],
            scratch_shapes=[pltpu.VMEM((count, width), F32)] * 2 + [pltpu.VMEM((count, chunk), BF16)] * 2,
        ),
        out_shape=[jax.ShapeDtypeStruct((width, ff // 2), BF16)] * 2
        + [jax.ShapeDtypeStruct((ff // 2 + chunk, width), BF16)] * 2
        + [jax.ShapeDtypeStruct((1, ff), F32), low, full, low, low, jax.ShapeDtypeStruct((8, width), F32)],
        compiler_params=pltpu.CompilerParams(vmem_limit_bytes=VMEM),
        cost_estimate=QUICK,
        name="mlp",
    )(core, keep, normed, mlp_grad, middle, cot, att, out_w, vectors, up_w, up_b, down_w)


def input_kernel(grads, weight, xs, middle_grad, gain, out, sums):
    span = xs.shape[1]
    back = None
    for j in range(3):
        part = dot_nt(grads[j], weight[:, j * span : (j + 1) * span])
        back = part if back is None else back + part
    hat, inv = centre_scale(xs[...].astype(F32))
    out[...] = (middle_grad[...] + norm_back(back * gain[...], hat, inv)).astype(BF16)

    @pl.when(pl.program_id(0) == 0)
    def _():
        sums[...] = jnp.zeros_like(sums)

    sums[0:1, :] += jnp.sum(back * hat, axis=0, keepdims=True)
    sums[1:2, :] += jnp.sum(back, axis=0, keepdims=True)


def input_call(grads, weight, xs, middle_grad, gain, tile=288):
    count, width = xs.shape
    return pl.pallas_call(
        input_kernel,
        grid=(count // tile,),
        in_specs=[pl.BlockSpec((3, tile, width), lambda i: (0, i, 0))]
        + [
            whole(weight.shape),
            pl.BlockSpec((tile, width), lambda i: (i, 0)),
            pl.BlockSpec((tile, width), lambda i: (i, 0)),
            whole((1, width)),
        ],
        out_specs=[pl.BlockSpec((tile, width), lambda i: (i, 0)), pl.BlockSpec((8, width), lambda i: (0, 0))],
        out_shape=[jax.ShapeDtypeStruct((count, width), BF16), jax.ShapeDtypeStruct((8, width), F32)],
        compiler_params=pltpu.CompilerParams(vmem_limit_bytes=VMEM),
        cost_estimate=QUICK,
        name="input_backward",
    )(grads, weight, xs, middle_grad, gain)


def unsort_kernel(me, rank, source, out):
    count, span = source.shape[0], rank.shape[0]
    place = lax.broadcasted_iota(jnp.int32, (span, count), 1)
    out[0] = dot((rank[...] == place).astype(BF16), source[...]).astype(BF16)


def unsort_call(me, rank_col, n, array):
    count, width = array.shape
    span = count // n
    return pl.pallas_call(
        unsort_kernel,
        grid_spec=pltpu.PrefetchScalarGridSpec(
            num_scalar_prefetch=1,
            grid=(n,),
            in_specs=[pl.BlockSpec((span, 1), lambda i, m: (i, 0)), whole((count, width))],
            out_specs=pl.BlockSpec((1, span, width), lambda i, m: (m[0] ^ i, 0, 0)),
        ),
        out_shape=jax.ShapeDtypeStruct((n, span, width), BF16),
        compiler_params=pltpu.CompilerParams(vmem_limit_bytes=VMEM),
        cost_estimate=QUICK,
        name="unsort",
    )(me, rank_col, array)


VECTORS = 128


def input_weights_kernel(core, normed, grads, first, second, third, up_sums, send, keep):
    mid, width = normed.shape[1], grads.shape[2]
    h = core[0] ^ 1 ^ pl.program_id(0)

    def write(out):
        for j in range(3):
            out[:, j * width : (j + 1) * width] = dot_tn(normed[...], grads[j]).astype(BF16)
        rows = [first[0:3, :], second[0:3, :], third[0:1, :]]
        for i in range(up_sums.shape[1] // width):
            rows.append(up_sums[:, pl.ds(pl.multiple_of(i * width + h * mid, 128), mid)])
        count = sum(row.shape[0] for row in rows)
        rows.append(jnp.zeros((VECTORS - count, mid), F32))
        out[:, 3 * width :] = jnp.concatenate(rows, axis=0).T.astype(BF16)

    pl.when(pl.program_id(0) == 0)(lambda: write(send))
    pl.when(pl.program_id(0) == 1)(lambda: write(keep))


def input_weights_call(core, normed, grads, first, second, third, up_sums):
    count, width = normed.shape
    half = jax.ShapeDtypeStruct((width // 2, 3 * width + VECTORS), BF16)
    rows = pl.BlockSpec((count, width // 2), lambda i, c: (0, c[0] ^ 1 ^ i))
    vector = pl.BlockSpec((8, width // 2), lambda i, c: (0, c[0] ^ 1 ^ i))
    return pl.pallas_call(
        input_weights_kernel,
        grid_spec=pltpu.PrefetchScalarGridSpec(
            num_scalar_prefetch=1,
            grid=(2,),
            in_specs=[rows, whole(grads.shape), vector, vector, vector, whole(up_sums.shape)],
            out_specs=[whole(half.shape)] * 2,
        ),
        out_shape=[half] * 2,
        compiler_params=pltpu.CompilerParams(vmem_limit_bytes=VMEM),
        cost_estimate=QUICK,
        name="input_weights",
    )(core, normed, grads, first, second, third, up_sums)


GROUPS = 4


def final_call(core, turns, blocks, groups, pieces, name, spread, outs, scratch=(), finish=None):
    size = blocks // groups
    rows = pieces[0].shape[0] // (blocks // 2)
    whole_tile = 1 if rows % 16 == 0 else 2

    def kernel(c, t, *refs):
        h, g = pl.program_id(0), pl.program_id(1)
        active = (h * groups + g) // (groups // 2)
        turn = t[h]
        place = g ^ (turn // size)

        def write(source):
            for j in range(0, size, whole_tile):
                part = source[j * rows : (j + whole_tile) * rows, :].astype(F32)
                for i in range(whole_tile):
                    spread(part[i * rows : (i + 1) * rows], (j + i) ^ (turn % size), place, refs[4:])

        for q in range(4):
            pl.when(active == q)(functools.partial(write, refs[q]))
        if finish is not None:
            pl.when(g == groups - 1)(lambda: finish(refs[4:]))

    def in_spec(q):
        def index(h, g, c, t):
            return jnp.clip(h * groups + g - q * (groups // 2), 0, groups // 2 - 1), 0

        return pl.BlockSpec((size * rows, pieces[q].shape[1]), index)

    def out_spec(block, index):
        return pl.BlockSpec(block, lambda h, g, c, t: index(h ^ c[0], g, lambda n: n ^ (t[h] // size)))

    return pl.pallas_call(
        kernel,
        grid_spec=pltpu.PrefetchScalarGridSpec(
            num_scalar_prefetch=2,
            grid=(2, groups),
            in_specs=[in_spec(q) for q in range(4)],
            out_specs=[out_spec(block, index) for _, block, index in outs],
            scratch_shapes=list(scratch),
        ),
        out_shape=[jax.ShapeDtypeStruct(shape, F32) for shape, _, _ in outs],
        compiler_params=pltpu.CompilerParams(vmem_limit_bytes=VMEM),
        cost_estimate=QUICK,
        name=name,
    )(core, turns, *pieces)


def rows_at(ref, place, value):
    rows = value.shape[0]
    ref[pl.ds(pl.multiple_of(place * rows, 8), rows), :] = value


def down_final(core, turns, blocks, pieces, ff):
    rows, width = pieces[0].shape[0] // (blocks // 2), pieces[0].shape[1]
    size = blocks // GROUPS * rows

    def spread(block, j, place, refs):
        @pl.when(place < GROUPS - 1)
        def _():
            rows_at(refs[0], j, block)

        @pl.when((place == GROUPS - 1) & (j * rows < width // 2))
        def _():
            rows_at(refs[1], j, block)

    def down_index(h, g, place):
        at = place(g)
        near = place(jnp.where(g == 0, 1, g - 1))
        return h * (GROUPS - 1) + jnp.where(at == GROUPS - 1, near, at), 0

    outs = [
        ((ff, width), (size, width), down_index),
        ((width, width), (width // 2, width), lambda h, g, place: (h, 0)),
    ]
    return final_call(core, turns, blocks, GROUPS, pieces, "down_final", spread, outs)


def up_final(core, turns, blocks, pieces):
    rows, cols = pieces[0].shape[0] * 2, pieces[0].shape[1]

    def spread(block, j, place, refs):
        rows_at(refs[0], j, block)

    outs = [((rows, 2 * cols), (rows // 2, cols), lambda h, g, place: (place(g), h))]
    return final_call(core, turns, blocks, 2, pieces, "up_final", spread, outs)[0]


def input_final(core, turns, blocks, pieces):
    width, cols = pieces[0].shape[0] * 4, pieces[0].shape[1]
    n, half = cols - 3 * width, width // 2

    def spread(block, j, place, refs):
        rows_at(refs[0], j, block[:, : 3 * width])
        rows_at(refs[2], place * (blocks // 2) + j, block[:, 3 * width :])

    def finish(refs):
        refs[1][...] = refs[2][...].T

    outs = [
        ((width, 3 * width), (half // 2, 3 * width), lambda h, g, place: (h * 2 + place(g), 0)),
        ((n, width), (n, half), lambda h, g, place: (0, h)),
    ]
    scratch = [pltpu.VMEM((half, n), F32)]
    return final_call(core, turns, blocks, 2, pieces, "input_final", spread, outs, scratch, finish)


def copy_kernel(source, out):
    out[...] = source[...]


def copy_call(array):
    spec = pl.BlockSpec((1, *array.shape[1:]), lambda i: (i, 0, 0))
    return pl.pallas_call(
        copy_kernel,
        grid=(array.shape[0],),
        in_specs=[spec],
        out_specs=spec,
        out_shape=jax.ShapeDtypeStruct(array.shape, array.dtype),
        compiler_params=pltpu.CompilerParams(vmem_limit_bytes=VMEM),
        cost_estimate=QUICK,
        name="copy",
    )(array)


MICRO = 2


def from_behind(value, axis, steps):
    count = lax.axis_size(axis)
    pairs = [(source, (source + steps) % count) for source in range(count)]
    return lax.ppermute(value, axis, pairs)


def norm_rows(values, gain, shift):
    centre = values - jnp.mean(values, axis=-1, keepdims=True)
    spread = jnp.mean(centre * centre, axis=-1, keepdims=True)
    return centre * lax.rsqrt(spread + eps_norm) * gain + shift


def gelu_exact(values):
    return jax.nn.gelu(values, approximate=False)


def split_heads(block):
    return block.reshape(block.shape[0], block.shape[1], HEADS, HEAD_DIM)


def take_rows(array, first_row, count_rows):
    return lax.slice_in_dim(array, first_row, first_row + count_rows, axis=0)


def masked_scores(query, keys, ids_query, ids_keys):
    scores = jnp.einsum(
        "rqhd,rkhd->rhqk", split_heads(query), split_heads(keys), preferred_element_type=jnp.float32
    ) * HEAD_DIM ** (-0.5)
    same = ids_query[:, None, :, None] == ids_keys[:, None, None, :]
    return jnp.where(same, scores, -jnp.inf)


def attend_piece(carry, query, ids_query, piece):
    keys, values, ids_keys = piece
    peak, total, accum = carry
    scores = masked_scores(query, keys, ids_query, ids_keys)
    top = jnp.maximum(peak, jnp.max(scores, axis=-1))
    weights = jnp.exp(scores - top[..., None])
    total = jnp.sum(weights, axis=-1)
    update = jnp.einsum(
        "rhqk,rkhd->rqhd",
        weights.astype(jnp.bfloat16),
        split_heads(values),
        preferred_element_type=jnp.float32,
    )
    return (top, total, update.reshape(accum.shape))


def attention_forward(query, keys, values, ids_query):
    rows_here, slots, width = query.shape
    start_state = (
        jnp.full((rows_here, HEADS, slots), -1e30, jnp.float32),
        jnp.zeros((rows_here, HEADS, slots), jnp.float32),
        jnp.zeros((rows_here, slots, width), jnp.float32),
    )
    carry = attend_piece(
        start_state,
        query,
        ids_query,
        (
            lax.all_gather(keys, "blk", axis=1, tiled=True),
            lax.all_gather(values, "blk", axis=1, tiled=True),
            lax.all_gather(ids_query, "blk", axis=1, tiled=True),
        ),
    )
    return (carry[0], carry[1], carry[2], None)


def attention_back(query, out_grad, ids_query, log_total, inner, piece):
    keys, values, ids_keys = piece
    scale = HEAD_DIM ** (-0.5)
    scores = masked_scores(query, keys, ids_query, ids_keys)
    probs = jnp.exp(scores - log_total[..., None])
    prob_grad = jnp.einsum(
        "rqhd,rkhd->rhqk",
        split_heads(out_grad),
        split_heads(values),
        preferred_element_type=jnp.float32,
    )
    score_grad = (probs * (prob_grad - inner[..., None])).astype(jnp.bfloat16)
    value_grad = jnp.einsum(
        "rhqk,rqhd->rkhd",
        probs.astype(jnp.bfloat16),
        split_heads(out_grad),
        preferred_element_type=jnp.float32,
    )
    key_grad = (
        jnp.einsum(
            "rhqk,rqhd->rkhd", score_grad, split_heads(query), preferred_element_type=jnp.float32
        )
        * scale
    )
    query_grad = (
        jnp.einsum(
            "rhqk,rkhd->rqhd", score_grad, split_heads(keys), preferred_element_type=jnp.float32
        )
        * scale
    )
    return (
        query_grad.reshape(query.shape),
        key_grad.reshape(keys.shape),
        value_grad.reshape(values.shape),
    )


def local(
    inputs,
    image_index,
    keep_mask,
    first_gain,
    first_shift,
    input_weight,
    input_bias,
    output_weight,
    output_bias,
    second_gain,
    second_shift,
    up_weight,
    up_bias,
    down_weight,
    down_bias,
    cotangent,
):
    rows_local, slots, width = inputs.shape
    rows_micro = rows_local // MICRO
    count = rows_micro * slots
    blocks = lax.axis_size("blk")
    params = (
        first_gain,
        first_shift,
        input_weight,
        input_bias,
        output_weight,
        output_bias,
        second_gain,
        second_shift,
        up_weight,
        up_bias,
        down_weight,
        down_bias,
    )
    sums = [jnp.zeros(item.shape, jnp.float32) for item in params]
    results = []
    input_grads = []
    for micro in range(MICRO):
        first_row = micro * rows_micro
        rows_in = take_rows(inputs, first_row, rows_micro).astype(jnp.float32).reshape(count, width)
        out_cot = (
            take_rows(cotangent, first_row, rows_micro).astype(jnp.float32).reshape(count, width)
        )
        ids_query = take_rows(image_index, first_row, rows_micro).astype(jnp.bfloat16)
        keep = take_rows(keep_mask, first_row, rows_micro).astype(jnp.float32) / keep_rate
        keep_attn = jnp.broadcast_to(keep[:, None, 0:1], (rows_micro, slots, 1)).reshape(count, 1)
        keep_mlp = jnp.broadcast_to(keep[:, None, 1:2], (rows_micro, slots, 1)).reshape(count, 1)
        normed = norm_rows(rows_in, first_gain, first_shift).astype(jnp.bfloat16)
        mixed = jnp.dot(normed, input_weight, preferred_element_type=jnp.float32)
        query = (
            (mixed[:, :width] + input_bias[0])
            .astype(jnp.bfloat16)
            .reshape(rows_micro, slots, width)
        )
        keys = mixed[:, width : 2 * width].astype(jnp.bfloat16).reshape(rows_micro, slots, width)
        values = (
            (mixed[:, 2 * width :] + input_bias[1])
            .astype(jnp.bfloat16)
            .reshape(rows_micro, slots, width)
        )
        top, total, accum, whole = attention_forward(query, keys, values, ids_query)
        attended = (split_heads(accum) / jnp.transpose(total, (0, 2, 1))[..., None]).reshape(
            count, width
        )
        log_total = top + jnp.log(total)
        attended_low = attended.astype(jnp.bfloat16)
        branch = (
            jnp.dot(attended_low, output_weight, preferred_element_type=jnp.float32) + output_bias
        )
        middle = rows_in + keep_attn * branch
        normed_second = norm_rows(middle, second_gain, second_shift).astype(jnp.bfloat16)
        hidden = jnp.dot(normed_second, up_weight, preferred_element_type=jnp.float32) + up_bias
        active = gelu_exact(hidden).astype(jnp.bfloat16)
        branch_second = jnp.dot(active, down_weight, preferred_element_type=jnp.float32) + down_bias
        results.append(
            (middle + keep_mlp * branch_second)
            .astype(jnp.bfloat16)
            .reshape(rows_micro, slots, width)
        )
        mlp_grad = (out_cot * keep_mlp).astype(jnp.bfloat16)
        sums[10] = sums[10] + jnp.dot(active.T, mlp_grad, preferred_element_type=jnp.float32)
        sums[11] = sums[11] + jnp.sum(mlp_grad.astype(jnp.float32), axis=0)
        active_grad = jnp.dot(mlp_grad, down_weight.T, preferred_element_type=jnp.float32)
        hidden_grad = jax.vjp(gelu_exact, hidden)[1](active_grad)[0].astype(jnp.bfloat16)
        sums[8] = sums[8] + jnp.dot(
            normed_second.T, hidden_grad, preferred_element_type=jnp.float32
        )
        sums[9] = sums[9] + jnp.sum(hidden_grad.astype(jnp.float32), axis=0)
        second_in_grad = jnp.dot(hidden_grad, up_weight.T, preferred_element_type=jnp.float32)
        middle_part, second_gain_part, second_shift_part = jax.vjp(
            norm_rows, middle, second_gain, second_shift
        )[1](second_in_grad)
        sums[6] = sums[6] + second_gain_part
        sums[7] = sums[7] + second_shift_part
        middle_grad = middle_part + out_cot
        branch_grad = (middle_grad * keep_attn).astype(jnp.bfloat16)
        sums[4] = sums[4] + jnp.dot(attended_low.T, branch_grad, preferred_element_type=jnp.float32)
        sums[5] = sums[5] + jnp.sum(branch_grad.astype(jnp.float32), axis=0)
        attended_grad = jnp.dot(
            branch_grad, output_weight.T, preferred_element_type=jnp.float32
        ).astype(jnp.bfloat16)
        out_grad = attended_grad.reshape(rows_micro, slots, width)
        inner = jnp.transpose(
            jnp.sum(
                split_heads(
                    (attended_grad.astype(jnp.float32) * attended).reshape(rows_micro, slots, width)
                ),
                axis=-1,
            ),
            (0, 2, 1),
        )
        query_grad = jnp.zeros((rows_micro, slots, width), jnp.float32)
        visiting = (keys, values, ids_query)
        key_grad = jnp.zeros((rows_micro, slots, width), jnp.float32)
        value_grad = jnp.zeros((rows_micro, slots, width), jnp.float32)
        for step in range(blocks):
            query_part, key_part, value_part = attention_back(
                query, out_grad, ids_query, log_total, inner, visiting
            )
            query_grad = query_grad + query_part
            key_grad, value_grad = (
                from_behind((key_grad + key_part).astype(jnp.bfloat16), "blk", 1).astype(
                    jnp.float32
                ),
                from_behind((value_grad + value_part).astype(jnp.bfloat16), "blk", 1).astype(
                    jnp.float32
                ),
            )
            if step + 1 < blocks:
                visiting = from_behind((visiting[0], visiting[1], visiting[2]), "blk", 1)
        joined_grad = (
            jnp.concatenate([query_grad, key_grad, value_grad], axis=-1)
            .astype(jnp.bfloat16)
            .reshape(count, 3 * width)
        )
        sums[2] = sums[2] + jnp.dot(normed.T, joined_grad, preferred_element_type=jnp.float32)
        joined_sums = jnp.sum(joined_grad.astype(jnp.float32), axis=0)
        sums[3] = sums[3] + jnp.stack([joined_sums[:width], joined_sums[2 * width :]])
        first_in_grad = jnp.dot(joined_grad, input_weight.T, preferred_element_type=jnp.float32)
        rows_part, first_gain_part, first_shift_part = jax.vjp(
            norm_rows, rows_in, first_gain, first_shift
        )[1](first_in_grad)
        sums[0] = sums[0] + first_gain_part
        sums[1] = sums[1] + first_shift_part
        input_grads.append(
            (rows_part + middle_grad).astype(jnp.bfloat16).reshape(rows_micro, slots, width)
        )
    totals = lax.psum(
        (
            sums[0],
            sums[1],
            sums[2],
            sums[3],
            sums[4],
            sums[5],
            sums[6],
            sums[7],
            sums[8],
            sums[9],
            sums[10],
            sums[11],
        ),
        ("rows", "blk"),
    )
    return (
        jnp.concatenate(results, axis=0),
        jnp.concatenate(input_grads, axis=0),
        totals[0],
        totals[1],
        totals[2],
        totals[3],
        totals[4],
        totals[5],
        totals[6],
        totals[7],
        totals[8],
        totals[9],
        totals[10],
        totals[11],
    )


def swap(value, axis, bit):
    return lax.ppermute(value, axis, [(i, i ^ bit) for i in range(lax.axis_size(axis))])


def side(axis, bit):
    return (lax.axis_index(axis) // bit) % 2


def after(value, *others):
    return lax.optimization_barrier((value, *others))[0]


def axis_bits(axis):
    bits, bit = [], 1
    while bit < lax.axis_size(axis):
        bits.append((axis, bit))
        bit *= 2
    return bits


def add_low(a, b):
    return (a.astype(F32) + b.astype(F32)).astype(BF16)


def swap_two(value, step):
    rows, blocks = lax.axis_size("rows"), lax.axis_size("blk")
    pairs = []
    for r in range(rows):
        for b in range(blocks):
            axis, bit = step[b % 2]
            other = (r ^ bit, b) if axis == "rows" else (r, b ^ bit)
            pairs.append((r * blocks + b, other[0] * blocks + other[1]))
    return lax.ppermute(value, ("rows", "blk"), pairs)


def side_two(step):
    return jnp.where(side("blk", 1) == 0, side(*step[0]), side(*step[1]))


class Order:
    def __init__(self):
        self.last = ()

    def hold(self, value):
        return after(value, *self.last) if self.last else value

    def advance(self, *parts):
        parts = [part for part in parts if part.result is None]
        if parts:
            held = lax.optimization_barrier(([part.recv for part in parts], self.last))[0]
            self.done(*[value for part, recv in zip(parts, held) for value in part.step(recv)])

    def done(self, *values):
        self.last = values
        return values[0] if len(values) == 1 else values


class Chain:
    def __init__(self, steps, send, keep):
        self.steps, self.at = steps, -1
        self.recv, self.keep, self.result = send, keep, None

    def step(self, recv):
        keep, n = self.keep, len(self.steps)
        if self.at < 0:
            send, self.recv = recv, swap(recv, "blk", 1)
        elif self.at < n:
            step = self.steps[self.at]
            half = keep.shape[0] // 2
            own = side_two(step)

            def part(which):
                return add_low(
                    lax.dynamic_slice_in_dim(keep, which * half, half, 0),
                    lax.dynamic_slice_in_dim(recv, which * half, half, 0),
                )

            send, self.keep = part(1 - own), part(own)
            self.recv = swap_two(send, step)
        elif self.at < 2 * n:
            send = add_low(keep, recv) if self.at == n else jnp.concatenate([keep, recv], axis=0)
            send = self.keep = lax.optimization_barrier(send)
            self.recv = swap_two(send, self.steps[2 * n - 1 - self.at])
        elif self.at == 2 * n:
            self.at, self.keep, self.recv = self.at + 1, (keep, recv), [swap(piece, "blk", 1) for piece in (keep, recv)]
            return keep, recv
        else:
            self.result, self.recv = (*keep, *recv), None
            return ()
        self.at += 1
        return send, self.keep


class Small:
    def __init__(self, value):
        count = lax.axis_size("rows") * lax.axis_size("blk")
        self.recv, self.result, self.sent = jnp.broadcast_to(value[None], (count, *value.shape)), None, False

    def step(self, recv):
        if not self.sent:
            self.recv, self.sent = lax.all_to_all(recv, ("rows", "blk"), 0, 0), True
            return (recv,)
        self.result, self.recv = jnp.sum(recv, axis=0), None
        return (self.result,)


class Home:
    def __init__(self, pieces):
        self.recv, self.result, self.sent = pieces, None, False

    def step(self, recv):
        if not self.sent:
            self.recv, self.sent = lax.all_to_all(recv, "blk", 0, 0), True
        else:
            self.result, self.recv = recv, None
        return (recv,)


def block_turns(steps):
    core = side("blk", 1)
    turns = []
    for c in range(2):
        turn = 0
        for step in steps:
            turn = turn * 2 + side(*step[c])
        turns.append(turn)
    first, second = jnp.where(core == 0, turns[0], turns[1]), jnp.where(core == 0, turns[1], turns[0])
    return core.astype(jnp.int32).reshape(1), jnp.stack([first, second]).astype(jnp.int32), 1 << len(steps)


def local_rows(
    inputs,
    image_index,
    keep_mask,
    first_gain,
    first_shift,
    input_weight,
    input_bias,
    output_weight,
    output_bias,
    second_gain,
    second_shift,
    up_weight,
    up_bias,
    down_weight,
    down_bias,
    cotangent,
):
    blocks, span, width = inputs.shape
    ff = up_weight.shape[1]
    me = lax.axis_index("blk")

    def row_piece(array, s):
        return lax.dynamic_index_in_dim(array, me ^ s, 0, keepdims=False)

    xs_send = [row_piece(inputs, s) for s in range(1, blocks)]
    xs_in = [row_piece(after(inputs, *xs_send), 0)] + [swap(x, "blk", s + 1) for s, x in enumerate(xs_send)]
    ids = [row_piece(image_index, 0)] + [
        swap(row_piece(after(image_index, *xs_send), s), "blk", s) for s in range(1, blocks)
    ]
    cots = [row_piece(cotangent, 0)] + [
        swap(after(row_piece(cotangent, s), *xs_send), "blk", s) for s in range(1, blocks)
    ]
    ids = jnp.concatenate(ids)
    image = jnp.where(ids < 0, 4, ids)
    order_key = image * ids.shape[0] + jnp.arange(ids.shape[0], dtype=jnp.int32)
    less = (order_key[None, :] < order_key[:, None]).astype(jnp.int32)
    rank = jnp.sum(less, axis=1)
    starts = jnp.sum((image[None, :] < jnp.arange(6, dtype=jnp.int32)[:, None]).astype(jnp.int32), axis=1)
    keep = lax.dynamic_index_in_dim(keep_mask, me, 0, keepdims=False).astype(F32) / keep_rate
    rank_row, rank_col = rank[None, :], rank[:, None]

    bias = jnp.stack([input_bias[0], jnp.zeros_like(input_bias[0]), input_bias[1]])
    xs, normed, qkv = qkv_call(rank_row, xs_in, first_gain[None], first_shift[None], input_weight, bias)
    attended, stat, att_low = forward_call(starts, qkv)
    vectors = jnp.stack([output_bias, second_gain, second_shift, down_bias])
    core = side("blk", 1).astype(jnp.int32).reshape(1)
    cot, middle, normed2, mlp_grad, sums_mid = middle_call(
        keep, rank_row, cots, att_low, xs, output_weight, vectors
    )
    (up_send, up_keep, down_send, down_keep, up_sums, result, middle_grad, branch, att_grad, sums2) = mlp_call(
        core, keep, normed2, mlp_grad, middle, cot, att_low, output_weight, vectors, up_weight, up_bias[None], down_weight
    )

    y, x, z = axis_bits("blk")[1], axis_bits("rows")[0], axis_bits("rows")[1:]
    far = [(d, d) for d in z[1:]]
    xy = [(x, y), (y, x), (z[0], z[0])] + far
    zx = [(z[0], z[0]), (x, y), (y, x)] + far
    order = Order()
    order.done(att_grad)
    up_chain, down_chain = Chain(zx, up_send, up_keep), Chain(xy, down_send, down_keep)

    order.advance(up_chain, down_chain)
    result_home = Home(order.done(unsort_call(me.reshape(1), rank_col, blocks, order.hold(result))))
    order.advance(up_chain, down_chain, result_home)
    grads, bias_sums = backward_call(starts, qkv, order.hold(att_grad), attended, stat, 0, PAIRS)
    order.done(grads)
    order.advance(up_chain, down_chain, result_home)
    input_chain = Chain(
        xy, *order.done(*input_weights_call(core, order.hold(normed), grads, bias_sums, sums2, sums_mid, up_sums))
    )
    order.advance(input_chain, up_chain, down_chain)
    inputs_grad, sums1 = order.done(*input_call(grads, input_weight, xs, order.hold(middle_grad), first_gain[None]))
    small = Small(sums1[:2])
    order.advance(input_chain, up_chain, down_chain, small)
    home = Home(order.done(unsort_call(me.reshape(1), rank_col, blocks, order.hold(inputs_grad))))
    order.advance(input_chain, up_chain, down_chain, small, home)
    order.advance(input_chain, up_chain, down_chain)
    order.advance(input_chain, up_chain, down_chain, home)
    while down_chain.at < 2 * len(xy):
        order.advance(input_chain, up_chain, down_chain)
    result_out = order.done(copy_call(order.hold(result_home.result)))
    inputs_out = order.done(copy_call(order.hold(home.result)))
    order.advance(input_chain, up_chain, down_chain)
    order.advance(input_chain, up_chain, down_chain)
    up_total = order.done(up_final(*block_turns(zx), (order.hold(up_chain.result[0]), *up_chain.result[1:])))
    order.advance(input_chain)
    down_total, out_total = order.done(
        *down_final(*block_turns(xy), (order.hold(down_chain.result[0]), *down_chain.result[1:]), ff)
    )
    while input_chain.result is None:
        order.advance(input_chain)
    input_total, sums = input_final(*block_turns(xy), input_chain.result)
    sums = jnp.concatenate([small.result, sums[:16]])

    return (
        result_out,
        inputs_out,
        sums[0],
        sums[1],
        input_total,
        jnp.stack([sums[2], sums[4]]),
        out_total,
        sums[7],
        sums[5],
        sums[6],
        up_total,
        sums[9:13].reshape(ff),
        down_total,
        sums[8],
    )


def solution(mesh):
    blocks, groups = mesh.shape["blk"], mesh.shape["rows"]

    def run(*args):
        whole_rows = args[0].shape[0] // groups == blocks == 4 and groups in (4, 8, 16)
        return jax.shard_map(
            local_rows if whole_rows else local,
            mesh=mesh,
            in_specs=(P("rows", "blk", None), P("rows", "blk"), P("rows", None)) + (P(),) * 12 + (P("rows", "blk", None),),
            out_specs=(P("rows", "blk", None),) * 2 + (P(),) * 12,
            check_vma=False,
        )(*args)

    return run
```
